128 devices in a mesh: row: 8 (over y, core), seq: 4 (over x), head: 4 (over z).
Axes of the slice: x: 4, y: 4, z: 4, core: 2. Of those that a mesh axis runs over, the one named last changes fastest.
Arguments:
- tokens: bfloat16 [8, 2048, 512], P('row', ('seq', 'head')), may hold values from -6 to 6
- starts: int32 [8, 6], P('row'), may hold values from 0 to 2047, as said below
- gain_one: float32 [512], replicated, may hold values from 0.25 to 1.75
- w_in: bfloat16 [512, 2048], replicated, may hold values from -0.25 to 0.25
- conv_weight: float32 [4, 1024], replicated, may hold values from -3 to 3
- conv_bias: float32 [1024], replicated, may hold values from -4 to 4
- w_x: bfloat16 [1024, 64], replicated, may hold values from -0.75 to 0.75
- w_dt: bfloat16 [32, 1024], replicated, may hold values from -0.5 to 0.5
- dt_bias: float32 [1024], replicated, may hold values from -9 to -3
- a_log: float32 [16, 1024], replicated, may hold values from 0 to 1.4
- d_skip: float32 [1024], replicated, may hold values from 0.5 to 1.5
- w_out: bfloat16 [1024, 512], replicated, may hold values from -0.375 to 0.375
- gain_two: float32 [512], replicated, may hold values from 0.25 to 1.75
- w_q: bfloat16 [512, 512], replicated, may hold values from -0.375 to 0.375
- w_k: bfloat16 [512, 512], replicated, may hold values from -0.375 to 0.375
- w_v: bfloat16 [512, 512], replicated, may hold values from -0.25 to 0.25
- w_o: bfloat16 [512, 512], replicated, may hold values from -2 to 2
- cotangent: bfloat16 [8, 2048, 512], P('row', ('seq', 'head')), may hold values from -6 to 6
Outputs:
- mixed: bfloat16 [8, 2048, 512], P('row', ('seq', 'head'))
- grad_tokens: float32 [8, 2048, 512], P('row', ('seq', 'head'))
- grad_gain_one: float32 [512], replicated
- grad_w_in: float32 [512, 2048], replicated
- grad_conv_weight: float32 [4, 1024], replicated
- grad_conv_bias: float32 [1024], replicated
- grad_w_x: float32 [1024, 64], replicated
- grad_w_dt: float32 [32, 1024], replicated
- grad_dt_bias: float32 [1024], replicated
- grad_a_log: float32 [16, 1024], replicated
- grad_d_skip: float32 [1024], replicated
- grad_w_out: float32 [1024, 512], replicated
- grad_gain_two: float32 [512], replicated
- grad_w_q: float32 [512, 512], replicated
- grad_w_k: float32 [512, 512], replicated
- grad_w_v: float32 [512, 512], replicated
- grad_w_o: float32 [512, 512], replicated
The draws below stay inside these ranges and needn't reach their ends.
Inputs may be any that keep to these rules, and one draw needn't show every extreme that they name: `starts`: each row holds the first positions of its 6 documents in strictly rising order, the first being 0. In each group of 1 row that share an index of row, one row drawn from the seed has a document that covers positions 127 to 1920, and that row's last document is the single position 2047.
All inputs are finite; a program needn't handle non-finite values.
Results may differ from the reference program's by a relative error of at most 0.03.
The reference program's roundings to bfloat16 on the way count: a program that leaves them out, or rounds other values in their place, can miss the bound.
Values may be sent and summed in bfloat16 or wider, within the bound.
No kernel may reach another device: no remote copies, remote signals or barrier semaphores. Data moves between devices by JAX's collectives and lax.ppermute only.
A program may use at most 192 MiB of HBM per device.

```python
import jax
import jax.numpy as jnp
from jax import lax

DMODEL = 512
INNER = 1024
STATE = 16
DTRANK = 32
XPROJ = 64
CONV = 4
HEADS = 8
HEAD_DIM = 64
LENGTH = 2048
DOCS = 6
SEQ_DEV = 1
SEQS = 8
PIECE = 128


def draw_starts(key, part):
    key = jax.random.fold_in(key, 11)
    extra_count = DOCS - 1
    spread_key, zone_key, pick_key = jax.random.split(key, 3)
    spread_keys = jax.random.split(spread_key, SEQS)
    zone_keys = jax.random.split(zone_key, SEQS)
    zone_size = 2 * PIECE - 3

    def spread_row(row_key):
        return jnp.sort(jax.random.permutation(row_key, LENGTH - 1)[:extra_count] + 1)

    def zone_row(row_key):
        chosen = jax.random.permutation(row_key, zone_size)[:extra_count - 1]
        mapped = jnp.where(chosen < PIECE - 1, chosen + 1, chosen + LENGTH - 2 * PIECE + 2)
        return jnp.sort(jnp.concatenate([mapped, jnp.full((1,), LENGTH - 1, jnp.int32)]).astype(jnp.int32))
    spread = jax.vmap(spread_row)(spread_keys).astype(jnp.int32)
    zoned = jax.vmap(zone_row)(zone_keys).astype(jnp.int32)
    groups = SEQS // SEQ_DEV
    chosen_row = jax.random.randint(pick_key, (groups,), 0, SEQ_DEV)
    row_ids = jnp.arange(SEQS, dtype=jnp.int32)
    long_row = row_ids % SEQ_DEV == jnp.repeat(chosen_row, SEQ_DEV)
    extra = jnp.where(long_row[:, None], zoned, spread)
    return jnp.concatenate([jnp.zeros((SEQS, 1), jnp.int32), extra], axis=1).astype(jnp.int32)


def steps_of(own_key, shape, cuts, low, high):
    gain, own = 1.0, jax.random.fold_in(own_key, 6)
    for dim, shards_of in cuts:
        draws = jnp.exp(jax.random.uniform(jax.random.fold_in(own, dim), (shards_of,), jnp.float32, low / len(cuts), high / len(cuts)))
        gain = gain * jnp.repeat(draws, shape[dim] // shards_of).reshape([-1 if axis == dim else 1 for axis in range(len(shape))])
    return gain


def gaussian(key, shape, width, reach, cuts=(), kind=jnp.bfloat16):
    values = jax.random.normal(key, shape, jnp.float32) * width
    if len(cuts) > 0:
        values = steps_of(key, shape, cuts, -0.22, 0.18) * values
    return jnp.clip(values, min=-reach, max=reach).astype(kind)


def setup_inputs(seed: int = 0) -> dict:
    streams_of = jax.random.split(jax.random.key(seed), 19)
    tokens = gaussian(streams_of[0], (SEQS, LENGTH, DMODEL), 1.0, 6.0, ((0, 8), (1, 16)))
    starts = draw_starts(jax.random.fold_in(streams_of[18], 71), 0)
    gain_one = jnp.clip(1.0 + 0.15 * jax.random.normal(streams_of[2], (DMODEL,), jnp.float32), 0.25, 1.75)
    w_in = gaussian(streams_of[3], (DMODEL, 2 * INNER), DMODEL ** -0.5, 0.25)
    conv_weight = gaussian(streams_of[4], (CONV, INNER), CONV ** -0.5, 3.0, (), jnp.float32)
    conv_bias = gaussian(streams_of[5], (INNER,), 0.3, 4.0, (), jnp.float32)
    w_x = gaussian(streams_of[6], (INNER, XPROJ), (INNER // 16) ** -0.5, 0.75)
    w_dt = gaussian(streams_of[7], (DTRANK, INNER), (4 * DTRANK) ** -0.5, 0.5)
    dt_bias = jnp.clip(jax.random.uniform(streams_of[8], (INNER,), jnp.float32, -9.0, -3.0), -9.0, -3.0)
    a_log = jnp.clip(jax.random.uniform(streams_of[9], (STATE, INNER), jnp.float32, 0.0, 1.4), 0.0, 1.4)
    d_skip = jnp.clip(jax.random.uniform(streams_of[10], (INNER,), jnp.float32, 0.5, 1.5), 0.5, 1.5)
    w_out = gaussian(streams_of[11], (INNER, DMODEL), (INNER // 4) ** -0.5, 0.375)
    gain_two = jnp.clip(1.0 + 0.15 * jax.random.normal(streams_of[12], (DMODEL,), jnp.float32), 0.25, 1.75)
    w_q = gaussian(streams_of[13], (DMODEL, DMODEL), (DMODEL // 2) ** -0.5, 0.375)
    w_k = gaussian(streams_of[14], (DMODEL, DMODEL), (DMODEL // 2) ** -0.5, 0.375)
    w_v = gaussian(streams_of[15], (DMODEL, DMODEL), DMODEL ** -0.5, 0.25)
    w_o = gaussian(streams_of[16], (DMODEL, DMODEL), (DMODEL // 64) ** -0.5, 2.0)
    cotangent = gaussian(streams_of[17], (SEQS, LENGTH, DMODEL), 1.0, 6.0, ((0, 8), (1, 16)))
    return {"tokens": tokens, "starts": starts, "gain_one": gain_one, "w_in": w_in, "conv_weight": conv_weight, "conv_bias": conv_bias, "w_x": w_x, "w_dt": w_dt, "dt_bias": dt_bias, "a_log": a_log, "d_skip": d_skip, "w_out": w_out, "gain_two": gain_two, "w_q": w_q, "w_k": w_k, "w_v": w_v, "w_o": w_o, "cotangent": cotangent}


epsilon = 1e-05
masked_score = -1e+30
exact_mode = lax.Precision.HIGHEST

@jax.custom_vjp
def low(v):
    return lax.optimization_barrier(v.astype(jnp.bfloat16)).astype(jnp.float32)

@jax.custom_vjp
def low_back(v):
    return v

def low_keep(v):
    return (low(v), None)

def low_pass(kept, grad):
    return (grad,)

def back_keep(v):
    return (v, None)

def back_low(kept, grad):
    return (low(grad),)
low.defvjp(low_keep, low_pass)
low_back.defvjp(back_keep, back_low)

def matmul(left, right):
    return jnp.dot(left, right, precision=exact_mode)

def rms_norm(values, gain_vec):
    return values * lax.rsqrt(lax.optimization_barrier(jnp.mean(values * values, axis=-1, keepdims=True)) + epsilon) * gain_vec

def doc_number(starts_row, positions):
    return lax.optimization_barrier(jnp.sum((starts_row[None, :] <= positions[:, None]).astype(jnp.int32), axis=1))

def selective_scan(step_size, act_vals, b_coef, c_coef, keep_mask, decay_rates):
    block_len = min(128, LENGTH)
    blocks = LENGTH // block_len

    def one_step(hidden, item_data):
        step_t, act_t, b_t, c_t, keep_t = item_data
        hidden = jnp.exp(step_t[None, :] * decay_rates) * keep_t * hidden + (step_t * act_t)[None, :] * b_t[:, None]
        return (hidden, lax.optimization_barrier(jnp.sum(hidden * c_t[:, None], axis=0)))

    def one_block(hidden, block_items):
        return lax.scan(one_step, hidden, block_items)
    shaped = tuple((array_in.reshape((blocks, block_len) + array_in.shape[1:]) for array_in in (step_size, act_vals, b_coef, c_coef, keep_mask)))
    final_state, outputs = lax.scan(jax.checkpoint(one_block), jnp.zeros((STATE, INNER), jnp.float32), shaped)
    return outputs.reshape(LENGTH, INNER)

def attention(queries, key_rows, value_rows, docs):
    block_len = min(512, LENGTH)
    blocks = LENGTH // block_len
    q_heads = queries.reshape(LENGTH, HEADS, HEAD_DIM)
    k_heads = key_rows.reshape(LENGTH, HEADS, HEAD_DIM)
    v_heads = value_rows.reshape(LENGTH, HEADS, HEAD_DIM)
    key_pos = jnp.arange(LENGTH, dtype=jnp.int32)

    def one_block(block_index):
        row_begin = (block_index * block_len).astype(jnp.int32)
        q_block = lax.dynamic_slice_in_dim(q_heads, row_begin, block_len, 0)
        query_pos = row_begin + jnp.arange(block_len, dtype=jnp.int32)
        query_doc = lax.dynamic_slice_in_dim(docs, row_begin, block_len, 0)
        allowed = (key_pos[None, :] <= query_pos[:, None]) & (docs[None, :] == query_doc[:, None])
        scores = low_back(jnp.einsum('qhd,khd->hqk', q_block, k_heads, precision=exact_mode) * HEAD_DIM ** (-0.5))
        scores = jnp.where(allowed[None], scores, masked_score)
        top_score = lax.optimization_barrier(jnp.max(scores, axis=-1, keepdims=True))
        weights = jnp.where(allowed[None], jnp.exp(scores - top_score), 0.0)
        prob_vals = weights / lax.optimization_barrier(jnp.sum(weights, axis=-1, keepdims=True))
        output = jnp.einsum('hqk,khd->qhd', low(prob_vals), v_heads, precision=exact_mode)
        return output.reshape(block_len, DMODEL)
    outputs = lax.map(jax.checkpoint(one_block), jnp.arange(blocks, dtype=jnp.int32))
    return outputs.reshape(LENGTH, DMODEL)

def layer(tokens_f, gain_one, w_in, conv_weight, conv_bias, w_x, w_dt, dt_bias, a_log, d_skip, w_out, gain_two, w_q, w_k, w_v, w_o, starts_row):
    positions = jnp.arange(LENGTH, dtype=jnp.int32)
    docs = doc_number(starts_row, positions)
    keep_mask = 1.0 - jnp.any(starts_row[None, :] == positions[:, None], axis=1).astype(jnp.float32)
    normed_one = low(rms_norm(tokens_f, gain_one))
    both_parts = low_back(low(matmul(normed_one, w_in)))
    conv_input = both_parts[:, :INNER]
    gate_vals = both_parts[:, INNER:]
    padded = jnp.pad(conv_input, ((CONV - 1, 0), (0, 0)))
    padded_doc = jnp.concatenate([jnp.zeros((CONV - 1,), jnp.int32), docs])
    conv_out = conv_bias + jnp.zeros_like(conv_input)
    for offset in range(CONV):
        same_doc = (padded_doc[offset:offset + LENGTH] == docs).astype(jnp.float32)[:, None]
        conv_out = conv_out + conv_weight[offset] * padded[offset:offset + LENGTH] * same_doc
    act_vals = low(jax.nn.silu(conv_out))
    x_proj = low_back(matmul(act_vals, w_x))
    dt_input = low(x_proj[:, :DTRANK])
    b_coef = x_proj[:, DTRANK:DTRANK + STATE]
    c_coef = x_proj[:, DTRANK + STATE:]
    step_size = jax.nn.softplus(low_back(matmul(dt_input, w_dt) + dt_bias))
    decay_rates = -jnp.exp(a_log)
    ssm_out = selective_scan(step_size, act_vals, b_coef, c_coef, keep_mask, decay_rates) + d_skip * act_vals
    gated = low_back(low(ssm_out * jax.nn.silu(gate_vals)))
    middle = tokens_f + low_back(matmul(gated, w_out))
    normed_two = low(rms_norm(middle, gain_two))
    queries = low_back(low(matmul(normed_two, w_q)))
    key_rows = low_back(low(matmul(normed_two, w_k)))
    value_rows = low_back(low(matmul(normed_two, w_v)))
    attended = low_back(low(attention(queries, key_rows, value_rows, docs)))
    return middle + low_back(matmul(attended, w_o))

def reference(tokens, starts, gain_one, w_in, conv_weight, conv_bias, w_x, w_dt, dt_bias, a_log, d_skip, w_out, gain_two, w_q, w_k, w_v, w_o, cotangent):
    params = (gain_one, w_in.astype(jnp.float32), conv_weight, conv_bias, w_x.astype(jnp.float32), w_dt.astype(jnp.float32), dt_bias, a_log, d_skip, w_out.astype(jnp.float32), gain_two, w_q.astype(jnp.float32), w_k.astype(jnp.float32), w_v.astype(jnp.float32), w_o.astype(jnp.float32))

    def one_row(totals, row_items):
        row_tokens, starts_row, row_cot = row_items

        def apply_layer(tokens_f, *weights):
            return layer(tokens_f, *weights, starts_row)
        result, pullback = jax.vjp(apply_layer, row_tokens.astype(jnp.float32), *params)
        grad_list = pullback(row_cot.astype(jnp.float32))
        totals = tuple((running + grad_one for running, grad_one in zip(totals, grad_list[1:])))
        return (totals, (result.astype(jnp.bfloat16), grad_list[0]))
    initial = tuple((jnp.zeros_like(param_one) for param_one in params))
    totals, outputs = lax.scan(one_row, initial, (tokens, starts, cotangent))
    mixed, grad_tokens = outputs
    return (mixed, grad_tokens, totals[0], totals[1], totals[2], totals[3], totals[4], totals[5], totals[6], totals[7], totals[8], totals[9], totals[10], totals[11], totals[12], totals[13], totals[14])
```

```python
import functools

import jax
import jax.numpy as jnp
from jax import lax
from jax.experimental import pallas as pl
from jax.experimental.pallas import tpu as pltpu
from jax.sharding import Mesh, PartitionSpec as P

T, D, E, N, R, HD = 128, 512, 1024, 16, 32, 64
HEADS, BLOCKS, HALF, DOCS, KERNEL, HALO = 8, 16, 64, 6, 4, 16
CHUNK, STEPS = 512, 8
ROWS = T + HALF
RESET = 1e4
LOG2E = 1.4426950408889634
EPS = 1e-05
MASKED = -1e30
PLACE = ("seq", "head")
ALL = ("y", "core", "seq", "head")
bf16, f32, i32 = jnp.bfloat16, jnp.float32, jnp.int32


def mm(a, b):
    return jnp.dot(a, b, preferred_element_type=f32)


def mm_nt(a, b):
    return lax.dot_general(a, b, (((1,), (1,)), ((), ())), preferred_element_type=f32)


def mm_tn(a, b):
    return lax.dot_general(a, b, (((0,), (0,)), ((), ())), preferred_element_type=f32)


def doc_of(meta, pos):
    count = jnp.zeros(pos.shape, i32)
    for k in range(DOCS):
        count = count + (meta[2 + k] <= pos).astype(i32)
    return count


def reset_of(meta, pos):
    hit = meta[2] == pos
    for k in range(1, DOCS):
        hit = hit | (meta[2 + k] == pos)
    return jnp.where(hit, RESET, 0.0)


def inverse_rms(x):
    return lax.rsqrt(jnp.mean(x * x, axis=-1, keepdims=True) + EPS)


def sigmoid(x):
    return 1.0 / (1.0 + jnp.exp(-x))


def silu_slope(x):
    s = sigmoid(x)
    return s * (1.0 + x * (1.0 - s))


def norm_back(values, inverse, gain, upstream):
    scaled = upstream * gain
    inner = jnp.mean(values * scaled, axis=-1, keepdims=True)
    back = inverse * scaled - values * (inverse * inverse * inverse) * inner
    return back, jnp.sum(upstream * values * inverse, axis=0, keepdims=True)


def columns(offset, meta):
    first = meta[0]
    return first + offset + lax.broadcasted_iota(i32, (T, 1), 0)


def scan_forward(dec_ref, sa_ref, bc_ref, rates2, start, part, emit):
    def block(i, h):
        bc = bc_ref[i]
        base = pl.multiple_of(i * STEPS, STEPS)
        for k in range(STEPS):
            t = base + k
            dec = dec_ref[pl.ds(t, 1), part]
            sa = sa_ref[pl.ds(t, 1), part]
            drive = bc[0:N, k : k + 1] * sa
            h = jnp.exp2(dec * rates2) * h + drive
            if emit is not None:
                emit(i, k, t, h, bc)
        return h

    return lax.fori_loop(0, T // STEPS, block, start)


def mamba_in(
    meta, tokens, halo, gain, w_in, conv_w, conv_b, w_x, w_dt, dt_b, a_log,
    send, ext_out, gate_out, conv_out, act_out, step_out, pre_out, bc_out, dt_out, total_out,
    ext, dec, sa, xp,
):
    own = tokens[...].astype(f32)
    before = halo[...].astype(f32)
    low_own = (own * inverse_rms(own) * gain[...]).astype(bf16)
    low_before = (before * inverse_rms(before) * gain[...]).astype(bf16)
    conv_own = mm(low_own, w_in[:, :E]).astype(bf16)
    conv_before = mm(low_before, w_in[:, :E]).astype(bf16)
    ext_out[0:HALO] = conv_before
    ext_out[HALO : HALO + T] = conv_own
    ext[0:HALO] = conv_before.astype(f32)
    ext[HALO : HALO + T] = conv_own.astype(f32)
    gate_out[...] = mm(low_own, w_in[:, E:]).astype(bf16)
    own_doc = doc_of(meta, columns(0, meta))
    conv = jnp.broadcast_to(conv_b[...], (T, E))
    for offset in range(KERNEL):
        same = (doc_of(meta, columns(offset - KERNEL + 1, meta)) == own_doc).astype(f32)
        low = HALO - KERNEL + 1 + offset
        conv = conv + conv_w[offset : offset + 1] * ext[low : low + T] * same
    conv_out[...] = conv
    act = (conv * sigmoid(conv)).astype(bf16)
    act_out[...] = act
    proj = mm(act, w_x[...])
    dt_low = proj[:, :R].astype(bf16)
    dt_out[...] = dt_low
    pre = mm(dt_low, w_dt[...]) + dt_b[...]
    pre_out[...] = pre
    step = jnp.maximum(pre, 0.0) + jnp.log1p(jnp.exp(-jnp.abs(pre)))
    step_out[...] = step
    held = step + reset_of(meta, columns(0, meta))
    dec[...] = held
    sa[...] = step * act.astype(f32)
    xp[...] = jnp.zeros((T, 128), f32)
    xp[:, 0 : R + 2 * N] = proj
    turned = xp[...].T
    for i in range(T // STEPS):
        bc_out[i, :, 0:STEPS] = turned[R : R + 2 * N, i * STEPS : (i + 1) * STEPS]
    total = jnp.sum(held, axis=0, keepdims=True)
    high = total.astype(bf16)
    rest = (total - high.astype(f32)).astype(bf16)
    send[N : N + 8] = jnp.concatenate([high, rest, jnp.zeros((6, E), bf16)], axis=0)
    for c in range(E // CHUNK):
        part = slice(c * CHUNK, (c + 1) * CHUNK)
        rates2 = -jnp.exp(a_log[:, part]) * LOG2E
        h = scan_forward(dec, sa, bc_out, rates2, jnp.zeros((N, CHUNK), f32), part, None)
        send[0:N, part] = h.astype(bf16)
    total_out[...] = total


def roll_half(x):
    return pltpu.roll(x, HALF, axis=1)


def mamba_out(
    meta, got, tokens, step, act, bc, gate, a_log, d_skip, w_out, gain, w_q, w_k, w_v, grad_att,
    send, start_out, ssm_out, gated_out, middle_out, normed_out,
    dec, sa, ssm,
):
    place = meta[1]
    dec[...] = step[...] + reset_of(meta, columns(0, meta))
    act_f = act[...].astype(f32)
    sa[...] = step[...] * act_f
    for c in range(E // CHUNK):
        part = slice(c * CHUNK, (c + 1) * CHUNK)
        rates2 = -jnp.exp(a_log[:, part]) * LOG2E

        def join(j, state):
            tail = got[j, N : N + 8, part].astype(f32)
            total = tail[0:1] + tail[1:2]
            return jnp.exp2(rates2 * total) * state + got[j, 0:N, part].astype(f32)

        start = lax.fori_loop(0, place, join, jnp.zeros((N, CHUNK), f32))
        start_out[:, part] = start

        def emit(i, k, t, h, cols):
            ssm[pl.ds(t, 1), part] = jnp.sum(h * cols[N : 2 * N, k : k + 1], axis=0, keepdims=True)

        scan_forward(dec, sa, bc, rates2, start, part, emit)
    result = ssm[...] + d_skip[...] * act_f
    ssm_out[...] = result
    gates = gate[...].astype(f32)
    gated = (result * (gates * sigmoid(gates))).astype(bf16)
    gated_out[...] = gated
    middle = tokens[...].astype(f32) + mm(gated, w_out[...])
    middle_out[...] = middle
    normed = (middle * inverse_rms(middle) * gain[...]).astype(bf16)
    normed_out[...] = normed
    queries = mm(normed, w_q[...]).astype(bf16).astype(f32) * (HD ** -0.5)
    keys = mm(normed, w_k[...])
    vals = mm(normed, w_v[...])
    grads = grad_att[...].astype(f32)
    low = lax.broadcasted_iota(i32, (T, 128), 1) < HALF
    for m in range(HEADS // 2):
        tile = slice(m * 128, (m + 1) * 128)
        for odd in range(2):
            for first, second, at, rows in ((keys, vals, 0, T), (queries, grads, T, HALF)):
                a, b = first[:, tile], second[:, tile]
                pair = jnp.where(low, a, roll_half(b)) if odd == 0 else jnp.where(low, roll_half(a), b)
                pair = pair.astype(bf16)
                dest = 2 * (2 * m + odd)
                if rows == T:
                    send[dest, 0:T] = pair
                    send[dest + 1, 0:T] = pair
                else:
                    send[dest, T:ROWS] = pair[0:HALF]
                    send[dest + 1, T:ROWS] = pair[HALF:T]


QCHUNK, QBLOCKS = 256, 4


def attention(meta, got, send, kv_t, scores, grads, kv_grad):
    parity = lax.rem(meta[1], 2)
    for i in range(BLOCKS):
        kv_t[:, i * T : (i + 1) * T] = got[i, 0:T].astype(f32).T.astype(bf16)
    lane = lax.broadcasted_iota(i32, (1, QCHUNK), 1)
    low_q = lax.broadcasted_iota(i32, (QCHUNK, 128), 1) < HD
    low_k = lax.broadcasted_iota(i32, (T, 128), 1) < HD
    key_row = lax.broadcasted_iota(i32, (T, QCHUNK), 0)
    for c in range(BLOCKS // QBLOCKS):
        qg = jnp.concatenate([got[c * QBLOCKS + b, T:ROWS] for b in range(QBLOCKS)], axis=0)
        q_only = jnp.where(low_q, qg.astype(f32), 0.0).astype(bf16)
        g_only = jnp.where(low_q, 0.0, qg.astype(f32)).astype(bf16)
        pos = (c * QBLOCKS + lane // HALF) * T + parity * HALF + lane % HALF
        begin = jnp.zeros((1, QCHUNK), i32)
        for k in range(DOCS):
            begin = jnp.maximum(begin, jnp.where(meta[2 + k] <= pos, meta[2 + k], 0))
        tiles = (c + 1) * QBLOCKS
        top = jnp.full((8, QCHUNK), MASKED, f32)
        for i in range(tiles):
            s = mm_nt(got[i, 0:T], q_only)
            allowed = key_row >= begin - i * T
            if i >= c * QBLOCKS:
                allowed = allowed & (key_row <= pos - i * T)
            s = jnp.where(allowed, s, MASKED)
            scores[i] = s
            top = jnp.maximum(top, jnp.max(s.reshape(T // 8, 8, QCHUNK), axis=0))
        top = jnp.max(top, axis=0, keepdims=True)
        total = jnp.zeros((8, QCHUNK), f32)
        cross = jnp.zeros((8, QCHUNK), f32)
        for i in range(tiles):
            p = jnp.exp2((scores[i] - top) * LOG2E)
            scores[i] = p
            g = mm_nt(got[i, 0:T], g_only)
            grads[i] = g
            total = total + jnp.sum(p.reshape(T // 8, 8, QCHUNK), axis=0)
            cross = cross + jnp.sum((p * g).reshape(T // 8, 8, QCHUNK), axis=0)
        inverse = 1.0 / jnp.sum(total, axis=0, keepdims=True)
        cross = jnp.sum(cross, axis=0, keepdims=True) * inverse
        out_t = jnp.zeros((128, QCHUNK), f32)
        dq_t = jnp.zeros((128, QCHUNK), f32)
        for i in range(tiles):
            prob = scores[i] * inverse
            low_p = prob.astype(bf16)
            low_s = (prob * (grads[i] - cross)).astype(bf16)
            turned = kv_t[:, i * T : (i + 1) * T]
            out_t = out_t + mm(turned, low_p)
            dq_t = dq_t + mm(turned, low_s)
            both = jnp.where(low_k, mm(low_s, qg), mm(low_p, qg))
            if i >= c * QBLOCKS:
                kv_grad[i] = both
            else:
                kv_grad[i] = kv_grad[i] + both
        pair = jnp.where(low_q, dq_t.T * (HD ** -0.5), out_t.T).astype(bf16)
        for b in range(QBLOCKS):
            send[c * QBLOCKS + b, T:ROWS] = pair[b * HALF : (b + 1) * HALF]
    for i in range(BLOCKS):
        send[i, 0:T] = kv_grad[i].astype(bf16)


def middle_back(
    meta, got, cot, middle, normed, gated, gate, ssm, act, step, bc, a_log, d_skip,
    w_o, w_q, w_k, w_v, w_out, gain,
    send, mixed, grad_mid_out, g_out, grad_gate_out,
    gw_o, gw_q, gw_k, gw_v, gw_out, g_gain, g_skip,
    att, dq, dk, dv, dec,
):
    low = lax.broadcasted_iota(i32, (HALF, 128), 1) < HALF
    low_t = lax.broadcasted_iota(i32, (T, 128), 1) < HALF
    for m in range(HEADS // 2):
        tile = slice(m * 128, (m + 1) * 128)
        for p in range(2):
            a = got[4 * m + p, T:ROWS].astype(f32)
            b = got[4 * m + 2 + p, T:ROWS].astype(f32)
            rows = slice(p * HALF, (p + 1) * HALF)
            dq[rows, tile] = jnp.where(low, a, roll_half(b)).astype(bf16)
            att[rows, tile] = jnp.where(low, roll_half(a), b).astype(bf16)
        a = got[4 * m, 0:T].astype(f32) + got[4 * m + 1, 0:T].astype(f32)
        b = got[4 * m + 2, 0:T].astype(f32) + got[4 * m + 3, 0:T].astype(f32)
        dk[:, tile] = jnp.where(low_t, a, roll_half(b)).astype(bf16)
        dv[:, tile] = jnp.where(low_t, roll_half(a), b).astype(bf16)
    cot_low = cot[...]
    values = middle[...]
    mixed[...] = (values + mm(att[...], w_o[...])).astype(bf16)
    gw_o[...] = mm_tn(att[...], cot_low)
    gw_q[...] = mm_tn(normed[...], dq[...])
    gw_k[...] = mm_tn(normed[...], dk[...])
    gw_v[...] = mm_tn(normed[...], dv[...])
    upstream = mm_nt(dq[...], w_q[...]) + mm_nt(dk[...], w_k[...]) + mm_nt(dv[...], w_v[...])
    back, gain_grad = norm_back(values, inverse_rms(values), gain[...], upstream)
    g_gain[...] = gain_grad
    grad_mid = cot_low.astype(f32) + back
    grad_mid_out[...] = grad_mid
    mid_low = grad_mid.astype(bf16)
    gw_out[...] = mm_tn(gated[...], mid_low)
    grad_gated = mm_nt(mid_low, w_out[...]).astype(bf16).astype(f32)
    gates = gate[...].astype(f32)
    sig = sigmoid(gates)
    g = grad_gated * (gates * sig)
    g_out[...] = g
    grad_gate_out[...] = (grad_gated * ssm[...] * (sig * (1.0 + gates * (1.0 - sig)))).astype(bf16)
    g_skip[...] = jnp.sum(g * act[...].astype(f32), axis=0, keepdims=True)
    dec[...] = step[...] + reset_of(meta, columns(0, meta))
    for c in range(E // CHUNK):
        part = slice(c * CHUNK, (c + 1) * CHUNK)
        rates2 = -jnp.exp(a_log[:, part]) * LOG2E

        def block(turn, carry):
            i = T // STEPS - 1 - turn
            cols = bc[i]
            base = pl.multiple_of(i * STEPS, STEPS)
            for k in reversed(range(STEPS)):
                t = base + k
                adjoint = g_out[pl.ds(t, 1), part] * cols[N : 2 * N, k : k + 1] + carry
                carry = jnp.exp2(dec[pl.ds(t, 1), part] * rates2) * adjoint
            return carry

        carry = lax.fori_loop(0, T // STEPS, block, jnp.zeros((N, CHUNK), f32))
        send[:, part] = carry.astype(bf16)


def mamba_back(
    meta, got, forward, start, g, act, step, pre, bc, dt_low, conv, ext_low, a_log, d_skip,
    conv_w, w_x, w_dt,
    own_out, edge_out, gw_x, gw_dt, g_dt_b, g_a_log, g_conv_w, g_conv_b,
    dec, sa, decay, kept, gs, ab, ext, padded,
):
    place = meta[1]
    dec[...] = step[...] + reset_of(meta, columns(0, meta))
    act_f = act[...].astype(f32)
    sa[...] = step[...] * act_f
    lane = lax.broadcasted_iota(i32, (N, 128), 1)
    grad_b = jnp.zeros((N, 128), f32)
    grad_c = jnp.zeros((N, 128), f32)
    for c in range(E // CHUNK):
        part = slice(c * CHUNK, (c + 1) * CHUNK)
        rates = -jnp.exp(a_log[:, part])
        rates2 = rates * LOG2E

        def join(turn, state):
            j = BLOCKS - 1 - turn
            tail = forward[j, N : N + 8, part].astype(f32)
            total = tail[0:1] + tail[1:2]
            return jnp.exp2(rates2 * total) * state + got[j, :, part].astype(f32)

        carry = lax.fori_loop(0, BLOCKS - 1 - place, join, jnp.zeros((N, CHUNK), f32))

        def ahead(i, state):
            h, acc = state
            cols = bc[i]
            base = pl.multiple_of(i * STEPS, STEPS)
            for k in range(STEPS):
                t = base + k
                factor = jnp.exp2(dec[pl.ds(t, 1), part] * rates2)
                moved = factor * h
                decay[t] = factor
                kept[t] = moved
                h = moved + cols[0:N, k : k + 1] * sa[pl.ds(t, 1), part]
                col = jnp.sum(h * g[pl.ds(t, 1), part], axis=1, keepdims=True)
                acc = acc + jnp.where(lane == t, col, 0.0)
            return h, acc

        _, grad_c = lax.fori_loop(0, T // STEPS, ahead, (start[:, part], grad_c))

        def behind(turn, state):
            carry, acc, along = state
            i = T // STEPS - 1 - turn
            cols = bc[i]
            base = pl.multiple_of(i * STEPS, STEPS)
            for k in reversed(range(STEPS)):
                t = base + k
                adjoint = g[pl.ds(t, 1), part] * cols[N : 2 * N, k : k + 1] + carry
                carry = decay[t] * adjoint
                log_grad = adjoint * kept[t]
                along = along + log_grad * step[pl.ds(t, 1), part]
                gs[pl.ds(t, 1), part] = jnp.sum(log_grad * rates, axis=0, keepdims=True)
                ab[pl.ds(t, 1), part] = jnp.sum(adjoint * cols[0:N, k : k + 1], axis=0, keepdims=True)
                col = jnp.sum(adjoint * sa[pl.ds(t, 1), part], axis=1, keepdims=True)
                acc = acc + jnp.where(lane == t, col, 0.0)
            return carry, acc, along

        _, grad_b, along = lax.fori_loop(
            0, T // STEPS, behind, (carry, grad_b, jnp.zeros((N, CHUNK), f32))
        )
        g_a_log[:, part] = along * rates
    adjoint_b = ab[...]
    grad_step = gs[...] + adjoint_b * act_f
    grad_act = g[...] * d_skip[...] + adjoint_b * step[...]
    grad_pre = (grad_step * sigmoid(pre[...])).astype(bf16)
    g_dt_b[...] = jnp.sum(grad_pre.astype(f32), axis=0, keepdims=True)
    gw_dt[...] = mm_tn(dt_low[...], grad_pre)
    turned = jnp.concatenate([grad_b, grad_c, jnp.zeros((128 - 2 * N, 128), f32)], axis=0).T
    grad_proj = jnp.concatenate([mm_nt(grad_pre, w_dt[...]), turned[:, 0 : 2 * N]], axis=1).astype(bf16)
    gw_x[...] = mm_tn(act[...], grad_proj)
    grad_act = grad_act + mm_nt(grad_proj, w_x[...])
    grad_conv = grad_act * silu_slope(conv[...])
    g_conv_b[...] = jnp.sum(grad_conv, axis=0, keepdims=True)
    padded[0:T] = grad_conv
    padded[T : T + 8] = jnp.zeros((8, E), f32)
    ext[...] = ext_low[...].astype(f32)
    own_doc = doc_of(meta, columns(0, meta))
    own = jnp.zeros((T, E), f32)
    lift = KERNEL - 1
    rows = lax.broadcasted_iota(i32, (T, 1), 0)
    for offset in range(KERNEL):
        same = (doc_of(meta, columns(offset - lift, meta)) == own_doc).astype(f32)
        low = HALO - lift + offset
        g_conv_w[offset : offset + 1] = jnp.sum(grad_conv * ext[low : low + T] * same, axis=0, keepdims=True)
        up = lift - offset
        ahead_same = (doc_of(meta, columns(0, meta)) == doc_of(meta, columns(up, meta))) & (rows < T - up)
        own = own + conv_w[offset : offset + 1] * padded[up : up + T] * ahead_same.astype(f32)
    own_out[...] = own
    first = meta[0]
    edges = []
    for row in range(lift):
        edge = jnp.zeros((1, E), f32)
        here = doc_of(meta, first - lift + row + jnp.zeros((1, 1), i32))
        for offset in range(row + 1):
            at = row - offset
            same = (doc_of(meta, first + at + jnp.zeros((1, 1), i32)) == here).astype(f32)
            edge = edge + conv_w[offset : offset + 1] * padded[at : at + 1] * same
        edges.append(edge)
    edge_out[...] = jnp.concatenate(edges + [jnp.zeros((8 - lift, E), f32)], axis=0)


def input_back(
    tokens, gain, w_in, own, edge, grad_gate, grad_mid,
    grad_tokens, gw_in, g_gain, full,
):
    full[...] = own[...]
    lift = KERNEL - 1
    full[T - lift : T] = own[T - lift : T] + edge[0:lift]
    values = tokens[...].astype(f32)
    inverse = inverse_rms(values)
    normed = (values * inverse * gain[...]).astype(bf16)
    grad_input = full[...].astype(bf16)
    gate = grad_gate[...]
    gw_in[:, :E] = mm_tn(normed, grad_input)
    gw_in[:, E:] = mm_tn(normed, gate)
    upstream = mm_nt(grad_input, w_in[:, :E]) + mm_nt(gate, w_in[:, E:])
    back, gain_grad = norm_back(values, inverse, gain[...], upstream)
    grad_tokens[...] = grad_mid[...] + back
    g_gain[...] = gain_grad


def call(body, name, outs, scratch, *args, smem=True):
    specs = [pl.BlockSpec(memory_space=pltpu.VMEM)] * len(args)
    if smem:
        specs[0] = pl.BlockSpec(memory_space=pltpu.SMEM)
    return pl.pallas_call(
        body,
        name=name,
        out_shape=[jax.ShapeDtypeStruct(s, t) for s, t in outs],
        in_specs=specs,
        out_specs=[pl.BlockSpec(memory_space=pltpu.VMEM)] * len(outs),
        scratch_shapes=[pltpu.VMEM(s, t) for s, t in scratch],
        compiler_params=pltpu.CompilerParams(vmem_limit_bytes=56 * 1024 * 1024),
    )(*args)


def shift(x, by):
    pairs = [(i, i + by) for i in range(BLOCKS) if 0 <= i + by < BLOCKS]
    return lax.ppermute(x, PLACE, pairs)


def swap(x):
    return lax.all_to_all(x, PLACE, 0, 0, tiled=True)


def spread(x):
    return swap(jnp.broadcast_to(x[None], (BLOCKS,) + x.shape))


def layer(
    tokens, starts, gain_one, w_in, conv_w, conv_b, w_x, w_dt, dt_bias, a_log, d_skip, w_out,
    gain_two, w_q, w_k, w_v, w_o, cotangent,
):
    tokens, cot = tokens[0], cotangent[0]
    place = lax.axis_index(PLACE)
    meta = jnp.concatenate([jnp.stack([place * T, place]).astype(i32), starts[0]])
    row = lambda v: v.reshape(1, -1)
    halo = shift(tokens[T - HALO :], 1)
    grad_att = mm_nt(cot, w_o).astype(bf16)
    te, tel = ((T, E), f32), ((T, E), bf16)
    send, ext, gate, conv, act, step, pre, bc, dt_low, _ = call(
        mamba_in, "mamba_in",
        [((N + 8, E), bf16), ((HALO + T, E), bf16), tel, te, tel, te, te,
         ((T // STEPS, 2 * N, 128), f32), ((T, R), bf16), ((1, E), f32)],
        [((HALO + T, E), f32), te, te, ((T, 128), f32)],
        meta, tokens, halo, row(gain_one), w_in, conv_w, row(conv_b), w_x, w_dt, row(dt_bias), a_log,
    )
    forward = spread(send)
    packed, start, ssm, gated, middle, normed = call(
        mamba_out, "mamba_out",
        [((BLOCKS, ROWS, 128), bf16), ((N, E), f32), te, tel, ((T, D), f32), ((T, D), bf16)],
        [te, te, te],
        meta, forward, tokens, step, act, bc, gate, a_log, row(d_skip), w_out, row(gain_two),
        w_q, w_k, w_v, grad_att,
    )
    (back,) = call(
        attention, "attention",
        [((BLOCKS, ROWS, 128), bf16)],
        [((128, BLOCKS * T), bf16), ((BLOCKS, T, QCHUNK), f32), ((BLOCKS, T, QCHUNK), f32),
         ((BLOCKS, T, 128), f32)],
        meta, swap(packed),
    )
    send, mixed, grad_mid, g, grad_gate, gw_o, gw_q, gw_k, gw_v, gw_out, g_gain_two, g_skip = call(
        middle_back, "middle_back",
        [((N, E), bf16), ((T, D), bf16), ((T, D), f32), te, tel,
         ((D, D), f32), ((D, D), f32), ((D, D), f32), ((D, D), f32), ((E, D), f32),
         ((1, D), f32), ((1, E), f32)],
        [((T, D), bf16)] * 4 + [te],
        meta, swap(back), cot, middle, normed, gated, gate, ssm, act, step, bc, a_log, row(d_skip),
        w_o, w_q, w_k, w_v, w_out, row(gain_two),
    )
    own, edge, gw_x, gw_dt, g_dt_b, g_a_log, g_conv_w, g_conv_b = call(
        mamba_back, "mamba_back",
        [te, ((8, E), f32), ((E, R + 2 * N), f32), ((R, E), f32), ((1, E), f32), ((N, E), f32),
         ((KERNEL, E), f32), ((1, E), f32)],
        [te, te, ((T, N, CHUNK), f32), ((T, N, CHUNK), f32), te, te, ((HALO + T, E), f32),
         ((T + 8, E), f32)],
        meta, spread(send), forward, start, g, act, step, pre, bc, dt_low, conv, ext, a_log,
        row(d_skip), conv_w, w_x, w_dt,
    )
    grad_tokens, gw_in, g_gain_one = call(
        input_back, "input_back",
        [((T, D), f32), ((D, 2 * E), f32), ((1, D), f32)],
        [te],
        tokens, row(gain_one), w_in, own, shift(edge, -1), grad_gate, grad_mid,
        smem=False,
    )
    summed = lax.psum(
        (g_gain_one[0], gw_in, g_conv_w, g_conv_b[0], gw_x, gw_dt, g_dt_b[0], g_a_log, g_skip[0],
         gw_out, g_gain_two[0], gw_q, gw_k, gw_v, gw_o),
        ALL,
    )
    return (mixed[None], grad_tokens[None]) + tuple(summed)


def solution(mesh):
    rows, seq, head = mesh.devices.shape
    fine = Mesh(mesh.devices.reshape(rows // 2, 2, seq, head), ALL)
    split = P(("y", "core"), PLACE, None)
    return jax.shard_map(
        layer,
        mesh=fine,
        in_specs=(split, P(("y", "core"), None)) + (P(),) * 15 + (split,),
        out_specs=(split, split) + (P(),) * 15,
        check_vma=False,
    )
```

```python
import functools

import jax
import jax.numpy as jnp
from jax import lax
from jax.experimental import pallas as pl
from jax.experimental.pallas import tpu as pltpu
from jax.sharding import Mesh, PartitionSpec as P

T, D, E, N, R, HD = 128, 512, 1024, 16, 32, 64
HEADS, BLOCKS, HALF, DOCS, KERNEL, HALO = 8, 16, 64, 6, 4, 16
LANES, STEPS = 128, 8
TILES = [slice(q * LANES, (q + 1) * LANES) for q in range(E // LANES)]
ROWS = T + HALF
RESET = 1e4
LOG2E = 1.4426950408889634
EPS = 1e-05
MASKED = -1e30
PLACE = ("seq", "head")
ALL = ("y", "core", "seq", "head")
SAME, SHARES, MAIN, SMALL = ("y", "seq", "head"), 64, 32, 8
bf16, f32, i32 = jnp.bfloat16, jnp.float32, jnp.int32


def mm(a, b):
    return jnp.dot(a, b, preferred_element_type=f32)


def mm_nt(a, b):
    return lax.dot_general(a, b, (((1,), (1,)), ((), ())), preferred_element_type=f32)


def mm_tn(a, b):
    return lax.dot_general(a, b, (((0,), (0,)), ((), ())), preferred_element_type=f32)


def doc_of(meta, pos):
    count = jnp.zeros(pos.shape, i32)
    for k in range(DOCS):
        count = count + (meta[2 + k] <= pos).astype(i32)
    return count


def reset_of(meta, pos):
    hit = meta[2] == pos
    for k in range(1, DOCS):
        hit = hit | (meta[2 + k] == pos)
    return jnp.where(hit, RESET, 0.0)


def inverse_rms(x):
    return lax.rsqrt(jnp.mean(x * x, axis=-1, keepdims=True) + EPS)


def sigmoid(x):
    return 1.0 / (1.0 + jnp.exp(-x))


def silu_slope(x):
    s = sigmoid(x)
    return s * (1.0 + x * (1.0 - s))


def norm_back(values, inverse, gain, upstream):
    scaled = upstream * gain
    inner = jnp.mean(values * scaled, axis=-1, keepdims=True)
    back = inverse * scaled - values * (inverse * inverse * inverse) * inner
    return back, jnp.sum(upstream * values * inverse, axis=0, keepdims=True)


def columns(offset, meta):
    first = meta[0]
    return first + offset + lax.broadcasted_iota(i32, (T, 1), 0)


def stack_sums(parts):
    row = lax.broadcasted_iota(i32, parts[0].shape, 0)
    for by in (1, 2, 4):
        first = (row & by) == 0
        parts = [
            jnp.where(first, a, b) + pltpu.roll(jnp.where(first, b, a), by, axis=0)
            for a, b in zip(parts[0::2], parts[1::2])
        ]
    return parts[0]


def column(block, low, k):
    return jnp.broadcast_to(block[low : low + N, k : k + 1], (N, LANES))


def halves(x):
    return x[0:8] + x[8:16]


def scan_forward(dec, sa, bc, rates2, start, result=None):
    def block(i, states):
        states = list(states)
        base = pl.multiple_of(i * STEPS, STEPS)
        cols = bc[i]
        sums = [[None] * STEPS for _ in TILES]
        for k in range(STEPS):
            b_col = column(cols, 0, k)
            c_col = column(cols, N, k)
            for q, tile in enumerate(TILES):
                factor = jnp.exp2(dec[pl.ds(base, STEPS), tile][k : k + 1] * rates2[:, tile])
                states[q] = factor * states[q] + b_col * sa[pl.ds(base, STEPS), tile][k : k + 1]
                if result is not None:
                    sums[q][k] = halves(states[q] * c_col)
        if result is not None:
            for q, tile in enumerate(TILES):
                result[pl.ds(base, STEPS), tile] = stack_sums(sums[q])
        return tuple(states)

    return lax.fori_loop(0, T // STEPS, block, tuple(start[:, tile] for tile in TILES))


def mamba_in(
    meta, tokens, halo, gain, w_in, conv_w, conv_b, w_x, w_dt, dt_b, a_log, cot, w_o,
    send, grad_att, low_out, ext_out, gate_out, conv_out, act_out, step_out, pre_out, bc_out, dt_out,
    ext, dec, sa, xp, end, rates2, zero,
):
    grad_att[...] = mm_nt(cot[...], w_o[...]).astype(bf16)
    own = tokens[...].astype(f32)
    before = halo[...].astype(f32)
    low_own = (own * inverse_rms(own) * gain[...]).astype(bf16)
    low_before = (before * inverse_rms(before) * gain[...]).astype(bf16)
    conv_own = mm(low_own, w_in[:, :E]).astype(bf16)
    conv_before = mm(low_before, w_in[:, :E]).astype(bf16)
    low_out[0:HALO] = low_before
    low_out[HALO : HALO + T] = low_own
    ext_out[0:HALO] = conv_before
    ext_out[HALO : HALO + T] = conv_own
    ext[0:HALO] = conv_before.astype(f32)
    ext[HALO : HALO + T] = conv_own.astype(f32)
    gate_out[...] = mm(low_own, w_in[:, E:]).astype(bf16)
    own_doc = doc_of(meta, columns(0, meta))
    conv = jnp.broadcast_to(conv_b[...], (T, E))
    for offset in range(KERNEL):
        same = (doc_of(meta, columns(offset - KERNEL + 1, meta)) == own_doc).astype(f32)
        low = HALO - KERNEL + 1 + offset
        conv = conv + conv_w[offset : offset + 1] * ext[low : low + T] * same
    conv_out[...] = conv
    act = (conv * sigmoid(conv)).astype(bf16)
    act_out[...] = act
    proj = mm_nt(act, w_x[...])
    dt_low = proj[:, :R].astype(bf16)
    dt_out[...] = dt_low
    pre = mm(dt_low, w_dt[...]) + dt_b[...]
    pre_out[...] = pre
    step = jnp.maximum(pre, 0.0) + jnp.log1p(jnp.exp(-jnp.abs(pre)))
    step_out[...] = step
    held = step + reset_of(meta, columns(0, meta))
    dec[...] = held
    sa[...] = step * act.astype(f32)
    xp[...] = jnp.zeros((T, 128), f32)
    xp[:, 0 : R + 2 * N] = proj
    turned = xp[...].T
    for i in range(T // STEPS):
        bc_out[i, :, 0:STEPS] = turned[R : R + 2 * N, i * STEPS : (i + 1) * STEPS]
    total = jnp.sum(held, axis=0, keepdims=True)
    high = total.astype(bf16)
    rest = (total - high.astype(f32)).astype(bf16)
    end[N : N + 8] = jnp.concatenate([high.astype(f32), rest.astype(f32), jnp.zeros((6, E), f32)], axis=0)
    rates2[...] = -jnp.exp(a_log[...]) * LOG2E
    zero[...] = jnp.zeros((N, E), f32)
    states = scan_forward(dec, sa, bc_out, rates2, zero)
    for q, tile in enumerate(TILES):
        end[0:N, tile] = states[q]
    ended = end[...].astype(bf16)
    for j in range(BLOCKS):
        send[j] = ended


def roll_half(x):
    return pltpu.roll(x, HALF, axis=1)


def mamba_out(
    meta, got, tokens, step, act, bc, gate, a_log, d_skip, w_out, gain, w_q, w_k, w_v, grad_att,
    send, start_out, ssm_out, gated_out, middle_out, normed_out,
    dec, sa, ssm, rates2,
):
    place = meta[1]
    rates2[...] = -jnp.exp(a_log[...]) * LOG2E
    dec[...] = step[...] + reset_of(meta, columns(0, meta))
    act_f = act[...].astype(f32)
    sa[...] = step[...] * act_f

    def join(j, state):
        tail = got[j, N : N + 8].astype(f32)
        total = tail[0:1] + tail[1:2]
        return jnp.exp2(rates2[...] * total) * state + got[j, 0:N].astype(f32)

    start_out[...] = lax.fori_loop(0, place, join, jnp.zeros((N, E), f32))
    scan_forward(dec, sa, bc, rates2, start_out, ssm)
    result = ssm[...] + d_skip[...] * act_f
    ssm_out[...] = result
    gates = gate[...].astype(f32)
    gated = (result * (gates * sigmoid(gates))).astype(bf16)
    gated_out[...] = gated
    middle = tokens[...].astype(f32) + mm(gated, w_out[...])
    middle_out[...] = middle
    normed = (middle * inverse_rms(middle) * gain[...]).astype(bf16)
    normed_out[...] = normed
    queries = mm(normed, w_q[...]).astype(bf16).astype(f32) * (HD ** -0.5)
    keys = mm(normed, w_k[...])
    vals = mm(normed, w_v[...])
    grads = grad_att[...].astype(f32)
    low = lax.broadcasted_iota(i32, (T, 128), 1) < HALF
    for m in range(HEADS // 2):
        tile = slice(m * 128, (m + 1) * 128)
        for odd in range(2):
            for first, second, at, rows in ((keys, vals, 0, T), (queries, grads, T, HALF)):
                a, b = first[:, tile], second[:, tile]
                pair = jnp.where(low, a, roll_half(b)) if odd == 0 else jnp.where(low, roll_half(a), b)
                pair = pair.astype(bf16)
                dest = 2 * (2 * m + odd)
                if rows == T:
                    send[dest, 0:T] = pair
                    send[dest + 1, 0:T] = pair
                else:
                    send[dest, T:ROWS] = pair[0:HALF]
                    send[dest + 1, T:ROWS] = pair[HALF:T]


QCHUNK, QBLOCKS = 256, 4


def attention(meta, got, send, kv_t, scores, grads, kv_grad):
    parity = lax.rem(meta[1], 2)
    for i in range(BLOCKS):
        kv_t[:, i * T : (i + 1) * T] = got[i, 0:T].astype(f32).T.astype(bf16)
    lane = lax.broadcasted_iota(i32, (1, QCHUNK), 1)
    low_q = lax.broadcasted_iota(i32, (QCHUNK, 128), 1) < HD
    low_k = lax.broadcasted_iota(i32, (T, 128), 1) < HD
    key_row = lax.broadcasted_iota(i32, (T, QCHUNK), 0)
    for c in range(BLOCKS // QBLOCKS):
        qg = jnp.concatenate([got[c * QBLOCKS + b, T:ROWS] for b in range(QBLOCKS)], axis=0)
        q_only = jnp.where(low_q, qg.astype(f32), 0.0).astype(bf16)
        g_only = jnp.where(low_q, 0.0, qg.astype(f32)).astype(bf16)
        pos = (c * QBLOCKS + lane // HALF) * T + parity * HALF + lane % HALF
        begin = jnp.zeros((1, QCHUNK), i32)
        for k in range(DOCS):
            begin = jnp.maximum(begin, jnp.where(meta[2 + k] <= pos, meta[2 + k], 0))
        tiles = (c + 1) * QBLOCKS
        top = jnp.full((8, QCHUNK), MASKED, f32)
        for i in range(tiles):
            s = mm_nt(got[i, 0:T], q_only)
            allowed = key_row >= begin - i * T
            if i >= c * QBLOCKS:
                allowed = allowed & (key_row <= pos - i * T)
            s = jnp.where(allowed, s, MASKED)
            scores[i] = s
            top = jnp.maximum(top, jnp.max(s.reshape(T // 8, 8, QCHUNK), axis=0))
        top = jnp.max(top, axis=0, keepdims=True)
        total = jnp.zeros((8, QCHUNK), f32)
        cross = jnp.zeros((8, QCHUNK), f32)
        for i in range(tiles):
            p = jnp.exp2((scores[i] - top) * LOG2E)
            scores[i] = p
            g = mm_nt(got[i, 0:T], g_only)
            grads[i] = g
            total = total + jnp.sum(p.reshape(T // 8, 8, QCHUNK), axis=0)
            cross = cross + jnp.sum((p * g).reshape(T // 8, 8, QCHUNK), axis=0)
        inverse = 1.0 / jnp.sum(total, axis=0, keepdims=True)
        cross = jnp.sum(cross, axis=0, keepdims=True) * inverse
        out_t = jnp.zeros((128, QCHUNK), f32)
        dq_t = jnp.zeros((128, QCHUNK), f32)
        for i in range(tiles):
            prob = scores[i] * inverse
            low_p = prob.astype(bf16)
            low_s = (prob * (grads[i] - cross)).astype(bf16)
            turned = kv_t[:, i * T : (i + 1) * T]
            out_t = out_t + mm(turned, low_p)
            dq_t = dq_t + mm(turned, low_s)
            both = jnp.where(low_k, mm(low_s, qg), mm(low_p, qg))
            if i >= c * QBLOCKS:
                kv_grad[i] = both
            else:
                kv_grad[i] = kv_grad[i] + both
        pair = jnp.where(low_q, dq_t.T * (HD ** -0.5), out_t.T).astype(bf16)
        for b in range(QBLOCKS):
            send[c * QBLOCKS + b, T:ROWS] = pair[b * HALF : (b + 1) * HALF]
    for i in range(BLOCKS):
        send[i, 0:T] = kv_grad[i].astype(bf16)


def middle_back(
    meta, got, cot, middle, normed, low_ext, gated, gate, ssm, act, step, bc, a_log, d_skip,
    w_o, w_q, w_k, w_v, w_out, gain,
    send, mixed, grad_mid_out, g_out, grad_gate_out, keep, give, g_gain, g_skip,
    att, dq, dk, dv, dec, end, rates2,
):
    low = lax.broadcasted_iota(i32, (HALF, 128), 1) < HALF
    low_t = lax.broadcasted_iota(i32, (T, 128), 1) < HALF
    for m in range(HEADS // 2):
        tile = slice(m * 128, (m + 1) * 128)
        for p in range(2):
            a = got[4 * m + p, T:ROWS].astype(f32)
            b = got[4 * m + 2 + p, T:ROWS].astype(f32)
            rows = slice(p * HALF, (p + 1) * HALF)
            dq[rows, tile] = jnp.where(low, a, roll_half(b)).astype(bf16)
            att[rows, tile] = jnp.where(low, roll_half(a), b).astype(bf16)
        a = got[4 * m, 0:T].astype(f32) + got[4 * m + 1, 0:T].astype(f32)
        b = got[4 * m + 2, 0:T].astype(f32) + got[4 * m + 3, 0:T].astype(f32)
        dk[:, tile] = jnp.where(low_t, a, roll_half(b)).astype(bf16)
        dv[:, tile] = jnp.where(low_t, roll_half(a), b).astype(bf16)
    cot_low = cot[...]
    values = middle[...]
    mixed[...] = (values + mm(att[...], w_o[...])).astype(bf16)
    upstream = mm_nt(dq[...], w_q[...]) + mm_nt(dk[...], w_k[...]) + mm_nt(dv[...], w_v[...])
    back, gain_grad = norm_back(values, inverse_rms(values), gain[...], upstream)
    g_gain[...] = gain_grad
    grad_mid = cot_low.astype(f32) + back
    grad_mid_out[...] = grad_mid
    mid_low = grad_mid.astype(bf16)
    grad_gated = mm_nt(mid_low, w_out[...]).astype(bf16).astype(f32)
    gates = gate[...].astype(f32)
    sig = sigmoid(gates)
    g = grad_gated * (gates * sig)
    g_out[...] = g
    grad_gate = (grad_gated * ssm[...] * (sig * (1.0 + gates * (1.0 - sig)))).astype(bf16)
    grad_gate_out[...] = grad_gate
    for first, second, core in ((keep, give, 0), (give, keep, 1)):

        @pl.when(meta[2 + DOCS] == core)
        def _():
            first[:, 0:D] = att[...]
            first[:, D : 2 * D] = cot_low
            first[:, 2 * D : 3 * D] = normed[...]
            first[:, 3 * D : 4 * D] = dq[...]
            first[:, 4 * D : 5 * D] = dk[...]
            first[:, 5 * D : 6 * D] = dv[...]
            second[:, 0:E] = gated[...]
            second[:, E : E + D] = mid_low
            second[:, E + D : 2 * E] = low_ext[HALO : HALO + T]
            second[:, 2 * E : 3 * E] = grad_gate

    g_skip[...] = jnp.sum(g * act[...].astype(f32), axis=0, keepdims=True)
    dec[...] = step[...] + reset_of(meta, columns(0, meta))
    rates2[...] = -jnp.exp(a_log[...]) * LOG2E

    def block(turn, carry):
        carry = list(carry)
        i = T // STEPS - 1 - turn
        base = pl.multiple_of(i * STEPS, STEPS)
        cols = bc[i]
        for k in reversed(range(STEPS)):
            c_col = column(cols, N, k)
            for q, tile in enumerate(TILES):
                factor = jnp.exp2(dec[pl.ds(base, STEPS), tile][k : k + 1] * rates2[:, tile])
                carry[q] = factor * (carry[q] + c_col * g_out[pl.ds(base, STEPS), tile][k : k + 1])
        return tuple(carry)

    carry = lax.fori_loop(0, T // STEPS, block, tuple(jnp.zeros((N, LANES), f32) for _ in TILES))
    for q, tile in enumerate(TILES):
        end[:, tile] = carry[q]
    ended = end[...].astype(bf16)
    for j in range(BLOCKS):
        send[j] = ended


def mamba_back(
    meta, got, forward, start, g, act, step, pre, bc, dt_low, conv, ext_low, a_log, d_skip,
    conv_w, w_x, w_dt, tokens, halo, gain, w_in, grad_gate, grad_mid, g_gain_two, g_skip,
    grad_tokens, tail, keep, give, part_keep,
    dec, sa, decay, kept, gs, ab, ext, padded, grad_ext, vec, wide, rates, rates2, sum_b, sum_c,
):
    place = meta[1]
    dec[...] = step[...] + reset_of(meta, columns(0, meta))
    act_f = act[...].astype(f32)
    sa[...] = step[...] * act_f
    rates[...] = -jnp.exp(a_log[...])
    rates2[...] = rates[...] * LOG2E

    def join(turn, state):
        j = BLOCKS - 1 - turn
        tail = forward[j, N : N + 8].astype(f32)
        total = tail[0:1] + tail[1:2]
        return jnp.exp2(rates2[...] * total) * state + got[j].astype(f32)

    wide[R : R + N] = lax.fori_loop(0, BLOCKS - 1 - place, join, jnp.zeros((N, E), f32))

    def ahead(i, states):
        states = list(states)
        base = pl.multiple_of(i * STEPS, STEPS)
        cols = bc[i]
        for k in range(STEPS):
            b_col = column(cols, 0, k)
            total = jnp.zeros((N, LANES), f32)
            for q, tile in enumerate(TILES):
                rows = pl.ds(base, STEPS), tile
                factor = jnp.exp2(dec[rows][k : k + 1] * rates2[:, tile])
                moved = factor * states[q]
                decay[base + k, :, tile] = factor
                kept[base + k, :, tile] = moved
                states[q] = moved + b_col * sa[rows][k : k + 1]
                total = total + states[q] * g[rows][k : k + 1]
            sum_c[base + k] = total
        return tuple(states)

    lax.fori_loop(0, T // STEPS, ahead, tuple(start[:, tile] for tile in TILES))
    first_carry = tuple(wide[R : R + N, tile] for tile in TILES)
    wide[R + N : R + 2 * N] = jnp.zeros((N, E), f32)

    def behind(turn, carry):
        carry = list(carry)
        i = T // STEPS - 1 - turn
        base = pl.multiple_of(i * STEPS, STEPS)
        cols = bc[i]
        by_rate = [[None] * STEPS for _ in TILES]
        by_b = [[None] * STEPS for _ in TILES]
        along = [wide[R + N : R + 2 * N, tile] for tile in TILES]
        for k in reversed(range(STEPS)):
            b_col = column(cols, 0, k)
            c_col = column(cols, N, k)
            total = jnp.zeros((N, LANES), f32)
            for q, tile in enumerate(TILES):
                rows = pl.ds(base, STEPS), tile
                adjoint = g[rows][k : k + 1] * c_col + carry[q]
                carry[q] = decay[base + k, :, tile] * adjoint
                log_grad = adjoint * kept[base + k, :, tile]
                along[q] = along[q] + log_grad * step[rows][k : k + 1]
                by_rate[q][k] = halves(log_grad * rates[:, tile])
                by_b[q][k] = halves(adjoint * b_col)
                total = total + adjoint * sa[rows][k : k + 1]
            sum_b[base + k] = total
        for q, tile in enumerate(TILES):
            wide[R + N : R + 2 * N, tile] = along[q]
            gs[pl.ds(base, STEPS), tile] = stack_sums(by_rate[q])
            ab[pl.ds(base, STEPS), tile] = stack_sums(by_b[q])
        return tuple(carry)

    lax.fori_loop(0, T // STEPS, behind, first_carry)
    wide[R : R + N] = wide[R + N : R + 2 * N] * rates[...]
    lane = lax.broadcasted_iota(i32, (LANES, LANES), 1)
    turned = jnp.zeros((T, LANES), f32)
    for at, sums in ((0, sum_b), (N, sum_c)):
        for n in range(N):
            one = (lane == at + n).astype(f32).astype(bf16)
            values = sums[:, n, :]
            high = values.astype(bf16)
            turned = turned + mm(high, one) + mm((values - high.astype(f32)).astype(bf16), one)
    adjoint_b = ab[...]
    grad_step = gs[...] + adjoint_b * act_f
    grad_act = g[...] * d_skip[...] + adjoint_b * step[...]
    grad_pre = (grad_step * sigmoid(pre[...])).astype(bf16)
    vec[...] = jnp.zeros((N, E), f32)
    vec[KERNEL + 1 : KERNEL + 2] = jnp.sum(grad_pre.astype(f32), axis=0, keepdims=True)
    vec[KERNEL + 2 : KERNEL + 3] = g_skip[...]
    wide[0:R] = mm_tn(dt_low[...], grad_pre)
    grad_proj = jnp.concatenate([mm_nt(grad_pre, w_dt[...]), turned[:, 0 : 2 * N]], axis=1).astype(bf16)
    gw_x = mm_tn(grad_proj, act[...])
    grad_act = grad_act + mm(grad_proj, w_x[...])
    grad_conv = grad_act * silu_slope(conv[...])
    vec[KERNEL : KERNEL + 1] = jnp.sum(grad_conv, axis=0, keepdims=True)
    padded[0:T] = grad_conv
    padded[T : T + 8] = jnp.zeros((8, E), f32)
    ext[...] = ext_low[...].astype(f32)
    own_doc = doc_of(meta, columns(0, meta))
    own = jnp.zeros((T, E), f32)
    lift = KERNEL - 1
    rows = lax.broadcasted_iota(i32, (T, 1), 0)
    for offset in range(KERNEL):
        same = (doc_of(meta, columns(offset - lift, meta)) == own_doc).astype(f32)
        low = HALO - lift + offset
        vec[offset : offset + 1] = jnp.sum(grad_conv * ext[low : low + T] * same, axis=0, keepdims=True)
        up = lift - offset
        ahead_same = (doc_of(meta, columns(0, meta)) == doc_of(meta, columns(up, meta))) & (rows < T - up)
        own = own + conv_w[offset : offset + 1] * padded[up : up + T] * ahead_same.astype(f32)
    grad_ext[HALO : HALO + T] = own
    first = meta[0]
    edges = [jnp.zeros((HALO - lift, E), f32)]
    for row in range(lift):
        edge = jnp.zeros((1, E), f32)
        here = doc_of(meta, first - lift + row + jnp.zeros((1, 1), i32))
        for offset in range(row + 1):
            at = row - offset
            same = (doc_of(meta, first + at + jnp.zeros((1, 1), i32)) == here).astype(f32)
            edge = edge + conv_w[offset : offset + 1] * padded[at : at + 1] * same
        edges.append(edge)
    grad_ext[0:HALO] = jnp.concatenate(edges, axis=0)
    low_edge = grad_ext[0:HALO].astype(bf16)
    low_own = grad_ext[HALO : HALO + T].astype(bf16)
    values = tokens[...].astype(f32)
    upstream = mm_nt(low_own, w_in[:, :E]) + mm_nt(grad_gate[...], w_in[:, E:])
    back, gain_own = norm_back(values, inverse_rms(values), gain[...], upstream)
    grad_tokens[...] = grad_mid[...] + back
    before = halo[...].astype(f32)
    back, gain_edge = norm_back(before, inverse_rms(before), gain[...], mm_nt(low_edge, w_in[:, :E]))
    tail[...] = back[HALO - 8 : HALO]
    vec[KERNEL + 3 : KERNEL + 4, 0:D] = gain_own + gain_edge
    vec[KERNEL + 3 : KERNEL + 4, D:E] = g_gain_two[...]
    wide[R + N : R + 2 * N] = vec[...]
    for core in range(2):

        @pl.when(meta[2 + DOCS] == core)
        def _():
            for j in range(D // 128):
                cols = slice(core * D + j * 128, core * D + (j + 1) * 128)
                keep[0:HALO, j * 128 : (j + 1) * 128] = low_edge[:, cols]
                keep[HALO : HALO + T, j * 128 : (j + 1) * 128] = low_own[:, cols]
                cols = slice((1 - core) * D + j * 128, (1 - core) * D + (j + 1) * 128)
                base = j * (HALO + T)
                give[base : base + HALO] = low_edge[:, cols]
                give[base + HALO : base + HALO + T] = low_own[:, cols]
            base = D // 128 * (HALO + T)
            for j in range(E // 128):
                cols = slice(j * 128, (j + 1) * 128)
                mine, other = (gw_x, wide) if core == 0 else (wide, gw_x)
                part_keep[j * 64 : (j + 1) * 64] = mine[:, cols]
                give[base + j * 64 : base + (j + 1) * 64] = other[:, cols].astype(bf16)


def early_weights(meta, keep, got, out, both):
    both[0:T] = keep[...]
    both[T : 2 * T] = got[...]
    left_right = (((0, 1), (2, 3), (2, 4), (2, 5)), ((0, 2), (1, 2), (3, 4), (3, 5)))
    for core in range(2):

        @pl.when(meta[2 + DOCS] == core)
        def _():
            for j, (a, b) in enumerate(left_right[core]):
                left, right = both[:, a * D : (a + 1) * D], both[:, b * D : (b + 1) * D]
                result = mm_tn(left, right).astype(bf16)
                for q in range(D // LANES):
                    out[(4 * j + q) * D : (4 * j + q + 1) * D] = result[:, q * LANES : (q + 1) * LANES]


def late_weights(keep, part_keep, low_own, low_other, got, out, whole):
    left = jnp.concatenate([low_own[...], low_other[...]], axis=0)
    rows = HALO + T
    for j in range(D // LANES):
        right = jnp.concatenate([keep[:, j * LANES : (j + 1) * LANES], got[j * rows : (j + 1) * rows]], axis=0)
        whole[j * D : (j + 1) * D] = mm_tn(left, right)
    base = D // LANES * rows
    whole[4 * D : 5 * D] = part_keep[...] + got[base : base + D].astype(f32)
    for d in range(SHARES):
        main = whole[d * MAIN : (d + 1) * MAIN]
        small = whole[4 * D + d * SMALL : 4 * D + (d + 1) * SMALL]
        out[d] = jnp.concatenate([main, small], axis=0).astype(bf16)


def add_up(early, late, out):
    first = early[0].astype(f32)
    second = late[0].astype(f32)
    for j in range(1, SHARES):
        first = first + early[j].astype(f32)
        second = second + late[j].astype(f32)
    low = jnp.concatenate([first, second], axis=0).astype(bf16)
    for j in range(SHARES):
        out[j] = low


def finish(meta, mine, other, gw_o, gw_q, gw_k, gw_v, gw_out, gw_in, gw_x, gw_dt, g_a_log, vec):
    is_zero = meta[2 + DOCS] == 0
    for d in range(SHARES):
        a, b = mine[d].astype(f32), other[d].astype(f32)
        zero = jnp.where(is_zero, a, b)
        one = jnp.where(is_zero, b, a)
        j, q, r = d // 16, d // 4 % 4, d % 4 * T
        tile = TILES[q]
        (gw_o, gw_q, gw_k, gw_v)[j][r : r + T, tile] = zero[0:T]
        if j < 2:
            gw_out[j * D + r : j * D + r + T, tile] = one[0:T]
        else:
            low = E + (j - 2) * D + q * LANES
            gw_in[r : r + T, low : low + LANES] = one[0:T]
        r = d % 16 * MAIN
        gw_in[r : r + MAIN, j * LANES : (j + 1) * LANES] = zero[T : T + MAIN]
        gw_in[r : r + MAIN, D + j * LANES : D + (j + 1) * LANES] = one[T : T + MAIN]
        tile, r = TILES[d // 8], d % 8 * SMALL
        gw_x[r : r + SMALL, tile] = zero[T + MAIN :]
        for out, low, high in ((gw_dt, 0, R), (g_a_log, R, R + N), (vec, R + N, R + 2 * N)):
            if low <= r < high:
                out[r - low : r - low + SMALL, tile] = one[T + MAIN :]


def call(body, name, outs, scratch, *args, smem=True):
    specs = [pl.BlockSpec(memory_space=pltpu.VMEM)] * len(args)
    if smem:
        specs[0] = pl.BlockSpec(memory_space=pltpu.SMEM)
    return pl.pallas_call(
        body,
        name=name,
        out_shape=[jax.ShapeDtypeStruct(s, t) for s, t in outs],
        in_specs=specs,
        out_specs=[pl.BlockSpec(memory_space=pltpu.VMEM)] * len(outs),
        scratch_shapes=[pltpu.VMEM(s, t) for s, t in scratch],
        compiler_params=pltpu.CompilerParams(vmem_limit_bytes=56 * 1024 * 1024),
    )(*args)


def shift(x, by):
    pairs = [(i, i + by) for i in range(BLOCKS) if 0 <= i + by < BLOCKS]
    return lax.ppermute(x, PLACE, pairs)


def swap(x):
    return lax.all_to_all(x, PLACE, 0, 0, tiled=True)


def partner(x):
    return lax.ppermute(x, "core", [(0, 1), (1, 0)])


def trade(x):
    return lax.all_to_all(x, SAME, 0, 0, tiled=True)


def layer(
    tokens, starts, gain_one, w_in, conv_w, conv_b, w_x, w_dt, dt_bias, a_log, d_skip, w_out,
    gain_two, w_q, w_k, w_v, w_o, cotangent,
):
    tokens, cot = tokens[0], cotangent[0]
    place = lax.axis_index(PLACE)
    core = lax.axis_index("core").astype(i32)
    meta = jnp.concatenate([jnp.stack([place * T, place]).astype(i32), starts[0], core[None]])
    row = lambda v: v.reshape(1, -1)
    halo = shift(tokens[T - HALO :], 1)
    tn = ((N, E), f32)
    te, tel, td, tdl = ((T, E), f32), ((T, E), bf16), ((T, D), f32), ((T, D), bf16)
    w_x = w_x.T
    send, grad_att, low_ext, ext, gate, conv, act, step, pre, bc, dt_low = call(
        mamba_in, "mamba_in",
        [((BLOCKS, N + 8, E), bf16), tdl, ((HALO + T, D), bf16), ((HALO + T, E), bf16), tel, te, tel, te, te,
         ((T // STEPS, 2 * N, 128), f32), ((T, R), bf16)],
        [((HALO + T, E), f32), te, te, ((T, 128), f32), ((N + 8, E), f32), tn, tn],
        meta, tokens, halo, row(gain_one), w_in, conv_w, row(conv_b), w_x, w_dt, row(dt_bias), a_log, cot, w_o,
    )
    low_other = partner(low_ext)
    forward = swap(send)
    packed, start, ssm, gated, middle, normed = call(
        mamba_out, "mamba_out",
        [((BLOCKS, ROWS, 128), bf16), ((N, E), f32), te, tel, td, tdl],
        [te, te, te, tn],
        meta, forward, tokens, step, act, bc, gate, a_log, row(d_skip), w_out, row(gain_two),
        w_q, w_k, w_v, grad_att,
    )
    (back,) = call(
        attention, "attention",
        [((BLOCKS, ROWS, 128), bf16)],
        [((128, BLOCKS * T), bf16), ((BLOCKS, T, QCHUNK), f32), ((BLOCKS, T, QCHUNK), f32),
         ((BLOCKS, T, 128), f32)],
        meta, swap(packed),
    )
    wide = ((T, 6 * D), bf16)
    send, mixed, grad_mid, g, grad_gate, keep, give, g_gain_two, g_skip = call(
        middle_back, "middle_back",
        [((BLOCKS, N, E), bf16), tdl, td, te, tel, wide, wide, ((1, D), f32), ((1, E), f32)],
        [tdl] * 4 + [te, tn, tn],
        meta, swap(back), cot, middle, normed, low_ext, gated, gate, ssm, act, step, bc, a_log,
        row(d_skip), w_o, w_q, w_k, w_v, w_out, row(gain_two),
    )
    (early,) = call(
        early_weights, "early_weights", [((16 * D, LANES), bf16)], [((2 * T, 6 * D), bf16)],
        meta, keep, partner(give),
    )
    early, behind = lax.optimization_barrier((early, swap(send)))
    early = trade(early.reshape(SHARES, T, LANES))
    grad_tokens, tail, keep, give, part_keep = call(
        mamba_back, "mamba_back",
        [td, ((8, D), f32), ((HALO + T, D), bf16), ((4 * (HALO + T) + D, 128), bf16), ((D, 128), f32)],
        [te, te, ((T, N, E), f32), ((T, N, E), f32), te, te, ((HALO + T, E), f32),
         ((T + 8, E), f32), ((HALO + T, E), f32), ((N, E), f32), ((64, E), f32), tn, tn,
         ((T, N, LANES), f32), ((T, N, LANES), f32)],
        meta, behind, forward, start, g, act, step, pre, bc, dt_low, conv, ext, a_log,
        row(d_skip), conv_w, w_x, w_dt, tokens, halo, row(gain_one), w_in, grad_gate, grad_mid,
        g_gain_two, g_skip,
    )
    (late,) = call(
        late_weights, "late_weights", [((SHARES, MAIN + SMALL, LANES), bf16)], [((5 * D, LANES), f32)],
        keep, part_keep, low_ext, low_other, partner(give), smem=False,
    )
    early, late = lax.optimization_barrier((early, late))
    late = trade(late)
    (total,) = call(
        add_up, "add_up", [((SHARES, T + MAIN + SMALL, LANES), bf16)], [], early, late, smem=False
    )
    total = trade(total)
    gw_o, gw_q, gw_k, gw_v, gw_out, gw_in, gw_x, gw_dt, g_a_log, vec = call(
        finish, "finish",
        [((D, D), f32)] * 4 + [((E, D), f32), ((D, 2 * E), f32), ((64, E), f32), ((R, E), f32), tn, tn],
        [],
        meta, total, partner(total),
    )
    grad_tokens = grad_tokens.at[T - 8 :].add(shift(tail, -1))
    return (
        mixed[None], grad_tokens[None], vec[KERNEL + 3, 0:D], gw_in, vec[0:KERNEL], vec[KERNEL], gw_x.T,
        gw_dt, vec[KERNEL + 1], g_a_log, vec[KERNEL + 2], gw_out, vec[KERNEL + 3, D:E], gw_q, gw_k,
        gw_v, gw_o,
    )


def solution(mesh):
    rows, seq, head = mesh.devices.shape
    fine = Mesh(mesh.devices.reshape(rows // 2, 2, seq, head), ALL)
    split = P(("y", "core"), PLACE, None)
    return jax.shard_map(
        layer,
        mesh=fine,
        in_specs=(split, P(("y", "core"), None)) + (P(),) * 15 + (split,),
        out_specs=(split, split) + (P(),) * 15,
        check_vma=False,
    )
```

```python
import functools

import jax
import jax.numpy as jnp
from jax import lax
from jax.experimental import pallas as pl
from jax.experimental.pallas import tpu as pltpu
from jax.sharding import Mesh, PartitionSpec as P

T, D, E, N, R, HD = 128, 512, 1024, 16, 32, 64
HEADS, BLOCKS, HALF, DOCS, KERNEL, HALO = 8, 16, 64, 6, 4, 16
LANES, STEPS = 128, 8
TILES = [slice(q * LANES, (q + 1) * LANES) for q in range(E // LANES)]
ROWS = T + HALF
RESET = 1e4
LOG2E = 1.4426950408889634
EPS = 1e-05
MASKED = -1e30
PLACE = ("seq", "head")
ALL = ("y", "core", "seq", "head")
SAME, SHARES, MAIN, SMALL = ("y", "seq", "head"), 64, 32, 8
bf16, f32, i32 = jnp.bfloat16, jnp.float32, jnp.int32


def mm(a, b):
    return jnp.dot(a, b, preferred_element_type=f32)


def mm_nt(a, b):
    return lax.dot_general(a, b, (((1,), (1,)), ((), ())), preferred_element_type=f32)


def mm_tn(a, b):
    return lax.dot_general(a, b, (((0,), (0,)), ((), ())), preferred_element_type=f32)


def doc_of(meta, pos):
    count = jnp.zeros(pos.shape, i32)
    for k in range(DOCS):
        count = count + (meta[2 + k] <= pos).astype(i32)
    return count


def reset_of(meta, pos):
    hit = meta[2] == pos
    for k in range(1, DOCS):
        hit = hit | (meta[2 + k] == pos)
    return jnp.where(hit, RESET, 0.0)


def inverse_rms(x):
    return lax.rsqrt(jnp.mean(x * x, axis=-1, keepdims=True) + EPS)


def sigmoid(x):
    return 1.0 / (1.0 + jnp.exp(-x))


def silu_slope(x):
    s = sigmoid(x)
    return s * (1.0 + x * (1.0 - s))


def norm_back(values, inverse, gain, upstream):
    scaled = upstream * gain
    inner = jnp.mean(values * scaled, axis=-1, keepdims=True)
    back = inverse * scaled - values * (inverse * inverse * inverse) * inner
    return back, jnp.sum(upstream * values * inverse, axis=0, keepdims=True)


def columns(offset, meta):
    first = meta[0]
    return first + offset + lax.broadcasted_iota(i32, (T, 1), 0)


def stack_sums(parts):
    row = lax.broadcasted_iota(i32, parts[0].shape, 0)
    for by in (1, 2, 4):
        first = (row & by) == 0
        parts = [
            jnp.where(first, a, b) + pltpu.roll(jnp.where(first, b, a), by, axis=0)
            for a, b in zip(parts[0::2], parts[1::2])
        ]
    return parts[0]


def column(block, low, k):
    return jnp.broadcast_to(block[low : low + N, k : k + 1], (N, LANES))


def halves(x):
    return x[0:8] + x[8:16]


def scan_forward(dec, sa, bc, rates2, start, result=None):
    def block(i, states):
        states = list(states)
        base = pl.multiple_of(i * STEPS, STEPS)
        cols = bc[i]
        sums = [[None] * STEPS for _ in TILES]
        for k in range(STEPS):
            b_col = column(cols, 0, k)
            c_col = column(cols, N, k)
            for q, tile in enumerate(TILES):
                factor = jnp.exp2(dec[pl.ds(base, STEPS), tile][k : k + 1] * rates2[:, tile])
                states[q] = factor * states[q] + b_col * sa[pl.ds(base, STEPS), tile][k : k + 1]
                if result is not None:
                    sums[q][k] = halves(states[q] * c_col)
        if result is not None:
            for q, tile in enumerate(TILES):
                result[pl.ds(base, STEPS), tile] = stack_sums(sums[q])
        return tuple(states)

    return lax.fori_loop(0, T // STEPS, block, tuple(start[:, tile] for tile in TILES))


def mamba_in(
    meta, tokens, halo, gain, w_in, conv_w, conv_b, w_x, w_dt, dt_b, a_log, cot, w_o,
    send, grad_att, low_out, ext_out, gate_out, conv_out, act_out, step_out, pre_out, bc_out, dt_out,
    ext, dec, sa, xp, end, rates2, zero,
):
    grad_att[...] = mm_nt(cot[...], w_o[...]).astype(bf16)
    own = tokens[...].astype(f32)
    before = halo[...].astype(f32)
    low_own = (own * inverse_rms(own) * gain[...]).astype(bf16)
    low_before = (before * inverse_rms(before) * gain[...]).astype(bf16)
    conv_own = mm(low_own, w_in[:, :E]).astype(bf16)
    conv_before = mm(low_before, w_in[:, :E]).astype(bf16)
    low_out[0:HALO] = low_before
    low_out[HALO : HALO + T] = low_own
    ext_out[0:HALO] = conv_before
    ext_out[HALO : HALO + T] = conv_own
    ext[0:HALO] = conv_before.astype(f32)
    ext[HALO : HALO + T] = conv_own.astype(f32)
    gate_out[...] = mm(low_own, w_in[:, E:]).astype(bf16)
    own_doc = doc_of(meta, columns(0, meta))
    conv = jnp.broadcast_to(conv_b[...], (T, E))
    for offset in range(KERNEL):
        same = (doc_of(meta, columns(offset - KERNEL + 1, meta)) == own_doc).astype(f32)
        low = HALO - KERNEL + 1 + offset
        conv = conv + conv_w[offset : offset + 1] * ext[low : low + T] * same
    conv_out[...] = conv
    act = (conv * sigmoid(conv)).astype(bf16)
    act_out[...] = act
    proj = mm_nt(act, w_x[...])
    dt_low = proj[:, :R].astype(bf16)
    dt_out[...] = dt_low
    pre = mm(dt_low, w_dt[...]) + dt_b[...]
    pre_out[...] = pre
    step = jnp.maximum(pre, 0.0) + jnp.log1p(jnp.exp(-jnp.abs(pre)))
    step_out[...] = step
    held = step + reset_of(meta, columns(0, meta))
    dec[...] = held
    sa[...] = step * act.astype(f32)
    xp[...] = jnp.zeros((T, 128), f32)
    xp[:, 0 : R + 2 * N] = proj
    turned = xp[...].T
    for i in range(T // STEPS):
        bc_out[i, :, 0:STEPS] = turned[R : R + 2 * N, i * STEPS : (i + 1) * STEPS]
    total = jnp.sum(held, axis=0, keepdims=True)
    high = total.astype(bf16)
    rest = (total - high.astype(f32)).astype(bf16)
    end[N : N + 8] = jnp.concatenate([high.astype(f32), rest.astype(f32), jnp.zeros((6, E), f32)], axis=0)
    rates2[...] = -jnp.exp(a_log[...]) * LOG2E
    zero[...] = jnp.zeros((N, E), f32)
    states = scan_forward(dec, sa, bc_out, rates2, zero)
    for q, tile in enumerate(TILES):
        end[0:N, tile] = states[q]
    ended = end[...].astype(bf16)
    for j in range(BLOCKS):
        send[j] = ended


def roll_half(x):
    return pltpu.roll(x, HALF, axis=1)


def mamba_out(
    meta, got, tokens, step, act, bc, gate, a_log, d_skip, w_out, gain, w_q, w_k, w_v, grad_att,
    send, start_out, ssm_out, gated_out, middle_out, normed_out,
    dec, sa, ssm, rates2,
):
    place = meta[1]
    rates2[...] = -jnp.exp(a_log[...]) * LOG2E
    dec[...] = step[...] + reset_of(meta, columns(0, meta))
    act_f = act[...].astype(f32)
    sa[...] = step[...] * act_f

    def join(j, state):
        tail = got[j, N : N + 8].astype(f32)
        total = tail[0:1] + tail[1:2]
        return jnp.exp2(rates2[...] * total) * state + got[j, 0:N].astype(f32)

    start_out[...] = lax.fori_loop(0, place, join, jnp.zeros((N, E), f32))
    scan_forward(dec, sa, bc, rates2, start_out, ssm)
    result = ssm[...] + d_skip[...] * act_f
    ssm_out[...] = result
    gates = gate[...].astype(f32)
    gated = (result * (gates * sigmoid(gates))).astype(bf16)
    gated_out[...] = gated
    middle = tokens[...].astype(f32) + mm(gated, w_out[...])
    middle_out[...] = middle
    normed = (middle * inverse_rms(middle) * gain[...]).astype(bf16)
    normed_out[...] = normed
    queries = mm(normed, w_q[...]).astype(bf16).astype(f32) * (HD ** -0.5)
    keys = mm(normed, w_k[...])
    vals = mm(normed, w_v[...])
    grads = grad_att[...].astype(f32)
    low = lax.broadcasted_iota(i32, (T, 128), 1) < HALF
    for m in range(HEADS // 2):
        tile = slice(m * 128, (m + 1) * 128)
        for odd in range(2):
            for first, second, at, rows in ((keys, vals, 0, T), (queries, grads, T, HALF)):
                a, b = first[:, tile], second[:, tile]
                pair = jnp.where(low, a, roll_half(b)) if odd == 0 else jnp.where(low, roll_half(a), b)
                pair = pair.astype(bf16)
                dest = 2 * (2 * m + odd)
                if rows == T:
                    send[dest, 0:T] = pair
                    send[dest + 1, 0:T] = pair
                else:
                    send[dest, T:ROWS] = pair[0:HALF]
                    send[dest + 1, T:ROWS] = pair[HALF:T]


QCHUNK, QBLOCKS = 256, 4


def attention(meta, got, send, kv_t, scores, grads, kv_grad):
    parity = lax.rem(meta[1], 2)
    for i in range(BLOCKS):
        kv_t[:, i * T : (i + 1) * T] = got[i, 0:T].astype(f32).T.astype(bf16)
    lane = lax.broadcasted_iota(i32, (1, QCHUNK), 1)
    low_q = lax.broadcasted_iota(i32, (QCHUNK, 128), 1) < HD
    low_k = lax.broadcasted_iota(i32, (T, 128), 1) < HD
    key_row = lax.broadcasted_iota(i32, (T, QCHUNK), 0)
    for c in range(BLOCKS // QBLOCKS):
        qg = jnp.concatenate([got[c * QBLOCKS + b, T:ROWS] for b in range(QBLOCKS)], axis=0)
        q_only = jnp.where(low_q, qg.astype(f32), 0.0).astype(bf16)
        g_only = jnp.where(low_q, 0.0, qg.astype(f32)).astype(bf16)
        pos = (c * QBLOCKS + lane // HALF) * T + parity * HALF + lane % HALF
        begin = jnp.zeros((1, QCHUNK), i32)
        for k in range(DOCS):
            begin = jnp.maximum(begin, jnp.where(meta[2 + k] <= pos, meta[2 + k], 0))
        tiles = (c + 1) * QBLOCKS
        top = jnp.full((8, QCHUNK), MASKED, f32)
        for i in range(tiles):
            s = mm_nt(got[i, 0:T], q_only)
            allowed = key_row >= begin - i * T
            if i >= c * QBLOCKS:
                allowed = allowed & (key_row <= pos - i * T)
            s = jnp.where(allowed, s, MASKED)
            scores[i] = s
            top = jnp.maximum(top, jnp.max(s.reshape(T // 8, 8, QCHUNK), axis=0))
        top = jnp.max(top, axis=0, keepdims=True)
        total = jnp.zeros((8, QCHUNK), f32)
        cross = jnp.zeros((8, QCHUNK), f32)
        for i in range(tiles):
            p = jnp.exp2((scores[i] - top) * LOG2E)
            scores[i] = p
            g = mm_nt(got[i, 0:T], g_only)
            grads[i] = g
            total = total + jnp.sum(p.reshape(T // 8, 8, QCHUNK), axis=0)
            cross = cross + jnp.sum((p * g).reshape(T // 8, 8, QCHUNK), axis=0)
        inverse = 1.0 / jnp.sum(total, axis=0, keepdims=True)
        cross = jnp.sum(cross, axis=0, keepdims=True) * inverse
        out_t = jnp.zeros((128, QCHUNK), f32)
        dq_t = jnp.zeros((128, QCHUNK), f32)
        for i in range(tiles):
            prob = scores[i] * inverse
            low_p = prob.astype(bf16)
            low_s = (prob * (grads[i] - cross)).astype(bf16)
            turned = kv_t[:, i * T : (i + 1) * T]
            out_t = out_t + mm(turned, low_p)
            dq_t = dq_t + mm(turned, low_s)
            both = jnp.where(low_k, mm(low_s, qg), mm(low_p, qg))
            if i >= c * QBLOCKS:
                kv_grad[i] = both
            else:
                kv_grad[i] = kv_grad[i] + both
        pair = jnp.where(low_q, dq_t.T * (HD ** -0.5), out_t.T).astype(bf16)
        for b in range(QBLOCKS):
            send[c * QBLOCKS + b, T:ROWS] = pair[b * HALF : (b + 1) * HALF]
    for i in range(BLOCKS):
        send[i, 0:T] = kv_grad[i].astype(bf16)


def middle_back(
    meta, got, cot, middle, normed, low_ext, gated, gate, ssm, act, step, bc, a_log, d_skip,
    w_o, w_q, w_k, w_v, w_out, gain,
    send, mixed, grad_mid_out, g_out, grad_gate_out, keep, give, g_gain, g_skip,
    att, dq, dk, dv, dec, end, rates2,
):
    low = lax.broadcasted_iota(i32, (HALF, 128), 1) < HALF
    low_t = lax.broadcasted_iota(i32, (T, 128), 1) < HALF
    for m in range(HEADS // 2):
        tile = slice(m * 128, (m + 1) * 128)
        for p in range(2):
            a = got[4 * m + p, T:ROWS].astype(f32)
            b = got[4 * m + 2 + p, T:ROWS].astype(f32)
            rows = slice(p * HALF, (p + 1) * HALF)
            dq[rows, tile] = jnp.where(low, a, roll_half(b)).astype(bf16)
            att[rows, tile] = jnp.where(low, roll_half(a), b).astype(bf16)
        a = got[4 * m, 0:T].astype(f32) + got[4 * m + 1, 0:T].astype(f32)
        b = got[4 * m + 2, 0:T].astype(f32) + got[4 * m + 3, 0:T].astype(f32)
        dk[:, tile] = jnp.where(low_t, a, roll_half(b)).astype(bf16)
        dv[:, tile] = jnp.where(low_t, roll_half(a), b).astype(bf16)
    cot_low = cot[...]
    values = middle[...]
    mixed[...] = (values + mm(att[...], w_o[...])).astype(bf16)
    upstream = mm_nt(dq[...], w_q[...]) + mm_nt(dk[...], w_k[...]) + mm_nt(dv[...], w_v[...])
    back, gain_grad = norm_back(values, inverse_rms(values), gain[...], upstream)
    g_gain[...] = gain_grad
    grad_mid = cot_low.astype(f32) + back
    grad_mid_out[...] = grad_mid
    mid_low = grad_mid.astype(bf16)
    grad_gated = mm_nt(mid_low, w_out[...]).astype(bf16).astype(f32)
    gates = gate[...].astype(f32)
    sig = sigmoid(gates)
    g = grad_gated * (gates * sig)
    g_out[...] = g
    grad_gate = (grad_gated * ssm[...] * (sig * (1.0 + gates * (1.0 - sig)))).astype(bf16)
    grad_gate_out[...] = grad_gate
    for first, second, core in ((keep, give, 0), (give, keep, 1)):

        @pl.when(meta[2 + DOCS] == core)
        def _():
            first[:, 0:D] = att[...]
            first[:, D : 2 * D] = cot_low
            first[:, 2 * D : 3 * D] = normed[...]
            first[:, 3 * D : 4 * D] = dq[...]
            first[:, 4 * D : 5 * D] = dk[...]
            first[:, 5 * D : 6 * D] = dv[...]
            second[:, 0:E] = gated[...]
            second[:, E : E + D] = mid_low
            second[:, E + D : 2 * E] = low_ext[HALO : HALO + T]
            second[:, 2 * E : 3 * E] = grad_gate

    g_skip[...] = jnp.sum(g * act[...].astype(f32), axis=0, keepdims=True)
    dec[...] = step[...] + reset_of(meta, columns(0, meta))
    rates2[...] = -jnp.exp(a_log[...]) * LOG2E

    def block(turn, carry):
        carry = list(carry)
        i = T // STEPS - 1 - turn
        base = pl.multiple_of(i * STEPS, STEPS)
        cols = bc[i]
        for k in reversed(range(STEPS)):
            c_col = column(cols, N, k)
            for q, tile in enumerate(TILES):
                factor = jnp.exp2(dec[pl.ds(base, STEPS), tile][k : k + 1] * rates2[:, tile])
                carry[q] = factor * (carry[q] + c_col * g_out[pl.ds(base, STEPS), tile][k : k + 1])
        return tuple(carry)

    carry = lax.fori_loop(0, T // STEPS, block, tuple(jnp.zeros((N, LANES), f32) for _ in TILES))
    for q, tile in enumerate(TILES):
        end[:, tile] = carry[q]
    ended = end[...].astype(bf16)
    for j in range(BLOCKS):
        send[j] = ended


def mamba_back(
    meta, got, forward, start, g, act, step, pre, bc, dt_low, conv, ext_low, a_log, d_skip,
    conv_w, w_x, w_dt, tokens, halo, gain, w_in, grad_gate, grad_mid, g_gain_two, g_skip,
    grad_tokens, tail, keep, give, part_keep,
    dec, sa, decay, kept, gs, ab, ext, padded, grad_ext, vec, wide, rates, rates2, sum_b, sum_c,
):
    place = meta[1]
    dec[...] = step[...] + reset_of(meta, columns(0, meta))
    act_f = act[...].astype(f32)
    sa[...] = step[...] * act_f
    rates[...] = -jnp.exp(a_log[...])
    rates2[...] = rates[...] * LOG2E

    def join(turn, state):
        j = BLOCKS - 1 - turn
        tail = forward[j, N : N + 8].astype(f32)
        total = tail[0:1] + tail[1:2]
        return jnp.exp2(rates2[...] * total) * state + got[j].astype(f32)

    wide[R : R + N] = lax.fori_loop(0, BLOCKS - 1 - place, join, jnp.zeros((N, E), f32))

    def ahead(i, states):
        states = list(states)
        base = pl.multiple_of(i * STEPS, STEPS)
        cols = bc[i]
        for k in range(STEPS):
            b_col = column(cols, 0, k)
            total = jnp.zeros((N, LANES), f32)
            for q, tile in enumerate(TILES):
                rows = pl.ds(base, STEPS), tile
                factor = jnp.exp2(dec[rows][k : k + 1] * rates2[:, tile])
                moved = factor * states[q]
                decay[base + k, :, tile] = factor
                kept[base + k, :, tile] = moved
                states[q] = moved + b_col * sa[rows][k : k + 1]
                total = total + states[q] * g[rows][k : k + 1]
            sum_c[base + k] = total
        return tuple(states)

    lax.fori_loop(0, T // STEPS, ahead, tuple(start[:, tile] for tile in TILES))
    first_carry = tuple(wide[R : R + N, tile] for tile in TILES)
    wide[R + N : R + 2 * N] = jnp.zeros((N, E), f32)

    def behind(turn, carry):
        carry = list(carry)
        i = T // STEPS - 1 - turn
        base = pl.multiple_of(i * STEPS, STEPS)
        cols = bc[i]
        by_rate = [[None] * STEPS for _ in TILES]
        by_b = [[None] * STEPS for _ in TILES]
        along = [wide[R + N : R + 2 * N, tile] for tile in TILES]
        for k in reversed(range(STEPS)):
            b_col = column(cols, 0, k)
            c_col = column(cols, N, k)
            total = jnp.zeros((N, LANES), f32)
            for q, tile in enumerate(TILES):
                rows = pl.ds(base, STEPS), tile
                adjoint = g[rows][k : k + 1] * c_col + carry[q]
                carry[q] = decay[base + k, :, tile] * adjoint
                log_grad = adjoint * kept[base + k, :, tile]
                along[q] = along[q] + log_grad * step[rows][k : k + 1]
                by_rate[q][k] = halves(log_grad * rates[:, tile])
                by_b[q][k] = halves(adjoint * b_col)
                total = total + adjoint * sa[rows][k : k + 1]
            sum_b[base + k] = total
        for q, tile in enumerate(TILES):
            wide[R + N : R + 2 * N, tile] = along[q]
            gs[pl.ds(base, STEPS), tile] = stack_sums(by_rate[q])
            ab[pl.ds(base, STEPS), tile] = stack_sums(by_b[q])
        return tuple(carry)

    lax.fori_loop(0, T // STEPS, behind, first_carry)
    wide[R : R + N] = wide[R + N : R + 2 * N] * rates[...]
    lane = lax.broadcasted_iota(i32, (LANES, LANES), 1)
    turned = jnp.zeros((T, LANES), f32)
    for at, sums in ((0, sum_b), (N, sum_c)):
        for n in range(N):
            one = (lane == at + n).astype(f32).astype(bf16)
            values = sums[:, n, :]
            high = values.astype(bf16)
            turned = turned + mm(high, one) + mm((values - high.astype(f32)).astype(bf16), one)
    adjoint_b = ab[...]
    grad_step = gs[...] + adjoint_b * act_f
    grad_act = g[...] * d_skip[...] + adjoint_b * step[...]
    grad_pre = (grad_step * sigmoid(pre[...])).astype(bf16)
    vec[...] = jnp.zeros((N, E), f32)
    vec[KERNEL + 1 : KERNEL + 2] = jnp.sum(grad_pre.astype(f32), axis=0, keepdims=True)
    vec[KERNEL + 2 : KERNEL + 3] = g_skip[...]
    wide[0:R] = mm_tn(dt_low[...], grad_pre)
    grad_proj = jnp.concatenate([mm_nt(grad_pre, w_dt[...]), turned[:, 0 : 2 * N]], axis=1).astype(bf16)
    gw_x = mm_tn(grad_proj, act[...])
    grad_act = grad_act + mm(grad_proj, w_x[...])
    grad_conv = grad_act * silu_slope(conv[...])
    vec[KERNEL : KERNEL + 1] = jnp.sum(grad_conv, axis=0, keepdims=True)
    padded[0:T] = grad_conv
    padded[T : T + 8] = jnp.zeros((8, E), f32)
    ext[...] = ext_low[...].astype(f32)
    own_doc = doc_of(meta, columns(0, meta))
    own = jnp.zeros((T, E), f32)
    lift = KERNEL - 1
    rows = lax.broadcasted_iota(i32, (T, 1), 0)
    for offset in range(KERNEL):
        same = (doc_of(meta, columns(offset - lift, meta)) == own_doc).astype(f32)
        low = HALO - lift + offset
        vec[offset : offset + 1] = jnp.sum(grad_conv * ext[low : low + T] * same, axis=0, keepdims=True)
        up = lift - offset
        ahead_same = (doc_of(meta, columns(0, meta)) == doc_of(meta, columns(up, meta))) & (rows < T - up)
        own = own + conv_w[offset : offset + 1] * padded[up : up + T] * ahead_same.astype(f32)
    grad_ext[HALO : HALO + T] = own
    first = meta[0]
    edges = [jnp.zeros((HALO - lift, E), f32)]
    for row in range(lift):
        edge = jnp.zeros((1, E), f32)
        here = doc_of(meta, first - lift + row + jnp.zeros((1, 1), i32))
        for offset in range(row + 1):
            at = row - offset
            same = (doc_of(meta, first + at + jnp.zeros((1, 1), i32)) == here).astype(f32)
            edge = edge + conv_w[offset : offset + 1] * padded[at : at + 1] * same
        edges.append(edge)
    grad_ext[0:HALO] = jnp.concatenate(edges, axis=0)
    low_edge = grad_ext[0:HALO].astype(bf16)
    low_own = grad_ext[HALO : HALO + T].astype(bf16)
    values = tokens[...].astype(f32)
    upstream = mm_nt(low_own, w_in[:, :E]) + mm_nt(grad_gate[...], w_in[:, E:])
    back, gain_own = norm_back(values, inverse_rms(values), gain[...], upstream)
    grad_tokens[...] = grad_mid[...] + back
    before = halo[...].astype(f32)
    back, gain_edge = norm_back(before, inverse_rms(before), gain[...], mm_nt(low_edge, w_in[:, :E]))
    tail[...] = back[HALO - 8 : HALO]
    vec[KERNEL + 3 : KERNEL + 4, 0:D] = gain_own + gain_edge
    vec[KERNEL + 3 : KERNEL + 4, D:E] = g_gain_two[...]
    wide[R + N : R + 2 * N] = vec[...]
    for core in range(2):

        @pl.when(meta[2 + DOCS] == core)
        def _():
            for j in range(D // 128):
                cols = slice(core * D + j * 128, core * D + (j + 1) * 128)
                keep[0:HALO, j * 128 : (j + 1) * 128] = low_edge[:, cols]
                keep[HALO : HALO + T, j * 128 : (j + 1) * 128] = low_own[:, cols]
                cols = slice((1 - core) * D + j * 128, (1 - core) * D + (j + 1) * 128)
                base = j * (HALO + T)
                give[base : base + HALO] = low_edge[:, cols]
                give[base + HALO : base + HALO + T] = low_own[:, cols]
            base = D // 128 * (HALO + T)
            for j in range(E // 128):
                cols = slice(j * 128, (j + 1) * 128)
                mine, other = (gw_x, wide) if core == 0 else (wide, gw_x)
                part_keep[j * 64 : (j + 1) * 64] = mine[:, cols]
                give[base + j * 64 : base + (j + 1) * 64] = other[:, cols].astype(bf16)


def early_weights(meta, keep, got, out, both):
    both[0:T] = keep[...]
    both[T : 2 * T] = got[...]
    left_right = (((0, 1), (2, 3), (2, 4), (2, 5)), ((0, 2), (1, 2), (3, 4), (3, 5)))
    for core in range(2):

        @pl.when(meta[2 + DOCS] == core)
        def _():
            for j, (a, b) in enumerate(left_right[core]):
                left, right = both[:, a * D : (a + 1) * D], both[:, b * D : (b + 1) * D]
                result = mm_tn(left, right).astype(bf16)
                for q in range(D // LANES):
                    out[(4 * j + q) * D : (4 * j + q + 1) * D] = result[:, q * LANES : (q + 1) * LANES]


def late_weights(keep, part_keep, low_own, low_other, got, early, out, whole):
    total = early[0].astype(f32)
    for j in range(1, SHARES):
        total = total + early[j].astype(f32)
    left = jnp.concatenate([low_own[...], low_other[...]], axis=0)
    rows = HALO + T
    for j in range(D // LANES):
        right = jnp.concatenate([keep[:, j * LANES : (j + 1) * LANES], got[j * rows : (j + 1) * rows]], axis=0)
        whole[j * D : (j + 1) * D] = mm_tn(left, right)
    base = D // LANES * rows
    whole[4 * D : 5 * D] = part_keep[...] + got[base : base + D].astype(f32)
    for d in range(SHARES):
        main = whole[d * MAIN : (d + 1) * MAIN]
        small = whole[4 * D + d * SMALL : 4 * D + (d + 1) * SMALL]
        out[d] = jnp.concatenate([total, main, small], axis=0).astype(bf16)


def add_late(got, out):
    total = got[0].astype(f32)[T:]
    for j in range(1, SHARES):
        total = total + got[j].astype(f32)[T:]
    low = total.astype(bf16)
    for j in range(SHARES):
        out[j] = low


def finish_early(meta, mine, other, gw_o, gw_q, gw_k, gw_v, gw_out, gw_in, gate, sem):
    is_zero = meta[2 + DOCS] == 0
    for d in reversed(range(SHARES)):
        a, b = mine[d].astype(f32)[0:T], other[d].astype(f32)[0:T]
        j, q, r = d // 16, d // 4 % 4, d % 4 * T
        tile = TILES[q]
        (gw_o, gw_q, gw_k, gw_v)[j][r : r + T, tile] = jnp.where(is_zero, a, b)
        one = jnp.where(is_zero, b, a)
        if j < 2:
            gw_out[j * D + r : j * D + r + T, tile] = one
        else:
            low = (j - 2) * D + q * LANES
            gate[r : r + T, low : low + LANES] = one
        if d == SHARES // 2:
            copy = pltpu.make_async_copy(gate, gw_in.at[:, pl.ds(E, E)], sem)
            copy.start()
    copy.wait()


def finish_late(
    meta, mine, other, _, gw_in, gw_x, gw_dt, g_a_log, g_conv_w, g_conv_b, g_dt_b, g_skip, g_gain_one,
    g_gain_two, conv, sem,
):
    is_zero = meta[2 + DOCS] == 0
    for d in range(SHARES):
        a, b = mine[d].astype(f32), other[d].astype(f32)
        zero = jnp.where(is_zero, a, b)
        one = jnp.where(is_zero, b, a)
        j, r = d // 16, d % 16 * MAIN
        conv[r : r + MAIN, j * LANES : (j + 1) * LANES] = zero[0:MAIN]
        conv[r : r + MAIN, D + j * LANES : D + (j + 1) * LANES] = one[0:MAIN]
        q, r = d // 8, d % 8 * SMALL
        tile = TILES[q]
        gw_x[r : r + SMALL, tile] = zero[MAIN:]
        for out, low, high in ((gw_dt, 0, R), (g_a_log, R, R + N)):
            if low <= r < high:
                out[r - low : r - low + SMALL, tile] = one[MAIN:]
        if r == R + N:
            g_conv_w[:, tile] = one[MAIN : MAIN + KERNEL]
            at = MAIN + KERNEL
            for i, out in enumerate((g_conv_b, g_dt_b, g_skip)):
                out[:, tile] = one[at + i : at + i + 1]
            out = g_gain_one if q < 4 else g_gain_two
            out[:, TILES[q % 4]] = one[at + 3 : at + 4]
    copy = pltpu.make_async_copy(conv, gw_in.at[:, pl.ds(0, E)], sem)
    copy.start()
    copy.wait()


MEGABYTES = dict(
    mamba_in=16, mamba_out=16, attention=16, middle_back=20, early_weights=12, mamba_back=36, late_weights=12,
    add_late=10, finish_early=24, finish_late=12,
)


def call(body, name, outs, scratch, *args, smem=True, outside=(), aliases=None, far=(), far_out=()):
    aliases = aliases or {}
    args = [pltpu.with_memory_space_constraint(x, pltpu.HBM) if i in far else x for i, x in enumerate(args)]
    specs = [pl.BlockSpec(memory_space=pl.ANY if i in aliases else pltpu.VMEM) for i in range(len(args))]
    if smem:
        specs[0] = pl.BlockSpec(memory_space=pltpu.SMEM)
    return pl.pallas_call(
        body,
        name=name,
        out_shape=[pltpu.HBM(s, t) if i in far_out else jax.ShapeDtypeStruct(s, t) for i, (s, t) in enumerate(outs)],
        in_specs=specs,
        out_specs=[pl.BlockSpec(memory_space=pl.ANY if i in outside else pltpu.VMEM) for i in range(len(outs))],
        scratch_shapes=[pltpu.VMEM(s, t) for s, t in scratch]
        + ([pltpu.SemaphoreType.DMA] if outside else []),
        input_output_aliases=aliases,
        compiler_params=pltpu.CompilerParams(vmem_limit_bytes=MEGABYTES[name] << 20),
    )(*args)


def shift(x, by):
    pairs = [(i, i + by) for i in range(BLOCKS) if 0 <= i + by < BLOCKS]
    return lax.ppermute(x, PLACE, pairs)


def swap(x):
    return lax.all_to_all(x, PLACE, 0, 0, tiled=True)


def partner(x):
    return lax.ppermute(x, "core", [(0, 1), (1, 0)])


def trade(x):
    return lax.all_to_all(x, SAME, 0, 0, tiled=True)


def layer(
    tokens, starts, gain_one, w_in, conv_w, conv_b, w_x, w_dt, dt_bias, a_log, d_skip, w_out,
    gain_two, w_q, w_k, w_v, w_o, cotangent,
):
    tokens, cot = tokens[0], cotangent[0]
    place = lax.axis_index(PLACE)
    core = lax.axis_index("core").astype(i32)
    meta = jnp.concatenate([jnp.stack([place * T, place]).astype(i32), starts[0], core[None]])
    row = lambda v: v.reshape(1, -1)
    halo = shift(tokens[T - HALO :], 1)
    tn = ((N, E), f32)
    te, tel, td, tdl = ((T, E), f32), ((T, E), bf16), ((T, D), f32), ((T, D), bf16)
    w_x = w_x.T
    send, grad_att, low_ext, ext, gate, conv, act, step, pre, bc, dt_low = call(
        mamba_in, "mamba_in",
        [((BLOCKS, N + 8, E), bf16), tdl, ((HALO + T, D), bf16), ((HALO + T, E), bf16), tel, te, tel, te, te,
         ((T // STEPS, 2 * N, 128), f32), ((T, R), bf16)],
        [((HALO + T, E), f32), te, te, ((T, 128), f32), ((N + 8, E), f32), tn, tn],
        meta, tokens, halo, row(gain_one), w_in, conv_w, row(conv_b), w_x, w_dt, row(dt_bias), a_log, cot, w_o,
        far=(1, 3, 4, 5, 6, 7, 8, 9, 10, 11, 12), far_out=(2, 3, 5, 8, 10),
    )
    low_other = partner(low_ext)
    forward = swap(send)
    packed, start, ssm, gated, middle, normed = call(
        mamba_out, "mamba_out",
        [((BLOCKS, ROWS, 128), bf16), ((N, E), f32), te, tel, td, tdl],
        [te, te, te, tn],
        meta, forward, tokens, step, act, bc, gate, a_log, row(d_skip), w_out, row(gain_two),
        w_q, w_k, w_v, grad_att, far_out=(1,),
    )
    (back,) = call(
        attention, "attention",
        [((BLOCKS, ROWS, 128), bf16)],
        [((128, BLOCKS * T), bf16), ((BLOCKS, T, QCHUNK), f32), ((BLOCKS, T, QCHUNK), f32),
         ((BLOCKS, T, 128), f32)],
        meta, swap(packed),
    )
    wide = ((T, 6 * D), bf16)
    send, mixed, grad_mid, g, grad_gate, keep, give, g_gain_two, g_skip = call(
        middle_back, "middle_back",
        [((BLOCKS, N, E), bf16), tdl, td, te, tel, wide, wide, ((1, D), f32), ((1, E), f32)],
        [tdl] * 4 + [te, tn, tn],
        meta, swap(back), cot, middle, normed, low_ext, gated, gate, ssm, act, step, bc, a_log,
        row(d_skip), w_o, w_q, w_k, w_v, w_out, row(gain_two), far_out=(1, 2, 3, 4, 7, 8),
    )
    (early,) = call(
        early_weights, "early_weights", [((16 * D, LANES), bf16)], [((2 * T, 6 * D), bf16)],
        meta, keep, partner(give),
    )
    early, behind = lax.optimization_barrier((early, swap(send)))
    early = trade(early.reshape(SHARES, T, LANES))
    grad_tokens, tail, keep, give, part_keep = call(
        mamba_back, "mamba_back",
        [td, ((8, D), f32), ((HALO + T, D), bf16), ((4 * (HALO + T) + D, 128), bf16), ((D, 128), f32)],
        [te, te, ((T, N, E), f32), ((T, N, E), f32), te, te, ((HALO + T, E), f32),
         ((T + 8, E), f32), ((HALO + T, E), f32), ((N, E), f32), ((64, E), f32), tn, tn,
         ((T, N, LANES), f32), ((T, N, LANES), f32)],
        meta, behind, forward, start, g, act, step, pre, bc, dt_low, conv, ext, a_log,
        row(d_skip), conv_w, w_x, w_dt, tokens, halo, row(gain_one), w_in, grad_gate, grad_mid,
        g_gain_two, g_skip, far=tuple(range(1, 25)), far_out=(0, 1, 2, 4),
    )
    (late,) = call(
        late_weights, "late_weights", [((SHARES, T + MAIN + SMALL, LANES), bf16)], [((5 * D, LANES), f32)],
        keep, part_keep, low_ext, low_other, partner(give), early, smem=False,
        far=(0, 1, 2, 3, 4, 5), far_out=(0,),
    )
    shares = trade(late)
    (late,) = call(add_late, "add_late", [((SHARES, MAIN + SMALL, LANES), bf16)], [], shares, smem=False, far=(0,))
    late = trade(late)
    gw_o, gw_q, gw_k, gw_v, gw_out, gw_in = call(
        finish_early, "finish_early",
        [((D, D), f32)] * 4 + [((E, D), f32), ((D, 2 * E), f32)], [((D, E), f32)],
        meta, shares, partner(shares), outside=(5,), far=(1, 2),
    )
    grad_tokens = grad_tokens.at[T - 8 :].add(shift(tail, -1))
    late, gw_in, grad_tokens = lax.optimization_barrier((late, gw_in, grad_tokens))
    gw_in, gw_x, gw_dt, g_a_log, g_conv_w, g_conv_b, g_dt_b, g_skip, g_gain_one, g_gain_two = call(
        finish_late, "finish_late",
        [((D, 2 * E), f32), ((64, E), f32), ((R, E), f32), tn, ((KERNEL, E), f32), ((1, E), f32),
         ((1, E), f32), ((1, E), f32), ((1, D), f32), ((1, D), f32)],
        [((D, E), f32)],
        meta, late, partner(late), gw_in, outside=(0,), aliases={3: 0},
    )
    return (
        mixed[None], grad_tokens[None], g_gain_one[0], gw_in, g_conv_w, g_conv_b[0], gw_x.T, gw_dt,
        g_dt_b[0], g_a_log, g_skip[0], gw_out, g_gain_two[0], gw_q, gw_k, gw_v, gw_o,
    )


def solution(mesh):
    rows, seq, head = mesh.devices.shape
    fine = Mesh(mesh.devices.reshape(rows // 2, 2, seq, head), ALL)
    split = P(("y", "core"), PLACE, None)
    return jax.shard_map(
        layer,
        mesh=fine,
        in_specs=(split, P(("y", "core"), None)) + (P(),) * 15 + (split,),
        out_specs=(split, split) + (P(),) * 15,
        check_vma=False,
    )
```

```python
import functools

import jax
import jax.numpy as jnp
from jax import lax
from jax.experimental import pallas as pl
from jax.experimental.pallas import tpu as pltpu
from jax.sharding import Mesh, PartitionSpec as P

T, D, E, N, R, HD = 128, 512, 1024, 16, 32, 64
HEADS, BLOCKS, HALF, DOCS, KERNEL, HALO = 8, 16, 64, 6, 4, 16
LANES, STEPS = 128, 8
TILES = [slice(q * LANES, (q + 1) * LANES) for q in range(E // LANES)]
ROWS = T + HALF
SENT = N * 8 + 16
RESET = 1e4
LOG2E = 1.4426950408889634
EPS = 1e-05
MASKED = -1e30
PLACE = ("seq", "head")
ALL = ("y", "core", "seq", "head")
SAME, SHARES, MAIN, SMALL, LATE = ("y", "seq", "head"), 64, 32, 8, 40
bf16, f32, i32 = jnp.bfloat16, jnp.float32, jnp.int32


def mm(a, b):
    return jnp.dot(a, b, preferred_element_type=f32)


def mm_nt(a, b):
    return lax.dot_general(a, b, (((1,), (1,)), ((), ())), preferred_element_type=f32)


def mm_tn(a, b):
    return lax.dot_general(a, b, (((0,), (0,)), ((), ())), preferred_element_type=f32)


def doc_of(meta, pos):
    count = jnp.zeros(pos.shape, i32)
    for k in range(DOCS):
        count = count + (meta[2 + k] <= pos).astype(i32)
    return count


def reset_of(meta, pos):
    hit = meta[2] == pos
    for k in range(1, DOCS):
        hit = hit | (meta[2 + k] == pos)
    return jnp.where(hit, RESET, 0.0)


def inverse_rms(x):
    return lax.rsqrt(jnp.mean(x * x, axis=-1, keepdims=True) + EPS)


def sigmoid(x):
    return 1.0 / (1.0 + jnp.exp(-x))


def silu_slope(x):
    s = sigmoid(x)
    return s * (1.0 + x * (1.0 - s))


def norm_back(values, inverse, gain, upstream):
    scaled = upstream * gain
    inner = jnp.mean(values * scaled, axis=-1, keepdims=True)
    back = inverse * scaled - values * (inverse * inverse * inverse) * inner
    return back, jnp.sum(upstream * values * inverse, axis=0, keepdims=True)


def columns(offset, meta):
    first = meta[0]
    return first + offset + lax.broadcasted_iota(i32, (T, 1), 0)


def stack_sums(parts):
    row = lax.broadcasted_iota(i32, parts[0].shape, 0)
    for by in (1, 2, 4):
        first = (row & by) == 0
        parts = [
            jnp.where(first, a, b) + pltpu.roll(jnp.where(first, b, a), by, axis=0)
            for a, b in zip(parts[0::2], parts[1::2])
        ]
    return parts[0]


def column(block, low, k):
    return jnp.broadcast_to(block[low : low + N, k : k + 1], (N, LANES))


def halves(x):
    return x[0:8] + x[8:16]


def scan_forward(dec, sa, bc, rates2, start, result=None):
    def block(i, states):
        states = list(states)
        base = pl.multiple_of(i * STEPS, STEPS)
        cols = bc[i]
        sums = [[None] * STEPS for _ in TILES]
        for k in range(STEPS):
            b_col = column(cols, 0, k)
            c_col = column(cols, N, k)
            for q, tile in enumerate(TILES):
                factor = jnp.exp2(dec[pl.ds(base, STEPS), tile][k : k + 1] * rates2[:, tile])
                states[q] = factor * states[q] + b_col * sa[pl.ds(base, STEPS), tile][k : k + 1]
                if result is not None:
                    sums[q][k] = halves(states[q] * c_col)
        if result is not None:
            for q, tile in enumerate(TILES):
                result[pl.ds(base, STEPS), tile] = stack_sums(sums[q])
        return tuple(states)

    return lax.fori_loop(0, T // STEPS, block, tuple(start[:, tile] for tile in TILES))


def mamba_in(
    meta, tokens, halo, gain, w_in, conv_w, conv_b, w_x, w_dt, dt_b, a_log, cot, w_o,
    send, grad_att, low_out, ext_out, gate_out, conv_out, act_out, step_out, pre_out, bc_out, dt_out,
    ext, dec, sa, xp, rates2, zero,
):
    grad_att[...] = mm_nt(cot[...], w_o[...]).astype(bf16)
    own = tokens[...].astype(f32)
    before = halo[...].astype(f32)
    low_own = (own * inverse_rms(own) * gain[...]).astype(bf16)
    low_before = (before * inverse_rms(before) * gain[...]).astype(bf16)
    conv_own = mm(low_own, w_in[:, :E]).astype(bf16)
    conv_before = mm(low_before, w_in[:, :E]).astype(bf16)
    low_out[0:HALO] = low_before
    low_out[HALO : HALO + T] = low_own
    ext_out[0:HALO] = conv_before
    ext_out[HALO : HALO + T] = conv_own
    ext[0:HALO] = conv_before.astype(f32)
    ext[HALO : HALO + T] = conv_own.astype(f32)
    gate_out[...] = mm(low_own, w_in[:, E:]).astype(bf16)
    own_doc = doc_of(meta, columns(0, meta))
    conv = jnp.broadcast_to(conv_b[...], (T, E))
    for offset in range(KERNEL):
        same = (doc_of(meta, columns(offset - KERNEL + 1, meta)) == own_doc).astype(f32)
        low = HALO - KERNEL + 1 + offset
        conv = conv + conv_w[offset : offset + 1] * ext[low : low + T] * same
    conv_out[...] = conv
    act = (conv * sigmoid(conv)).astype(bf16)
    act_out[...] = act
    proj = mm_nt(act, w_x[...])
    dt_low = proj[:, :R].astype(bf16)
    dt_out[...] = dt_low
    pre = mm(dt_low, w_dt[...]) + dt_b[...]
    pre_out[...] = pre
    step = jnp.maximum(pre, 0.0) + jnp.log1p(jnp.exp(-jnp.abs(pre)))
    step_out[...] = step
    held = step + reset_of(meta, columns(0, meta))
    dec[...] = held
    sa[...] = step * act.astype(f32)
    xp[...] = jnp.zeros((T, 128), f32)
    xp[:, 0 : R + 2 * N] = proj
    turned = xp[...].T
    for i in range(T // STEPS):
        bc_out[i, :, 0:STEPS] = turned[R : R + 2 * N, i * STEPS : (i + 1) * STEPS]
    total = jnp.sum(held, axis=0, keepdims=True)
    high = total.astype(bf16)
    rest = (total - high.astype(f32)).astype(bf16)
    rates2[...] = -jnp.exp(a_log[...]) * LOG2E
    zero[...] = jnp.zeros((N, E), f32)
    states = scan_forward(dec, sa, bc_out, rates2, zero)
    sums = [high[:, tile].astype(f32) for tile in TILES] + [rest[:, tile].astype(f32) for tile in TILES]
    ended = jnp.concatenate(list(states) + sums, axis=0).astype(bf16)
    for j in range(BLOCKS):
        send[j] = ended


def joined(blocks, first, last, ends, rates2):
    def join(turn, states):
        sent = blocks[first(turn)].astype(f32)
        own = sent if ends is None else ends[first(turn)].astype(f32)
        total = sent[N * 8 : N * 8 + 8] + sent[N * 8 + 8 : N * 8 + 16]
        return tuple(
            jnp.exp2(rates2[:, tile] * total[q : q + 1]) * states[q] + own[q * N : (q + 1) * N]
            for q, tile in enumerate(TILES)
        )

    return lax.fori_loop(0, last, join, tuple(jnp.zeros((N, LANES), f32) for _ in TILES))


def roll_half(x):
    return pltpu.roll(x, HALF, axis=1)


def mamba_out(
    meta, got, tokens, step, act, bc, gate, a_log, d_skip, w_out, gain, w_q, w_k, w_v, grad_att,
    send, start_out, ssm_out, gated_out, middle_out, normed_out,
    dec, sa, ssm, rates2,
):
    place = meta[1]
    rates2[...] = -jnp.exp(a_log[...]) * LOG2E
    dec[...] = step[...] + reset_of(meta, columns(0, meta))
    act_f = act[...].astype(f32)
    sa[...] = step[...] * act_f
    for tile, state in zip(TILES, joined(got, lambda turn: turn, place, None, rates2)):
        start_out[:, tile] = state
    scan_forward(dec, sa, bc, rates2, start_out, ssm)
    result = ssm[...] + d_skip[...] * act_f
    ssm_out[...] = result
    gates = gate[...].astype(f32)
    gated = (result * (gates * sigmoid(gates))).astype(bf16)
    gated_out[...] = gated
    middle = tokens[...].astype(f32) + mm(gated, w_out[...])
    middle_out[...] = middle
    normed = (middle * inverse_rms(middle) * gain[...]).astype(bf16)
    normed_out[...] = normed
    queries = mm(normed, w_q[...]).astype(bf16).astype(f32) * (HD ** -0.5)
    keys = mm(normed, w_k[...])
    vals = mm(normed, w_v[...])
    grads = grad_att[...].astype(f32)
    low = lax.broadcasted_iota(i32, (T, 128), 1) < HALF
    for m in range(HEADS // 2):
        tile = slice(m * 128, (m + 1) * 128)
        for odd in range(2):
            for first, second, at, rows in ((keys, vals, 0, T), (queries, grads, T, HALF)):
                a, b = first[:, tile], second[:, tile]
                pair = jnp.where(low, a, roll_half(b)) if odd == 0 else jnp.where(low, roll_half(a), b)
                pair = pair.astype(bf16)
                dest = 2 * (2 * m + odd)
                if rows == T:
                    send[dest, 0:T] = pair
                    send[dest + 1, 0:T] = pair
                else:
                    send[dest, T:ROWS] = pair[0:HALF]
                    send[dest + 1, T:ROWS] = pair[HALF:T]


QCHUNK, QBLOCKS = 256, 4


def attention(meta, got, send, kv_t, scores, grads, kv_grad):
    parity = lax.rem(meta[1], 2)
    for i in range(BLOCKS):
        kv_t[:, i * T : (i + 1) * T] = got[i, 0:T].astype(f32).T.astype(bf16)
    lane = lax.broadcasted_iota(i32, (1, QCHUNK), 1)
    low_q = lax.broadcasted_iota(i32, (QCHUNK, 128), 1) < HD
    low_k = lax.broadcasted_iota(i32, (T, 128), 1) < HD
    key_row = lax.broadcasted_iota(i32, (T, QCHUNK), 0)
    for c in range(BLOCKS // QBLOCKS):
        qg = jnp.concatenate([got[c * QBLOCKS + b, T:ROWS] for b in range(QBLOCKS)], axis=0)
        q_only = jnp.where(low_q, qg.astype(f32), 0.0).astype(bf16)
        g_only = jnp.where(low_q, 0.0, qg.astype(f32)).astype(bf16)
        pos = (c * QBLOCKS + lane // HALF) * T + parity * HALF + lane % HALF
        begin = jnp.zeros((1, QCHUNK), i32)
        for k in range(DOCS):
            begin = jnp.maximum(begin, jnp.where(meta[2 + k] <= pos, meta[2 + k], 0))
        tiles = (c + 1) * QBLOCKS
        top = jnp.full((8, QCHUNK), MASKED, f32)
        for i in range(tiles):
            s = mm_nt(got[i, 0:T], q_only)
            allowed = key_row >= begin - i * T
            if i >= c * QBLOCKS:
                allowed = allowed & (key_row <= pos - i * T)
            s = jnp.where(allowed, s, MASKED)
            scores[i] = s
            top = jnp.maximum(top, jnp.max(s.reshape(T // 8, 8, QCHUNK), axis=0))
        top = jnp.max(top, axis=0, keepdims=True)
        total = jnp.zeros((8, QCHUNK), f32)
        cross = jnp.zeros((8, QCHUNK), f32)
        for i in range(tiles):
            p = jnp.exp2((scores[i] - top) * LOG2E)
            scores[i] = p
            g = mm_nt(got[i, 0:T], g_only)
            grads[i] = g
            total = total + jnp.sum(p.reshape(T // 8, 8, QCHUNK), axis=0)
            cross = cross + jnp.sum((p * g).reshape(T // 8, 8, QCHUNK), axis=0)
        inverse = 1.0 / jnp.sum(total, axis=0, keepdims=True)
        cross = jnp.sum(cross, axis=0, keepdims=True) * inverse
        out_t = jnp.zeros((128, QCHUNK), f32)
        dq_t = jnp.zeros((128, QCHUNK), f32)
        for i in range(tiles):
            prob = scores[i] * inverse
            low_p = prob.astype(bf16)
            low_s = (prob * (grads[i] - cross)).astype(bf16)
            turned = kv_t[:, i * T : (i + 1) * T]
            out_t = out_t + mm(turned, low_p)
            dq_t = dq_t + mm(turned, low_s)
            both = jnp.where(low_k, mm(low_s, qg), mm(low_p, qg))
            if i >= c * QBLOCKS:
                kv_grad[i] = both
            else:
                kv_grad[i] = kv_grad[i] + both
        pair = jnp.where(low_q, dq_t.T * (HD ** -0.5), out_t.T).astype(bf16)
        for b in range(QBLOCKS):
            send[c * QBLOCKS + b, T:ROWS] = pair[b * HALF : (b + 1) * HALF]
    for i in range(BLOCKS):
        send[i, 0:T] = kv_grad[i].astype(bf16)


def middle_back(
    meta, got, cot, middle, normed, low_ext, gated, gate, ssm, act, step, bc, a_log, d_skip,
    w_o, w_q, w_k, w_v, w_out, gain,
    send, mixed, grad_mid_out, g_out, grad_gate_out, keep, give, g_gain, g_skip,
    att, dq, dk, dv, dec, rates2,
):
    low = lax.broadcasted_iota(i32, (HALF, 128), 1) < HALF
    low_t = lax.broadcasted_iota(i32, (T, 128), 1) < HALF
    for m in range(HEADS // 2):
        tile = slice(m * 128, (m + 1) * 128)
        for p in range(2):
            a = got[4 * m + p, T:ROWS].astype(f32)
            b = got[4 * m + 2 + p, T:ROWS].astype(f32)
            rows = slice(p * HALF, (p + 1) * HALF)
            dq[rows, tile] = jnp.where(low, a, roll_half(b)).astype(bf16)
            att[rows, tile] = jnp.where(low, roll_half(a), b).astype(bf16)
        a = got[4 * m, 0:T].astype(f32) + got[4 * m + 1, 0:T].astype(f32)
        b = got[4 * m + 2, 0:T].astype(f32) + got[4 * m + 3, 0:T].astype(f32)
        dk[:, tile] = jnp.where(low_t, a, roll_half(b)).astype(bf16)
        dv[:, tile] = jnp.where(low_t, roll_half(a), b).astype(bf16)
    cot_low = cot[...]
    values = middle[...]
    mixed[...] = (values + mm(att[...], w_o[...])).astype(bf16)
    upstream = mm_nt(dq[...], w_q[...]) + mm_nt(dk[...], w_k[...]) + mm_nt(dv[...], w_v[...])
    back, gain_grad = norm_back(values, inverse_rms(values), gain[...], upstream)
    g_gain[...] = gain_grad
    grad_mid = cot_low.astype(f32) + back
    grad_mid_out[...] = grad_mid
    mid_low = grad_mid.astype(bf16)
    grad_gated = mm_nt(mid_low, w_out[...]).astype(bf16).astype(f32)
    gates = gate[...].astype(f32)
    sig = sigmoid(gates)
    g = grad_gated * (gates * sig)
    g_out[...] = g
    grad_gate = (grad_gated * ssm[...] * (sig * (1.0 + gates * (1.0 - sig)))).astype(bf16)
    grad_gate_out[...] = grad_gate
    for first, second, core in ((keep, give, 0), (give, keep, 1)):

        @pl.when(meta[2 + DOCS] == core)
        def _():
            first[:, 0:D] = att[...]
            first[:, D : 2 * D] = cot_low
            first[:, 2 * D : 3 * D] = normed[...]
            first[:, 3 * D : 4 * D] = dq[...]
            first[:, 4 * D : 5 * D] = dk[...]
            first[:, 5 * D : 6 * D] = dv[...]
            second[:, 0:E] = gated[...]
            second[:, E : E + D] = mid_low
            second[:, E + D : 2 * E] = low_ext[HALO : HALO + T]
            second[:, 2 * E : 3 * E] = grad_gate

    g_skip[...] = jnp.sum(g * act[...].astype(f32), axis=0, keepdims=True)
    dec[...] = step[...] + reset_of(meta, columns(0, meta))
    rates2[...] = -jnp.exp(a_log[...]) * LOG2E

    def block(turn, carry):
        carry = list(carry)
        i = T // STEPS - 1 - turn
        base = pl.multiple_of(i * STEPS, STEPS)
        cols = bc[i]
        for k in reversed(range(STEPS)):
            c_col = column(cols, N, k)
            for q, tile in enumerate(TILES):
                factor = jnp.exp2(dec[pl.ds(base, STEPS), tile][k : k + 1] * rates2[:, tile])
                carry[q] = factor * (carry[q] + c_col * g_out[pl.ds(base, STEPS), tile][k : k + 1])
        return tuple(carry)

    carry = lax.fori_loop(0, T // STEPS, block, tuple(jnp.zeros((N, LANES), f32) for _ in TILES))
    ended = jnp.concatenate(carry, axis=0).astype(bf16)
    for j in range(BLOCKS):
        send[j] = ended


def mamba_back(
    meta, got, forward, start, g, act, step, pre_far, bc, dt_low_far, conv_far, ext_low_far, a_log, d_skip,
    conv_w, w_x_far, w_dt_far, tokens_far, halo, gain, w_in_far, grad_gate_far, grad_mid_far, g_gain_two, g_skip,
    grad_tokens, tail, keep, give, part_keep,
    dec, sa, decay, kept, gs, ab, ext, padded, grad_ext, vec, wide, rates, rates2, sum_b, sum_c,
    pre, dt_low, conv, ext_low, w_x, w_dt, tokens, w_in, grad_gate, grad_mid, sems,
):
    place = meta[1]
    loads = [
        pltpu.make_async_copy(source, held, sems.at[i])
        for i, (source, held) in enumerate(
            ((pre_far, pre), (dt_low_far, dt_low), (conv_far, conv), (ext_low_far, ext_low), (w_x_far, w_x), (w_dt_far, w_dt), (tokens_far, tokens), (w_in_far, w_in), (grad_gate_far, grad_gate), (grad_mid_far, grad_mid))
        )
    ]
    for load in loads:
        load.start()
    dec[...] = step[...] + reset_of(meta, columns(0, meta))
    act_f = act[...].astype(f32)
    sa[...] = step[...] * act_f
    rates[...] = -jnp.exp(a_log[...])
    rates2[...] = rates[...] * LOG2E

    ahead_carry = joined(forward, lambda turn: BLOCKS - 1 - turn, BLOCKS - 1 - place, got, rates2)
    for tile, state in zip(TILES, ahead_carry):
        wide[R : R + N, tile] = state

    def ahead(i, states):
        states = list(states)
        base = pl.multiple_of(i * STEPS, STEPS)
        cols = bc[i]
        for k in range(STEPS):
            b_col = column(cols, 0, k)
            total = jnp.zeros((N, LANES), f32)
            for q, tile in enumerate(TILES):
                rows = pl.ds(base, STEPS), tile
                factor = jnp.exp2(dec[rows][k : k + 1] * rates2[:, tile])
                moved = factor * states[q]
                decay[base + k, :, tile] = factor
                kept[base + k, :, tile] = moved
                states[q] = moved + b_col * sa[rows][k : k + 1]
                total = total + states[q] * g[rows][k : k + 1]
            sum_c[base + k] = total
        return tuple(states)

    lax.fori_loop(0, T // STEPS, ahead, tuple(start[:, tile] for tile in TILES))
    first_carry = tuple(wide[R : R + N, tile] for tile in TILES)
    wide[R + N : R + 2 * N] = jnp.zeros((N, E), f32)

    def behind(turn, carry):
        carry = list(carry)
        i = T // STEPS - 1 - turn
        base = pl.multiple_of(i * STEPS, STEPS)
        cols = bc[i]
        by_rate = [[None] * STEPS for _ in TILES]
        by_b = [[None] * STEPS for _ in TILES]
        along = [wide[R + N : R + 2 * N, tile] for tile in TILES]
        for k in reversed(range(STEPS)):
            b_col = column(cols, 0, k)
            c_col = column(cols, N, k)
            total = jnp.zeros((N, LANES), f32)
            for q, tile in enumerate(TILES):
                rows = pl.ds(base, STEPS), tile
                adjoint = g[rows][k : k + 1] * c_col + carry[q]
                carry[q] = decay[base + k, :, tile] * adjoint
                log_grad = adjoint * kept[base + k, :, tile]
                along[q] = along[q] + log_grad * step[rows][k : k + 1]
                by_rate[q][k] = halves(log_grad * rates[:, tile])
                by_b[q][k] = halves(adjoint * b_col)
                total = total + adjoint * sa[rows][k : k + 1]
            sum_b[base + k] = total
        for q, tile in enumerate(TILES):
            wide[R + N : R + 2 * N, tile] = along[q]
            gs[pl.ds(base, STEPS), tile] = stack_sums(by_rate[q])
            ab[pl.ds(base, STEPS), tile] = stack_sums(by_b[q])
        return tuple(carry)

    lax.fori_loop(0, T // STEPS, behind, first_carry)
    wide[R : R + N] = wide[R + N : R + 2 * N] * rates[...]
    lane = lax.broadcasted_iota(i32, (LANES, LANES), 1)
    turned = jnp.zeros((T, LANES), f32)
    for at, sums in ((0, sum_b), (N, sum_c)):
        for n in range(N):
            one = (lane == at + n).astype(f32).astype(bf16)
            values = sums[:, n, :]
            high = values.astype(bf16)
            turned = turned + mm(high, one) + mm((values - high.astype(f32)).astype(bf16), one)
    for load in loads:
        load.wait()
    adjoint_b = ab[...]
    grad_step = gs[...] + adjoint_b * act_f
    grad_act = g[...] * d_skip[...] + adjoint_b * step[...]
    grad_pre = (grad_step * sigmoid(pre[...])).astype(bf16)
    vec[...] = jnp.zeros((N, E), f32)
    vec[KERNEL + 1 : KERNEL + 2] = jnp.sum(grad_pre.astype(f32), axis=0, keepdims=True)
    vec[KERNEL + 2 : KERNEL + 3] = g_skip[...]
    wide[0:R] = mm_tn(dt_low[...], grad_pre)
    grad_proj = jnp.concatenate([mm_nt(grad_pre, w_dt[...]), turned[:, 0 : 2 * N]], axis=1).astype(bf16)
    gw_x = mm_tn(grad_proj, act[...])
    grad_act = grad_act + mm(grad_proj, w_x[...])
    grad_conv = grad_act * silu_slope(conv[...])
    vec[KERNEL : KERNEL + 1] = jnp.sum(grad_conv, axis=0, keepdims=True)
    padded[0:T] = grad_conv
    padded[T : T + 8] = jnp.zeros((8, E), f32)
    ext[...] = ext_low[...].astype(f32)
    own_doc = doc_of(meta, columns(0, meta))
    own = jnp.zeros((T, E), f32)
    lift = KERNEL - 1
    rows = lax.broadcasted_iota(i32, (T, 1), 0)
    for offset in range(KERNEL):
        same = (doc_of(meta, columns(offset - lift, meta)) == own_doc).astype(f32)
        low = HALO - lift + offset
        vec[offset : offset + 1] = jnp.sum(grad_conv * ext[low : low + T] * same, axis=0, keepdims=True)
        up = lift - offset
        ahead_same = (doc_of(meta, columns(0, meta)) == doc_of(meta, columns(up, meta))) & (rows < T - up)
        own = own + conv_w[offset : offset + 1] * padded[up : up + T] * ahead_same.astype(f32)
    grad_ext[HALO : HALO + T] = own
    first = meta[0]
    edges = [jnp.zeros((HALO - lift, E), f32)]
    for row in range(lift):
        edge = jnp.zeros((1, E), f32)
        here = doc_of(meta, first - lift + row + jnp.zeros((1, 1), i32))
        for offset in range(row + 1):
            at = row - offset
            same = (doc_of(meta, first + at + jnp.zeros((1, 1), i32)) == here).astype(f32)
            edge = edge + conv_w[offset : offset + 1] * padded[at : at + 1] * same
        edges.append(edge)
    grad_ext[0:HALO] = jnp.concatenate(edges, axis=0)
    low_edge = grad_ext[0:HALO].astype(bf16)
    low_own = grad_ext[HALO : HALO + T].astype(bf16)
    values = tokens[...].astype(f32)
    upstream = mm_nt(low_own, w_in[:, :E]) + mm_nt(grad_gate[...], w_in[:, E:])
    back, gain_own = norm_back(values, inverse_rms(values), gain[...], upstream)
    grad_tokens[...] = grad_mid[...] + back
    before = halo[...].astype(f32)
    back, gain_edge = norm_back(before, inverse_rms(before), gain[...], mm_nt(low_edge, w_in[:, :E]))
    tail[...] = back[HALO - 8 : HALO]
    vec[KERNEL + 3 : KERNEL + 4, 0:D] = gain_own + gain_edge
    vec[KERNEL + 3 : KERNEL + 4, D:E] = g_gain_two[...]
    wide[R + N : R + 2 * N] = vec[...]
    for core in range(2):

        @pl.when(meta[2 + DOCS] == core)
        def _():
            for j in range(D // 128):
                cols = slice(core * D + j * 128, core * D + (j + 1) * 128)
                keep[0:HALO, j * 128 : (j + 1) * 128] = low_edge[:, cols]
                keep[HALO : HALO + T, j * 128 : (j + 1) * 128] = low_own[:, cols]
                cols = slice((1 - core) * D + j * 128, (1 - core) * D + (j + 1) * 128)
                base = j * (HALO + T)
                give[base : base + HALO] = low_edge[:, cols]
                give[base + HALO : base + HALO + T] = low_own[:, cols]
            base = D // 128 * (HALO + T)
            for j in range(E // 128):
                cols = slice(j * 128, (j + 1) * 128)
                mine, other = (gw_x, wide) if core == 0 else (wide, gw_x)
                part_keep[j * 64 : (j + 1) * 64] = mine[:, cols]
                give[base + j * 64 : base + (j + 1) * 64] = other[:, cols].astype(bf16)


def early_weights(meta, keep, got, out, both):
    both[0:T] = keep[...]
    both[T : 2 * T] = got[...]
    left_right = (((0, 1), (2, 3), (2, 4), (2, 5)), ((0, 2), (1, 2), (3, 4), (3, 5)))
    for core in range(2):

        @pl.when(meta[2 + DOCS] == core)
        def _():
            for j, (a, b) in enumerate(left_right[core]):
                left, right = both[:, a * D : (a + 1) * D], both[:, b * D : (b + 1) * D]
                result = mm_tn(left, right).astype(bf16)
                for q in range(D // LANES):
                    out[(4 * j + q) * D : (4 * j + q + 1) * D] = result[:, q * LANES : (q + 1) * LANES]


def late_weights(keep, part_keep, low_own, low_other, got, out, whole):
    left = jnp.concatenate([low_own[...], low_other[...]], axis=0)
    rows = HALO + T
    for j in range(D // LANES):
        right = jnp.concatenate([keep[:, j * LANES : (j + 1) * LANES], got[j * rows : (j + 1) * rows]], axis=0)
        whole[j * D : (j + 1) * D] = mm_tn(left, right)
    base = D // LANES * rows
    whole[4 * D : 5 * D] = part_keep[...] + got[base : base + D].astype(f32)
    for d in range(SHARES):
        main = whole[d * MAIN : (d + 1) * MAIN]
        small = whole[4 * D + d * SMALL : 4 * D + (d + 1) * SMALL]
        out[d] = jnp.concatenate([main, small], axis=0).astype(bf16)


def add_early(early, late, out):
    total = early[0].astype(f32)
    for j in range(1, SHARES):
        total = total + early[j].astype(f32)
    for j in range(SHARES):
        out[j] = jnp.concatenate([late[j].astype(f32), total], axis=0).astype(bf16)


def add_late(got, out, held, sem):
    copy = pltpu.make_async_copy(got.at[:, pl.ds(0, 3 * N)], held, sem)
    copy.start()
    copy.wait()
    total = held[0].astype(f32)[0:LATE]
    for j in range(1, SHARES):
        total = total + held[j].astype(f32)[0:LATE]
    low = total.astype(bf16)
    for j in range(SHARES):
        out[j] = low


def finish_early(meta, mine, other, gw_o, gw_q, gw_k, gw_v, gw_out, gw_in, gate, sem):
    is_zero = meta[2 + DOCS] == 0
    for d in reversed(range(SHARES)):
        a, b = mine[d].astype(f32)[LATE:], other[d].astype(f32)[LATE:]
        j, q, r = d // 16, d // 4 % 4, d % 4 * T
        tile = TILES[q]
        (gw_o, gw_q, gw_k, gw_v)[j][r : r + T, tile] = jnp.where(is_zero, a, b)
        one = jnp.where(is_zero, b, a)
        if j < 2:
            gw_out[j * D + r : j * D + r + T, tile] = one
        else:
            low = (j - 2) * D + q * LANES
            gate[r : r + T, low : low + LANES] = one
        if d == SHARES // 2:
            copy = pltpu.make_async_copy(gate, gw_in.at[:, pl.ds(E, E)], sem)
            copy.start()
    copy.wait()


def finish_late(
    meta, mine, other, _, gw_in, gw_x, gw_dt, g_a_log, g_conv_w, g_conv_b, g_dt_b, g_skip, g_gain_one,
    g_gain_two, conv, sems,
):
    is_zero = meta[2 + DOCS] == 0
    copies = []
    for d in range(SHARES):
        a, b = mine[d].astype(f32), other[d].astype(f32)
        zero = jnp.where(is_zero, a, b)
        one = jnp.where(is_zero, b, a)
        j, r = d // 16, d % 16 * MAIN
        conv[r : r + MAIN, j * LANES : (j + 1) * LANES] = zero[0:MAIN]
        conv[r : r + MAIN, D + j * LANES : D + (j + 1) * LANES] = one[0:MAIN]
        if d % 16 == 15:
            for side in range(2):
                cols = pl.ds(side * D + j * LANES, LANES)
                copies.append(pltpu.make_async_copy(conv.at[:, cols], gw_in.at[:, cols], sems.at[side, j]))
                copies[-1].start()
        q, r = d // 8, d % 8 * SMALL
        tile = TILES[q]
        gw_x[r : r + SMALL, tile] = zero[MAIN:]
        for out, low, high in ((gw_dt, 0, R), (g_a_log, R, R + N)):
            if low <= r < high:
                out[r - low : r - low + SMALL, tile] = one[MAIN:]
        if r == R + N:
            g_conv_w[:, tile] = one[MAIN : MAIN + KERNEL]
            at = MAIN + KERNEL
            for i, out in enumerate((g_conv_b, g_dt_b, g_skip)):
                out[:, tile] = one[at + i : at + i + 1]
            out = g_gain_one if q < 4 else g_gain_two
            out[:, TILES[q % 4]] = one[at + 3 : at + 4]
    for copy in copies:
        copy.wait()


MEGABYTES = dict(
    mamba_in=16, mamba_out=16, attention=16, middle_back=20, early_weights=12, mamba_back=38, late_weights=12,
    add_late=8, add_early=14, finish_early=24, finish_late=12,
)


def call(body, name, outs, scratch, *args, smem=True, outside=(), aliases=None, far=(), far_out=(), there=(), sems=()):
    aliases = aliases or {}
    args = [pltpu.with_memory_space_constraint(x, pltpu.HBM) if i in far else x for i, x in enumerate(args)]
    specs = [pl.BlockSpec(memory_space=pl.ANY if i in aliases or i in there else pltpu.VMEM) for i in range(len(args))]
    if smem:
        specs[0] = pl.BlockSpec(memory_space=pltpu.SMEM)
    return pl.pallas_call(
        body,
        name=name,
        out_shape=[pltpu.HBM(s, t) if i in far_out else jax.ShapeDtypeStruct(s, t) for i, (s, t) in enumerate(outs)],
        in_specs=specs,
        out_specs=[pl.BlockSpec(memory_space=pl.ANY if i in outside else pltpu.VMEM) for i in range(len(outs))],
        scratch_shapes=[pltpu.VMEM(s, t) for s, t in scratch]
        + [pltpu.SemaphoreType.DMA(n) for n in sems],
        input_output_aliases=aliases,
        compiler_params=pltpu.CompilerParams(vmem_limit_bytes=MEGABYTES[name] << 20),
    )(*args)


def shift(x, by):
    pairs = [(i, i + by) for i in range(BLOCKS) if 0 <= i + by < BLOCKS]
    return lax.ppermute(x, PLACE, pairs)


def swap(x):
    return lax.all_to_all(x, PLACE, 0, 0, tiled=True)


def partner(x):
    return lax.ppermute(x, "core", [(0, 1), (1, 0)])


def trade(x):
    return lax.all_to_all(x, SAME, 0, 0, tiled=True)


def layer(
    tokens, starts, gain_one, w_in, conv_w, conv_b, w_x, w_dt, dt_bias, a_log, d_skip, w_out,
    gain_two, w_q, w_k, w_v, w_o, cotangent,
):
    tokens, cot = tokens[0], cotangent[0]
    place = lax.axis_index(PLACE)
    core = lax.axis_index("core").astype(i32)
    meta = jnp.concatenate([jnp.stack([place * T, place]).astype(i32), starts[0], core[None]])
    row = lambda v: v.reshape(1, -1)
    halo = shift(tokens[T - HALO :], 1)
    tn = ((N, E), f32)
    te, tel, td, tdl = ((T, E), f32), ((T, E), bf16), ((T, D), f32), ((T, D), bf16)
    w_x = w_x.T
    send, grad_att, low_ext, ext, gate, conv, act, step, pre, bc, dt_low = call(
        mamba_in, "mamba_in",
        [((BLOCKS, SENT, LANES), bf16), tdl, ((HALO + T, D), bf16), ((HALO + T, E), bf16), tel, te, tel, te, te,
         ((T // STEPS, 2 * N, 128), f32), ((T, R), bf16)],
        [((HALO + T, E), f32), te, te, ((T, 128), f32), tn, tn],
        meta, tokens, halo, row(gain_one), w_in, conv_w, row(conv_b), w_x, w_dt, row(dt_bias), a_log, cot, w_o,
        far=(1, 3, 4, 5, 6, 7, 8, 9, 10, 11, 12), far_out=(2, 3, 5, 8, 10),
    )
    low_other = partner(low_ext)
    forward = swap(send)
    packed, start, ssm, gated, middle, normed = call(
        mamba_out, "mamba_out",
        [((BLOCKS, ROWS, 128), bf16), ((N, E), f32), te, tel, td, tdl],
        [te, te, te, tn],
        meta, forward, tokens, step, act, bc, gate, a_log, row(d_skip), w_out, row(gain_two),
        w_q, w_k, w_v, grad_att, far_out=(1,),
    )
    (back,) = call(
        attention, "attention",
        [((BLOCKS, ROWS, 128), bf16)],
        [((128, BLOCKS * T), bf16), ((BLOCKS, T, QCHUNK), f32), ((BLOCKS, T, QCHUNK), f32),
         ((BLOCKS, T, 128), f32)],
        meta, swap(packed),
    )
    wide = ((T, 6 * D), bf16)
    send, mixed, grad_mid, g, grad_gate, keep, give, g_gain_two, g_skip = call(
        middle_back, "middle_back",
        [((BLOCKS, N * 8, LANES), bf16), tdl, td, te, tel, wide, wide, ((1, D), f32), ((1, E), f32)],
        [tdl] * 4 + [te, tn],
        meta, swap(back), cot, middle, normed, low_ext, gated, gate, ssm, act, step, bc, a_log,
        row(d_skip), w_o, w_q, w_k, w_v, w_out, row(gain_two), far_out=(1, 2, 3, 4, 5, 7, 8),
    )
    (early,) = call(
        early_weights, "early_weights", [((16 * D, LANES), bf16)], [((2 * T, 6 * D), bf16)],
        meta, keep, partner(give), far=(1,),
    )
    early, behind, low_other = lax.optimization_barrier((early, swap(send), low_other))
    early = trade(early.reshape(SHARES, T, LANES))
    grad_tokens, tail, keep, give, part_keep = call(
        mamba_back, "mamba_back",
        [td, ((8, D), f32), ((HALO + T, D), bf16), ((4 * (HALO + T) + D, 128), bf16), ((D, 128), f32)],
        [te, te, ((T, N, E), f32), ((T, N, E), f32), te, te, ((HALO + T, E), f32),
         ((T + 8, E), f32), ((HALO + T, E), f32), ((N, E), f32), ((64, E), f32), tn, tn,
         ((T, N, LANES), f32), ((T, N, LANES), f32),
         te, ((T, R), bf16), te, ((HALO + T, E), bf16), ((64, E), bf16), ((R, E), bf16), tdl, ((D, 2 * E), bf16), tel, td],
        meta, behind, forward, start, g, act, step, pre, bc, dt_low, conv, ext, a_log,
        row(d_skip), conv_w, w_x, w_dt, tokens, halo, row(gain_one), w_in, grad_gate, grad_mid,
        g_gain_two, g_skip, far=tuple(range(1, 25)), far_out=(0, 1, 2, 4),
        there=(7, 9, 10, 11, 15, 16, 17, 20, 21, 22), sems=((10,),),
    )
    early, tail = lax.optimization_barrier((early, shift(tail, -1)))
    (late,) = call(
        late_weights, "late_weights", [((SHARES, LATE, LANES), bf16)], [((5 * D, LANES), f32)],
        keep, part_keep, low_ext, low_other, partner(give), smem=False, far=(0, 1, 2, 3, 4), far_out=(0,),
    )
    (both,) = call(
        add_early, "add_early", [((SHARES, LATE + T, LANES), bf16)], [], early, late, smem=False,
        far=(1,), far_out=(0,),
    )
    shares = trade(both)
    (late,) = call(
        add_late, "add_late", [((SHARES, LATE, LANES), bf16)], [((SHARES, 3 * N, LANES), bf16)],
        shares, smem=False, far=(0,), there=(0,), sems=((),),
    )
    late = trade(late)
    gw_o, gw_q, gw_k, gw_v, gw_out, gw_in = call(
        finish_early, "finish_early",
        [((D, D), f32)] * 4 + [((E, D), f32), ((D, 2 * E), f32)], [((D, E), f32)],
        meta, shares, partner(shares), outside=(5,), far=(1, 2), sems=((),),
    )
    grad_tokens = grad_tokens.at[T - 8 :].add(tail)
    late, gw_in, grad_tokens = lax.optimization_barrier((late, gw_in, grad_tokens))
    gw_in, gw_x, gw_dt, g_a_log, g_conv_w, g_conv_b, g_dt_b, g_skip, g_gain_one, g_gain_two = call(
        finish_late, "finish_late",
        [((D, 2 * E), f32), ((64, E), f32), ((R, E), f32), tn, ((KERNEL, E), f32), ((1, E), f32),
         ((1, E), f32), ((1, E), f32), ((1, D), f32), ((1, D), f32)],
        [((D, E), f32)],
        meta, late, partner(late), gw_in, outside=(0,), aliases={3: 0}, sems=((2, 4),),
    )
    return (
        mixed[None], grad_tokens[None], g_gain_one[0], gw_in, g_conv_w, g_conv_b[0], gw_x.T, gw_dt,
        g_dt_b[0], g_a_log, g_skip[0], gw_out, g_gain_two[0], gw_q, gw_k, gw_v, gw_o,
    )


def solution(mesh):
    rows, seq, head = mesh.devices.shape
    fine = Mesh(mesh.devices.reshape(rows // 2, 2, seq, head), ALL)
    split = P(("y", "core"), PLACE, None)
    return jax.shard_map(
        layer,
        mesh=fine,
        in_specs=(split, P(("y", "core"), None)) + (P(),) * 15 + (split,),
        out_specs=(split, split) + (P(),) * 15,
        check_vma=False,
    )
```

```python
import functools

import jax
import jax.numpy as jnp
from jax import lax
from jax.experimental import pallas as pl
from jax.experimental.pallas import tpu as pltpu
from jax.sharding import Mesh, PartitionSpec as P

T, D, E, N, R, HD = 128, 512, 1024, 16, 32, 64
HEADS, BLOCKS, HALF, DOCS, KERNEL, HALO = 8, 16, 64, 6, 4, 16
LANES, STEPS = 128, 8
TILES = [slice(q * LANES, (q + 1) * LANES) for q in range(E // LANES)]
ROWS = T + HALF
SENT = N * 8 + 16
RESET = 1e4
LOG2E = 1.4426950408889634
EPS = 1e-05
MASKED = -1e30
PLACE = ("seq", "head")
ALL = ("y", "core", "seq", "head")
SAME, SHARES, MAIN, SMALL, LATE = ("y", "seq", "head"), 64, 32, 8, 40
bf16, f32, i32 = jnp.bfloat16, jnp.float32, jnp.int32


def mm(a, b):
    return jnp.dot(a, b, preferred_element_type=f32)


def mm_nt(a, b):
    return lax.dot_general(a, b, (((1,), (1,)), ((), ())), preferred_element_type=f32)


def mm_tn(a, b):
    return lax.dot_general(a, b, (((0,), (0,)), ((), ())), preferred_element_type=f32)


def doc_of(meta, pos):
    count = jnp.zeros(pos.shape, i32)
    for k in range(DOCS):
        count = count + (meta[2 + k] <= pos).astype(i32)
    return count


def reset_of(meta, pos):
    hit = meta[2] == pos
    for k in range(1, DOCS):
        hit = hit | (meta[2 + k] == pos)
    return jnp.where(hit, RESET, 0.0)


def inverse_rms(x):
    return lax.rsqrt(jnp.mean(x * x, axis=-1, keepdims=True) + EPS)


def sigmoid(x):
    return 1.0 / (1.0 + jnp.exp(-x))


def silu_slope(x):
    s = sigmoid(x)
    return s * (1.0 + x * (1.0 - s))


def norm_back(values, inverse, gain, upstream):
    scaled = upstream * gain
    inner = jnp.mean(values * scaled, axis=-1, keepdims=True)
    back = inverse * scaled - values * (inverse * inverse * inverse) * inner
    return back, jnp.sum(upstream * values * inverse, axis=0, keepdims=True)


def columns(offset, meta):
    first = meta[0]
    return first + offset + lax.broadcasted_iota(i32, (T, 1), 0)


def stack_sums(parts):
    row = lax.broadcasted_iota(i32, parts[0].shape, 0)
    for by in (1, 2, 4):
        first = (row & by) == 0
        parts = [
            jnp.where(first, a, b) + pltpu.roll(jnp.where(first, b, a), by, axis=0)
            for a, b in zip(parts[0::2], parts[1::2])
        ]
    return parts[0]


def column(block, low, k):
    return jnp.broadcast_to(block[low : low + N, k : k + 1], (N, LANES))


def halves(x):
    return x[0:8] + x[8:16]


def scan_forward(dec, sa, bc, rates2, start, result=None):
    def block(i, states):
        states = list(states)
        base = pl.multiple_of(i * STEPS, STEPS)
        cols = bc[i]
        sums = [[None] * STEPS for _ in TILES]
        for k in range(STEPS):
            b_col = column(cols, 0, k)
            c_col = column(cols, N, k)
            for q, tile in enumerate(TILES):
                factor = jnp.exp2(dec[pl.ds(base, STEPS), tile][k : k + 1] * rates2[:, tile])
                states[q] = factor * states[q] + b_col * sa[pl.ds(base, STEPS), tile][k : k + 1]
                if result is not None:
                    sums[q][k] = halves(states[q] * c_col)
        if result is not None:
            for q, tile in enumerate(TILES):
                result[pl.ds(base, STEPS), tile] = stack_sums(sums[q])
        return tuple(states)

    return lax.fori_loop(0, T // STEPS, block, tuple(start[:, tile] for tile in TILES))


def mamba_in(
    meta, tokens, halo, gain, w_in, conv_w, conv_b, w_x, w_dt, dt_b, a_log, cot, w_o,
    send, grad_att, low_out, ext_out, gate_out, conv_out, act_out, step_out, pre_out, bc_out, dt_out,
    ext, dec, sa, xp, rates2, zero,
):
    grad_att[...] = mm_nt(cot[...], w_o[...]).astype(bf16)
    own = tokens[...].astype(f32)
    before = halo[...].astype(f32)
    low_own = (own * inverse_rms(own) * gain[...]).astype(bf16)
    low_before = (before * inverse_rms(before) * gain[...]).astype(bf16)
    conv_own = mm(low_own, w_in[:, :E]).astype(bf16)
    conv_before = mm(low_before, w_in[:, :E]).astype(bf16)
    low_out[0:HALO] = low_before
    low_out[HALO : HALO + T] = low_own
    ext_out[0:HALO] = conv_before
    ext_out[HALO : HALO + T] = conv_own
    ext[0:HALO] = conv_before.astype(f32)
    ext[HALO : HALO + T] = conv_own.astype(f32)
    gate_out[...] = mm(low_own, w_in[:, E:]).astype(bf16)
    own_doc = doc_of(meta, columns(0, meta))
    conv = jnp.broadcast_to(conv_b[...], (T, E))
    for offset in range(KERNEL):
        same = (doc_of(meta, columns(offset - KERNEL + 1, meta)) == own_doc).astype(f32)
        low = HALO - KERNEL + 1 + offset
        conv = conv + conv_w[offset : offset + 1] * ext[low : low + T] * same
    conv_out[...] = conv
    act = (conv * sigmoid(conv)).astype(bf16)
    act_out[...] = act
    proj = mm_nt(act, w_x[...])
    dt_low = proj[:, :R].astype(bf16)
    dt_out[...] = dt_low
    pre = mm(dt_low, w_dt[...]) + dt_b[...]
    pre_out[...] = pre
    step = jnp.maximum(pre, 0.0) + jnp.log1p(jnp.exp(-jnp.abs(pre)))
    step_out[...] = step
    held = step + reset_of(meta, columns(0, meta))
    dec[...] = held
    sa[...] = step * act.astype(f32)
    xp[...] = jnp.zeros((T, 128), f32)
    xp[:, 0 : R + 2 * N] = proj
    turned = xp[...].T
    for i in range(T // STEPS):
        bc_out[i, :, 0:STEPS] = turned[R : R + 2 * N, i * STEPS : (i + 1) * STEPS]
    total = jnp.sum(held, axis=0, keepdims=True)
    high = total.astype(bf16)
    rest = (total - high.astype(f32)).astype(bf16)
    rates2[...] = -jnp.exp(a_log[...]) * LOG2E
    zero[...] = jnp.zeros((N, E), f32)
    states = scan_forward(dec, sa, bc_out, rates2, zero)
    sums = [high[:, tile].astype(f32) for tile in TILES] + [rest[:, tile].astype(f32) for tile in TILES]
    ended = jnp.concatenate(list(states) + sums, axis=0).astype(bf16)
    for j in range(BLOCKS):
        send[j] = ended


def joined(blocks, first, last, ends, rates2):
    def join(turn, states):
        sent = blocks[first(turn)].astype(f32)
        own = sent if ends is None else ends[first(turn)].astype(f32)
        total = sent[N * 8 : N * 8 + 8] + sent[N * 8 + 8 : N * 8 + 16]
        return tuple(
            jnp.exp2(rates2[:, tile] * total[q : q + 1]) * states[q] + own[q * N : (q + 1) * N]
            for q, tile in enumerate(TILES)
        )

    return lax.fori_loop(0, last, join, tuple(jnp.zeros((N, LANES), f32) for _ in TILES))


def roll_half(x):
    return pltpu.roll(x, HALF, axis=1)


def mamba_out(
    meta, got, tokens, step, act, bc, gate, a_log, d_skip, w_out, gain, w_q, w_k, w_v, grad_att,
    send, start_out, ssm_out, gated_out, middle_out, normed_out,
    dec, sa, ssm, rates2,
):
    place = meta[1]
    rates2[...] = -jnp.exp(a_log[...]) * LOG2E
    dec[...] = step[...] + reset_of(meta, columns(0, meta))
    act_f = act[...].astype(f32)
    sa[...] = step[...] * act_f
    for tile, state in zip(TILES, joined(got, lambda turn: turn, place, None, rates2)):
        start_out[:, tile] = state
    scan_forward(dec, sa, bc, rates2, start_out, ssm)
    result = ssm[...] + d_skip[...] * act_f
    ssm_out[...] = result
    gates = gate[...].astype(f32)
    gated = (result * (gates * sigmoid(gates))).astype(bf16)
    gated_out[...] = gated
    middle = tokens[...].astype(f32) + mm(gated, w_out[...])
    middle_out[...] = middle
    normed = (middle * inverse_rms(middle) * gain[...]).astype(bf16)
    normed_out[...] = normed
    queries = mm(normed, w_q[...]).astype(bf16).astype(f32) * (HD ** -0.5)
    keys = mm(normed, w_k[...])
    vals = mm(normed, w_v[...])
    grads = grad_att[...].astype(f32)
    low = lax.broadcasted_iota(i32, (T, 128), 1) < HALF
    for m in range(HEADS // 2):
        tile = slice(m * 128, (m + 1) * 128)
        for odd in range(2):
            for first, second, at, rows in ((keys, vals, 0, T), (queries, grads, T, HALF)):
                a, b = first[:, tile], second[:, tile]
                pair = jnp.where(low, a, roll_half(b)) if odd == 0 else jnp.where(low, roll_half(a), b)
                pair = pair.astype(bf16)
                dest = 2 * (2 * m + odd)
                if rows == T:
                    send[dest, 0:T] = pair
                    send[dest + 1, 0:T] = pair
                else:
                    send[dest, T:ROWS] = pair[0:HALF]
                    send[dest + 1, T:ROWS] = pair[HALF:T]


QCHUNK, QBLOCKS = 256, 4


def attention(meta, got, send, kv_t, scores, grads, kv_grad):
    parity = lax.rem(meta[1], 2)
    for i in range(BLOCKS):
        kv_t[:, i * T : (i + 1) * T] = got[i, 0:T].astype(f32).T.astype(bf16)
    lane = lax.broadcasted_iota(i32, (1, QCHUNK), 1)
    low_q = lax.broadcasted_iota(i32, (QCHUNK, 128), 1) < HD
    low_k = lax.broadcasted_iota(i32, (T, 128), 1) < HD
    key_row = lax.broadcasted_iota(i32, (T, QCHUNK), 0)
    for c in range(BLOCKS // QBLOCKS):
        qg = jnp.concatenate([got[c * QBLOCKS + b, T:ROWS] for b in range(QBLOCKS)], axis=0)
        q_only = jnp.where(low_q, qg.astype(f32), 0.0).astype(bf16)
        g_only = jnp.where(low_q, 0.0, qg.astype(f32)).astype(bf16)
        pos = (c * QBLOCKS + lane // HALF) * T + parity * HALF + lane % HALF
        begin = jnp.zeros((1, QCHUNK), i32)
        for k in range(DOCS):
            begin = jnp.maximum(begin, jnp.where(meta[2 + k] <= pos, meta[2 + k], 0))
        tiles = (c + 1) * QBLOCKS
        top = jnp.full((8, QCHUNK), MASKED, f32)
        for i in range(tiles):
            s = mm_nt(got[i, 0:T], q_only)
            allowed = key_row >= begin - i * T
            if i >= c * QBLOCKS:
                allowed = allowed & (key_row <= pos - i * T)
            s = jnp.where(allowed, s, MASKED)
            scores[i] = s
            top = jnp.maximum(top, jnp.max(s.reshape(T // 8, 8, QCHUNK), axis=0))
        top = jnp.max(top, axis=0, keepdims=True)
        total = jnp.zeros((8, QCHUNK), f32)
        cross = jnp.zeros((8, QCHUNK), f32)
        for i in range(tiles):
            p = jnp.exp2((scores[i] - top) * LOG2E)
            scores[i] = p
            g = mm_nt(got[i, 0:T], g_only)
            grads[i] = g
            total = total + jnp.sum(p.reshape(T // 8, 8, QCHUNK), axis=0)
            cross = cross + jnp.sum((p * g).reshape(T // 8, 8, QCHUNK), axis=0)
        inverse = 1.0 / jnp.sum(total, axis=0, keepdims=True)
        cross = jnp.sum(cross, axis=0, keepdims=True) * inverse
        out_t = jnp.zeros((128, QCHUNK), f32)
        dq_t = jnp.zeros((128, QCHUNK), f32)
        for i in range(tiles):
            prob = scores[i] * inverse
            low_p = prob.astype(bf16)
            low_s = (prob * (grads[i] - cross)).astype(bf16)
            turned = kv_t[:, i * T : (i + 1) * T]
            out_t = out_t + mm(turned, low_p)
            dq_t = dq_t + mm(turned, low_s)
            both = jnp.where(low_k, mm(low_s, qg), mm(low_p, qg))
            if i >= c * QBLOCKS:
                kv_grad[i] = both
            else:
                kv_grad[i] = kv_grad[i] + both
        pair = jnp.where(low_q, dq_t.T * (HD ** -0.5), out_t.T).astype(bf16)
        for b in range(QBLOCKS):
            send[c * QBLOCKS + b, T:ROWS] = pair[b * HALF : (b + 1) * HALF]
    for i in range(BLOCKS):
        send[i, 0:T] = kv_grad[i].astype(bf16)


def middle_back(
    meta, got, cot, middle, normed, low_ext, gated, gate, ssm, act, step, bc, a_log, d_skip,
    w_o, w_q, w_k, w_v, w_out, gain,
    send, mixed_far, grad_mid_far, g_far, grad_gate_far, keep_far, give, g_gain, g_skip,
    att, dq, dk, dv, dec, rates2, mixed, grad_mid_out, g_out, grad_gate_out, keep, sems,
):
    low = lax.broadcasted_iota(i32, (HALF, 128), 1) < HALF
    low_t = lax.broadcasted_iota(i32, (T, 128), 1) < HALF
    for m in range(HEADS // 2):
        tile = slice(m * 128, (m + 1) * 128)
        for p in range(2):
            a = got[4 * m + p, T:ROWS].astype(f32)
            b = got[4 * m + 2 + p, T:ROWS].astype(f32)
            rows = slice(p * HALF, (p + 1) * HALF)
            dq[rows, tile] = jnp.where(low, a, roll_half(b)).astype(bf16)
            att[rows, tile] = jnp.where(low, roll_half(a), b).astype(bf16)
        a = got[4 * m, 0:T].astype(f32) + got[4 * m + 1, 0:T].astype(f32)
        b = got[4 * m + 2, 0:T].astype(f32) + got[4 * m + 3, 0:T].astype(f32)
        dk[:, tile] = jnp.where(low_t, a, roll_half(b)).astype(bf16)
        dv[:, tile] = jnp.where(low_t, roll_half(a), b).astype(bf16)
    cot_low = cot[...]
    values = middle[...]
    mixed[...] = (values + mm(att[...], w_o[...])).astype(bf16)
    upstream = mm_nt(dq[...], w_q[...]) + mm_nt(dk[...], w_k[...]) + mm_nt(dv[...], w_v[...])
    back, gain_grad = norm_back(values, inverse_rms(values), gain[...], upstream)
    g_gain[...] = gain_grad
    grad_mid = cot_low.astype(f32) + back
    grad_mid_out[...] = grad_mid
    mid_low = grad_mid.astype(bf16)
    grad_gated = mm_nt(mid_low, w_out[...]).astype(bf16).astype(f32)
    gates = gate[...].astype(f32)
    sig = sigmoid(gates)
    g = grad_gated * (gates * sig)
    g_out[...] = g
    grad_gate = (grad_gated * ssm[...] * (sig * (1.0 + gates * (1.0 - sig)))).astype(bf16)
    grad_gate_out[...] = grad_gate
    for first, second, core in ((keep, give, 0), (give, keep, 1)):

        @pl.when(meta[2 + DOCS] == core)
        def _():
            first[:, 0:D] = att[...]
            first[:, D : 2 * D] = cot_low
            first[:, 2 * D : 3 * D] = normed[...]
            first[:, 3 * D : 4 * D] = dq[...]
            first[:, 4 * D : 5 * D] = dk[...]
            first[:, 5 * D : 6 * D] = dv[...]
            second[:, 0:E] = gated[...]
            second[:, E : E + D] = mid_low
            second[:, E + D : 2 * E] = low_ext[HALO : HALO + T]
            second[:, 2 * E : 3 * E] = grad_gate

    g_skip[...] = jnp.sum(g * act[...].astype(f32), axis=0, keepdims=True)
    saves = [
        pltpu.make_async_copy(held, place, sems.at[i])
        for i, (held, place) in enumerate(
            ((mixed, mixed_far), (grad_mid_out, grad_mid_far), (g_out, g_far), (grad_gate_out, grad_gate_far), (keep, keep_far))
        )
    ]
    for save in saves:
        save.start()
    dec[...] = step[...] + reset_of(meta, columns(0, meta))
    rates2[...] = -jnp.exp(a_log[...]) * LOG2E

    def block(turn, carry):
        carry = list(carry)
        i = T // STEPS - 1 - turn
        base = pl.multiple_of(i * STEPS, STEPS)
        cols = bc[i]
        for k in reversed(range(STEPS)):
            c_col = column(cols, N, k)
            for q, tile in enumerate(TILES):
                factor = jnp.exp2(dec[pl.ds(base, STEPS), tile][k : k + 1] * rates2[:, tile])
                carry[q] = factor * (carry[q] + c_col * g_out[pl.ds(base, STEPS), tile][k : k + 1])
        return tuple(carry)

    carry = lax.fori_loop(0, T // STEPS, block, tuple(jnp.zeros((N, LANES), f32) for _ in TILES))
    ended = jnp.concatenate(carry, axis=0).astype(bf16)
    for j in range(BLOCKS):
        send[j] = ended
    for save in saves:
        save.wait()


def mamba_back(
    meta, got, forward, start, g, act, step, pre_far, bc, dt_low_far, conv_far, ext_low_far, a_log, d_skip,
    conv_w, w_x_far, w_dt_far, tokens_far, halo, gain, w_in_far, grad_gate_far, grad_mid_far, g_gain_two, g_skip,
    grad_tokens, tail, keep, give, part_keep,
    dec, sa, decay, kept, gs, ab, ext, padded, grad_ext, vec, wide, rates, rates2, sum_b, sum_c,
    pre, dt_low, conv, ext_low, w_x, w_dt, tokens, w_in, grad_gate, grad_mid, sems,
):
    place = meta[1]
    loads = [
        pltpu.make_async_copy(source, held, sems.at[i])
        for i, (source, held) in enumerate(
            ((pre_far, pre), (dt_low_far, dt_low), (conv_far, conv), (ext_low_far, ext_low), (w_x_far, w_x), (w_dt_far, w_dt), (tokens_far, tokens), (w_in_far, w_in), (grad_gate_far, grad_gate), (grad_mid_far, grad_mid))
        )
    ]
    for load in loads:
        load.start()
    dec[...] = step[...] + reset_of(meta, columns(0, meta))
    act_f = act[...].astype(f32)
    sa[...] = step[...] * act_f
    rates[...] = -jnp.exp(a_log[...])
    rates2[...] = rates[...] * LOG2E

    ahead_carry = joined(forward, lambda turn: BLOCKS - 1 - turn, BLOCKS - 1 - place, got, rates2)
    for tile, state in zip(TILES, ahead_carry):
        wide[R : R + N, tile] = state

    def ahead(i, states):
        states = list(states)
        base = pl.multiple_of(i * STEPS, STEPS)
        cols = bc[i]
        for k in range(STEPS):
            b_col = column(cols, 0, k)
            total = jnp.zeros((N, LANES), f32)
            for q, tile in enumerate(TILES):
                rows = pl.ds(base, STEPS), tile
                factor = jnp.exp2(dec[rows][k : k + 1] * rates2[:, tile])
                moved = factor * states[q]
                decay[base + k, :, tile] = factor
                kept[base + k, :, tile] = moved
                states[q] = moved + b_col * sa[rows][k : k + 1]
                total = total + states[q] * g[rows][k : k + 1]
            sum_c[base + k] = total
        return tuple(states)

    lax.fori_loop(0, T // STEPS, ahead, tuple(start[:, tile] for tile in TILES))
    first_carry = tuple(wide[R : R + N, tile] for tile in TILES)
    wide[R + N : R + 2 * N] = jnp.zeros((N, E), f32)

    def behind(turn, carry):
        carry = list(carry)
        i = T // STEPS - 1 - turn
        base = pl.multiple_of(i * STEPS, STEPS)
        cols = bc[i]
        by_rate = [[None] * STEPS for _ in TILES]
        by_b = [[None] * STEPS for _ in TILES]
        along = [wide[R + N : R + 2 * N, tile] for tile in TILES]
        for k in reversed(range(STEPS)):
            b_col = column(cols, 0, k)
            c_col = column(cols, N, k)
            total = jnp.zeros((N, LANES), f32)
            for q, tile in enumerate(TILES):
                rows = pl.ds(base, STEPS), tile
                adjoint = g[rows][k : k + 1] * c_col + carry[q]
                carry[q] = decay[base + k, :, tile] * adjoint
                log_grad = adjoint * kept[base + k, :, tile]
                along[q] = along[q] + log_grad * step[rows][k : k + 1]
                by_rate[q][k] = halves(log_grad * rates[:, tile])
                by_b[q][k] = halves(adjoint * b_col)
                total = total + adjoint * sa[rows][k : k + 1]
            sum_b[base + k] = total
        for q, tile in enumerate(TILES):
            wide[R + N : R + 2 * N, tile] = along[q]
            gs[pl.ds(base, STEPS), tile] = stack_sums(by_rate[q])
            ab[pl.ds(base, STEPS), tile] = stack_sums(by_b[q])
        return tuple(carry)

    lax.fori_loop(0, T // STEPS, behind, first_carry)
    wide[R : R + N] = wide[R + N : R + 2 * N] * rates[...]
    lane = lax.broadcasted_iota(i32, (LANES, LANES), 1)
    turned = jnp.zeros((T, LANES), f32)
    for at, sums in ((0, sum_b), (N, sum_c)):
        for n in range(N):
            one = (lane == at + n).astype(f32).astype(bf16)
            values = sums[:, n, :]
            high = values.astype(bf16)
            turned = turned + mm(high, one) + mm((values - high.astype(f32)).astype(bf16), one)
    for load in loads:
        load.wait()
    adjoint_b = ab[...]
    grad_step = gs[...] + adjoint_b * act_f
    grad_act = g[...] * d_skip[...] + adjoint_b * step[...]
    grad_pre = (grad_step * sigmoid(pre[...])).astype(bf16)
    vec[...] = jnp.zeros((N, E), f32)
    vec[KERNEL + 1 : KERNEL + 2] = jnp.sum(grad_pre.astype(f32), axis=0, keepdims=True)
    vec[KERNEL + 2 : KERNEL + 3] = g_skip[...]
    wide[0:R] = mm_tn(dt_low[...], grad_pre)
    grad_proj = jnp.concatenate([mm_nt(grad_pre, w_dt[...]), turned[:, 0 : 2 * N]], axis=1).astype(bf16)
    gw_x = mm_tn(grad_proj, act[...])
    grad_act = grad_act + mm(grad_proj, w_x[...])
    grad_conv = grad_act * silu_slope(conv[...])
    vec[KERNEL : KERNEL + 1] = jnp.sum(grad_conv, axis=0, keepdims=True)
    padded[0:T] = grad_conv
    padded[T : T + 8] = jnp.zeros((8, E), f32)
    ext[...] = ext_low[...].astype(f32)
    own_doc = doc_of(meta, columns(0, meta))
    own = jnp.zeros((T, E), f32)
    lift = KERNEL - 1
    rows = lax.broadcasted_iota(i32, (T, 1), 0)
    for offset in range(KERNEL):
        same = (doc_of(meta, columns(offset - lift, meta)) == own_doc).astype(f32)
        low = HALO - lift + offset
        vec[offset : offset + 1] = jnp.sum(grad_conv * ext[low : low + T] * same, axis=0, keepdims=True)
        up = lift - offset
        ahead_same = (doc_of(meta, columns(0, meta)) == doc_of(meta, columns(up, meta))) & (rows < T - up)
        own = own + conv_w[offset : offset + 1] * padded[up : up + T] * ahead_same.astype(f32)
    grad_ext[HALO : HALO + T] = own
    first = meta[0]
    edges = [jnp.zeros((HALO - lift, E), f32)]
    for row in range(lift):
        edge = jnp.zeros((1, E), f32)
        here = doc_of(meta, first - lift + row + jnp.zeros((1, 1), i32))
        for offset in range(row + 1):
            at = row - offset
            same = (doc_of(meta, first + at + jnp.zeros((1, 1), i32)) == here).astype(f32)
            edge = edge + conv_w[offset : offset + 1] * padded[at : at + 1] * same
        edges.append(edge)
    grad_ext[0:HALO] = jnp.concatenate(edges, axis=0)
    low_edge = grad_ext[0:HALO].astype(bf16)
    low_own = grad_ext[HALO : HALO + T].astype(bf16)
    values = tokens[...].astype(f32)
    upstream = mm_nt(low_own, w_in[:, :E]) + mm_nt(grad_gate[...], w_in[:, E:])
    back, gain_own = norm_back(values, inverse_rms(values), gain[...], upstream)
    grad_tokens[...] = grad_mid[...] + back
    before = halo[...].astype(f32)
    back, gain_edge = norm_back(before, inverse_rms(before), gain[...], mm_nt(low_edge, w_in[:, :E]))
    tail[...] = back[HALO - 8 : HALO]
    vec[KERNEL + 3 : KERNEL + 4, 0:D] = gain_own + gain_edge
    vec[KERNEL + 3 : KERNEL + 4, D:E] = g_gain_two[...]
    wide[R + N : R + 2 * N] = vec[...]
    for core in range(2):

        @pl.when(meta[2 + DOCS] == core)
        def _():
            for j in range(D // 128):
                cols = slice(core * D + j * 128, core * D + (j + 1) * 128)
                keep[0:HALO, j * 128 : (j + 1) * 128] = low_edge[:, cols]
                keep[HALO : HALO + T, j * 128 : (j + 1) * 128] = low_own[:, cols]
                cols = slice((1 - core) * D + j * 128, (1 - core) * D + (j + 1) * 128)
                base = j * (HALO + T)
                give[base : base + HALO] = low_edge[:, cols]
                give[base + HALO : base + HALO + T] = low_own[:, cols]
            base = D // 128 * (HALO + T)
            for j in range(E // 128):
                cols = slice(j * 128, (j + 1) * 128)
                mine, other = (gw_x, wide) if core == 0 else (wide, gw_x)
                part_keep[j * 64 : (j + 1) * 64] = mine[:, cols]
                give[base + j * 64 : base + (j + 1) * 64] = other[:, cols].astype(bf16)


def early_weights(meta, keep, got, out, both):
    both[0:T] = keep[...]
    both[T : 2 * T] = got[...]
    left_right = (((0, 1), (2, 3), (2, 4), (2, 5)), ((0, 2), (1, 2), (3, 4), (3, 5)))
    for core in range(2):

        @pl.when(meta[2 + DOCS] == core)
        def _():
            for j, (a, b) in enumerate(left_right[core]):
                left, right = both[:, a * D : (a + 1) * D], both[:, b * D : (b + 1) * D]
                result = mm_tn(left, right).astype(bf16)
                for q in range(D // LANES):
                    out[(4 * j + q) * D : (4 * j + q + 1) * D] = result[:, q * LANES : (q + 1) * LANES]


def late_weights(keep, part_keep, low_own, low_other, got, out, whole):
    left = jnp.concatenate([low_own[...], low_other[...]], axis=0)
    rows = HALO + T
    for j in range(D // LANES):
        right = jnp.concatenate([keep[:, j * LANES : (j + 1) * LANES], got[j * rows : (j + 1) * rows]], axis=0)
        whole[j * D : (j + 1) * D] = mm_tn(left, right)
    base = D // LANES * rows
    whole[4 * D : 5 * D] = part_keep[...] + got[base : base + D].astype(f32)
    for d in range(SHARES):
        main = whole[d * MAIN : (d + 1) * MAIN]
        small = whole[4 * D + d * SMALL : 4 * D + (d + 1) * SMALL]
        out[d] = jnp.concatenate([main, small], axis=0).astype(bf16)


def add_early(early, late, out):
    total = early[0].astype(f32)
    for j in range(1, SHARES):
        total = total + early[j].astype(f32)
    for j in range(SHARES):
        out[j] = jnp.concatenate([late[j].astype(f32), total], axis=0).astype(bf16)


def add_late(got, out, held, sem):
    copy = pltpu.make_async_copy(got.at[:, pl.ds(0, 3 * N)], held, sem)
    copy.start()
    copy.wait()
    total = held[0].astype(f32)[0:LATE]
    for j in range(1, SHARES):
        total = total + held[j].astype(f32)[0:LATE]
    low = total.astype(bf16)
    for j in range(SHARES):
        out[j] = low


def finish_early(meta, mine, other, gw_o, gw_q, gw_k, gw_v, gw_out, gw_in, gate, sem):
    is_zero = meta[2 + DOCS] == 0
    for d in reversed(range(SHARES)):
        a, b = mine[d].astype(f32)[LATE:], other[d].astype(f32)[LATE:]
        j, q, r = d // 16, d // 4 % 4, d % 4 * T
        tile = TILES[q]
        (gw_o, gw_q, gw_k, gw_v)[j][r : r + T, tile] = jnp.where(is_zero, a, b)
        one = jnp.where(is_zero, b, a)
        if j < 2:
            gw_out[j * D + r : j * D + r + T, tile] = one
        else:
            low = (j - 2) * D + q * LANES
            gate[r : r + T, low : low + LANES] = one
        if d == SHARES // 2:
            copy = pltpu.make_async_copy(gate, gw_in.at[:, pl.ds(E, E)], sem)
            copy.start()
    copy.wait()


def finish_late(
    meta, mine, other, _, gw_in, gw_x, gw_dt, g_a_log, g_conv_w, g_conv_b, g_dt_b, g_skip, g_gain_one,
    g_gain_two, conv, sems,
):
    is_zero = meta[2 + DOCS] == 0
    copies = []
    for d in range(SHARES):
        a, b = mine[d].astype(f32), other[d].astype(f32)
        zero = jnp.where(is_zero, a, b)
        one = jnp.where(is_zero, b, a)
        j, r = d // 16, d % 16 * MAIN
        conv[r : r + MAIN, j * LANES : (j + 1) * LANES] = zero[0:MAIN]
        conv[r : r + MAIN, D + j * LANES : D + (j + 1) * LANES] = one[0:MAIN]
        if d % 16 == 15:
            for side in range(2):
                cols = pl.ds(side * D + j * LANES, LANES)
                copies.append(pltpu.make_async_copy(conv.at[:, cols], gw_in.at[:, cols], sems.at[side, j]))
                copies[-1].start()
        q, r = d // 8, d % 8 * SMALL
        tile = TILES[q]
        gw_x[r : r + SMALL, tile] = zero[MAIN:]
        for out, low, high in ((gw_dt, 0, R), (g_a_log, R, R + N)):
            if low <= r < high:
                out[r - low : r - low + SMALL, tile] = one[MAIN:]
        if r == R + N:
            g_conv_w[:, tile] = one[MAIN : MAIN + KERNEL]
            at = MAIN + KERNEL
            for i, out in enumerate((g_conv_b, g_dt_b, g_skip)):
                out[:, tile] = one[at + i : at + i + 1]
            out = g_gain_one if q < 4 else g_gain_two
            out[:, TILES[q % 4]] = one[at + 3 : at + 4]
    for copy in copies:
        copy.wait()


MEGABYTES = dict(
    mamba_in=16, mamba_out=16, attention=16, middle_back=20, early_weights=12, mamba_back=38, late_weights=12,
    add_late=8, add_early=14, finish_early=24, finish_late=12,
)


def call(body, name, outs, scratch, *args, smem=True, outside=(), aliases=None, far=(), far_out=(), there=(), sems=()):
    aliases = aliases or {}
    args = [pltpu.with_memory_space_constraint(x, pltpu.HBM) if i in far else x for i, x in enumerate(args)]
    specs = [pl.BlockSpec(memory_space=pl.ANY if i in aliases or i in there else pltpu.VMEM) for i in range(len(args))]
    if smem:
        specs[0] = pl.BlockSpec(memory_space=pltpu.SMEM)
    return pl.pallas_call(
        body,
        name=name,
        out_shape=[pltpu.HBM(s, t) if i in far_out else jax.ShapeDtypeStruct(s, t) for i, (s, t) in enumerate(outs)],
        in_specs=specs,
        out_specs=[pl.BlockSpec(memory_space=pl.ANY if i in outside else pltpu.VMEM) for i in range(len(outs))],
        scratch_shapes=[pltpu.VMEM(s, t) for s, t in scratch]
        + [pltpu.SemaphoreType.DMA(n) for n in sems],
        input_output_aliases=aliases,
        compiler_params=pltpu.CompilerParams(vmem_limit_bytes=MEGABYTES[name] << 20),
    )(*args)


def shift(x, by):
    pairs = [(i, i + by) for i in range(BLOCKS) if 0 <= i + by < BLOCKS]
    return lax.ppermute(x, PLACE, pairs)


def swap(x):
    return lax.all_to_all(x, PLACE, 0, 0, tiled=True)


def partner(x):
    return lax.ppermute(x, "core", [(0, 1), (1, 0)])


def trade(x):
    return lax.all_to_all(x, SAME, 0, 0, tiled=True)


def layer(
    tokens, starts, gain_one, w_in, conv_w, conv_b, w_x, w_dt, dt_bias, a_log, d_skip, w_out,
    gain_two, w_q, w_k, w_v, w_o, cotangent,
):
    tokens, cot = tokens[0], cotangent[0]
    place = lax.axis_index(PLACE)
    core = lax.axis_index("core").astype(i32)
    meta = jnp.concatenate([jnp.stack([place * T, place]).astype(i32), starts[0], core[None]])
    row = lambda v: v.reshape(1, -1)
    halo = shift(tokens[T - HALO :], 1)
    tn = ((N, E), f32)
    te, tel, td, tdl = ((T, E), f32), ((T, E), bf16), ((T, D), f32), ((T, D), bf16)
    w_x = w_x.T
    send, grad_att, low_ext, ext, gate, conv, act, step, pre, bc, dt_low = call(
        mamba_in, "mamba_in",
        [((BLOCKS, SENT, LANES), bf16), tdl, ((HALO + T, D), bf16), ((HALO + T, E), bf16), tel, te, tel, te, te,
         ((T // STEPS, 2 * N, 128), f32), ((T, R), bf16)],
        [((HALO + T, E), f32), te, te, ((T, 128), f32), tn, tn],
        meta, tokens, halo, row(gain_one), w_in, conv_w, row(conv_b), w_x, w_dt, row(dt_bias), a_log, cot, w_o,
        far=(1, 3, 4, 5, 6, 7, 8, 9, 10, 11, 12), far_out=(2, 3, 5, 8, 10),
    )
    low_other = partner(low_ext)
    forward = swap(send)
    packed, start, ssm, gated, middle, normed = call(
        mamba_out, "mamba_out",
        [((BLOCKS, ROWS, 128), bf16), ((N, E), f32), te, tel, td, tdl],
        [te, te, te, tn],
        meta, forward, tokens, step, act, bc, gate, a_log, row(d_skip), w_out, row(gain_two),
        w_q, w_k, w_v, grad_att, far_out=(1,),
    )
    (back,) = call(
        attention, "attention",
        [((BLOCKS, ROWS, 128), bf16)],
        [((128, BLOCKS * T), bf16), ((BLOCKS, T, QCHUNK), f32), ((BLOCKS, T, QCHUNK), f32),
         ((BLOCKS, T, 128), f32)],
        meta, swap(packed),
    )
    wide = ((T, 6 * D), bf16)
    send, mixed, grad_mid, g, grad_gate, keep, give, g_gain_two, g_skip = call(
        middle_back, "middle_back",
        [((BLOCKS, N * 8, LANES), bf16), tdl, td, te, tel, wide, wide, ((1, D), f32), ((1, E), f32)],
        [tdl] * 4 + [te, tn, tdl, td, te, tel, wide],
        meta, swap(back), cot, middle, normed, low_ext, gated, gate, ssm, act, step, bc, a_log,
        row(d_skip), w_o, w_q, w_k, w_v, w_out, row(gain_two), far_out=(1, 2, 3, 4, 5, 7, 8),
        outside=(1, 2, 3, 4, 5), sems=((5,),),
    )
    (early,) = call(
        early_weights, "early_weights", [((16 * D, LANES), bf16)], [((2 * T, 6 * D), bf16)],
        meta, keep, partner(give), far=(1,),
    )
    early, behind, low_other = lax.optimization_barrier((early, swap(send), low_other))
    early = trade(early.reshape(SHARES, T, LANES))
    grad_tokens, tail, keep, give, part_keep = call(
        mamba_back, "mamba_back",
        [td, ((8, D), f32), ((HALO + T, D), bf16), ((4 * (HALO + T) + D, 128), bf16), ((D, 128), f32)],
        [te, te, ((T, N, E), f32), ((T, N, E), f32), te, te, ((HALO + T, E), f32),
         ((T + 8, E), f32), ((HALO + T, E), f32), ((N, E), f32), ((64, E), f32), tn, tn,
         ((T, N, LANES), f32), ((T, N, LANES), f32),
         te, ((T, R), bf16), te, ((HALO + T, E), bf16), ((64, E), bf16), ((R, E), bf16), tdl, ((D, 2 * E), bf16), tel, td],
        meta, behind, forward, start, g, act, step, pre, bc, dt_low, conv, ext, a_log,
        row(d_skip), conv_w, w_x, w_dt, tokens, halo, row(gain_one), w_in, grad_gate, grad_mid,
        g_gain_two, g_skip, far=tuple(range(1, 25)), far_out=(0, 1, 2, 4),
        there=(7, 9, 10, 11, 15, 16, 17, 20, 21, 22), sems=((10,),),
    )
    (late,) = call(
        late_weights, "late_weights", [((SHARES, LATE, LANES), bf16)], [((5 * D, LANES), f32)],
        keep, part_keep, low_ext, low_other, partner(give), smem=False, far=(0, 1, 2, 3), far_out=(0,),
    )
    (both,) = call(
        add_early, "add_early", [((SHARES, LATE + T, LANES), bf16)], [], early, late, smem=False,
        far=(1,), far_out=(0,),
    )
    shares = trade(both)
    (late,) = call(
        add_late, "add_late", [((SHARES, LATE, LANES), bf16)], [((SHARES, 3 * N, LANES), bf16)],
        shares, smem=False, far=(0,), there=(0,), sems=((),),
    )
    late = trade(late)
    gw_o, gw_q, gw_k, gw_v, gw_out, gw_in = call(
        finish_early, "finish_early",
        [((D, D), f32)] * 4 + [((E, D), f32), ((D, 2 * E), f32)], [((D, E), f32)],
        meta, shares, partner(shares), outside=(5,), far=(1, 2), sems=((),),
    )
    grad_tokens, gw_in = lax.optimization_barrier((grad_tokens, gw_in))
    grad_tokens = grad_tokens.at[T - 8 :].add(shift(tail, -1))
    late, gw_in, grad_tokens = lax.optimization_barrier((late, gw_in, grad_tokens))
    gw_in, gw_x, gw_dt, g_a_log, g_conv_w, g_conv_b, g_dt_b, g_skip, g_gain_one, g_gain_two = call(
        finish_late, "finish_late",
        [((D, 2 * E), f32), ((64, E), f32), ((R, E), f32), tn, ((KERNEL, E), f32), ((1, E), f32),
         ((1, E), f32), ((1, E), f32), ((1, D), f32), ((1, D), f32)],
        [((D, E), f32)],
        meta, late, partner(late), gw_in, outside=(0,), aliases={3: 0}, sems=((2, 4),),
    )
    return (
        mixed[None], grad_tokens[None], g_gain_one[0], gw_in, g_conv_w, g_conv_b[0], gw_x.T, gw_dt,
        g_dt_b[0], g_a_log, g_skip[0], gw_out, g_gain_two[0], gw_q, gw_k, gw_v, gw_o,
    )


def solution(mesh):
    rows, seq, head = mesh.devices.shape
    fine = Mesh(mesh.devices.reshape(rows // 2, 2, seq, head), ALL)
    split = P(("y", "core"), PLACE, None)
    return jax.shard_map(
        layer,
        mesh=fine,
        in_specs=(split, P(("y", "core"), None)) + (P(),) * 15 + (split,),
        out_specs=(split, split) + (P(),) * 15,
        check_vma=False,
    )
```

```python
import functools

import jax
import jax.numpy as jnp
from jax import lax
from jax.experimental import pallas as pl
from jax.experimental.pallas import tpu as pltpu
from jax.sharding import Mesh, PartitionSpec as P

T, D, E, N, R, HD = 128, 512, 1024, 16, 32, 64
HEADS, BLOCKS, HALF, DOCS, KERNEL, HALO = 8, 16, 64, 6, 4, 16
LANES, STEPS = 128, 8
TILES = [slice(q * LANES, (q + 1) * LANES) for q in range(E // LANES)]
ROWS = T + HALF
SENT = N * 8 + 16
RESET = 1e4
LOG2E = 1.4426950408889634
EPS = 1e-05
MASKED = -1e30
PLACE = ("seq", "head")
ALL = ("y", "core", "seq", "head")
SAME, SHARES, MAIN, SMALL, LATE = ("y", "seq", "head"), 64, 32, 8, 40
bf16, f32, i32 = jnp.bfloat16, jnp.float32, jnp.int32


def mm(a, b):
    return jnp.dot(a, b, preferred_element_type=f32)


def mm_nt(a, b):
    return lax.dot_general(a, b, (((1,), (1,)), ((), ())), preferred_element_type=f32)


def mm_tn(a, b):
    return lax.dot_general(a, b, (((0,), (0,)), ((), ())), preferred_element_type=f32)


def doc_of(meta, pos):
    count = jnp.zeros(pos.shape, i32)
    for k in range(DOCS):
        count = count + (meta[2 + k] <= pos).astype(i32)
    return count


def reset_of(meta, pos):
    hit = meta[2] == pos
    for k in range(1, DOCS):
        hit = hit | (meta[2 + k] == pos)
    return jnp.where(hit, RESET, 0.0)


def inverse_rms(x):
    return lax.rsqrt(jnp.mean(x * x, axis=-1, keepdims=True) + EPS)


def sigmoid(x):
    return 1.0 / (1.0 + jnp.exp(-x))


def silu_slope(x):
    s = sigmoid(x)
    return s * (1.0 + x * (1.0 - s))


def norm_back(values, inverse, gain, upstream):
    scaled = upstream * gain
    inner = jnp.mean(values * scaled, axis=-1, keepdims=True)
    back = inverse * scaled - values * (inverse * inverse * inverse) * inner
    return back, jnp.sum(upstream * values * inverse, axis=0, keepdims=True)


def columns(offset, meta):
    first = meta[0]
    return first + offset + lax.broadcasted_iota(i32, (T, 1), 0)


def stack_sums(parts):
    row = lax.broadcasted_iota(i32, parts[0].shape, 0)
    for by in (1, 2, 4):
        first = (row & by) == 0
        parts = [
            jnp.where(first, a, b) + pltpu.roll(jnp.where(first, b, a), by, axis=0)
            for a, b in zip(parts[0::2], parts[1::2])
        ]
    return parts[0]


def column(block, low, k):
    return jnp.broadcast_to(block[low : low + N, k : k + 1], (N, LANES))


def halves(x):
    return x[0:8] + x[8:16]


def scan_forward(dec, sa, bc, rates2, start, result=None):
    def block(i, states):
        states = list(states)
        base = pl.multiple_of(i * STEPS, STEPS)
        cols = bc[i]
        sums = [[None] * STEPS for _ in TILES]
        for k in range(STEPS):
            b_col = column(cols, 0, k)
            c_col = column(cols, N, k)
            for q, tile in enumerate(TILES):
                factor = jnp.exp2(dec[pl.ds(base, STEPS), tile][k : k + 1] * rates2[:, tile])
                states[q] = factor * states[q] + b_col * sa[pl.ds(base, STEPS), tile][k : k + 1]
                if result is not None:
                    sums[q][k] = halves(states[q] * c_col)
        if result is not None:
            for q, tile in enumerate(TILES):
                result[pl.ds(base, STEPS), tile] = stack_sums(sums[q])
        return tuple(states)

    return lax.fori_loop(0, T // STEPS, block, tuple(start[:, tile] for tile in TILES))


def mamba_in(
    meta, tokens, halo, gain, w_in, conv_w, conv_b, w_x, w_dt, dt_b, a_log, cot, w_o,
    send, grad_att, low_out, ext_out, gate_out, conv_out, act_out, step_out, pre_out, bc_out, dt_out,
    ext, dec, sa, xp, rates2, zero,
):
    grad_att[...] = mm_nt(cot[...], w_o[...]).astype(bf16)
    own = tokens[...].astype(f32)
    before = halo[...].astype(f32)
    low_own = (own * inverse_rms(own) * gain[...]).astype(bf16)
    low_before = (before * inverse_rms(before) * gain[...]).astype(bf16)
    conv_own = mm(low_own, w_in[:, :E]).astype(bf16)
    conv_before = mm(low_before, w_in[:, :E]).astype(bf16)
    low_out[0:HALO] = low_before
    low_out[HALO : HALO + T] = low_own
    ext_out[0:HALO] = conv_before
    ext_out[HALO : HALO + T] = conv_own
    ext[0:HALO] = conv_before.astype(f32)
    ext[HALO : HALO + T] = conv_own.astype(f32)
    gate_out[...] = mm(low_own, w_in[:, E:]).astype(bf16)
    own_doc = doc_of(meta, columns(0, meta))
    conv = jnp.broadcast_to(conv_b[...], (T, E))
    for offset in range(KERNEL):
        same = (doc_of(meta, columns(offset - KERNEL + 1, meta)) == own_doc).astype(f32)
        low = HALO - KERNEL + 1 + offset
        conv = conv + conv_w[offset : offset + 1] * ext[low : low + T] * same
    conv_out[...] = conv
    act = (conv * sigmoid(conv)).astype(bf16)
    act_out[...] = act
    proj = mm_nt(act, w_x[...])
    dt_low = proj[:, :R].astype(bf16)
    dt_out[...] = dt_low
    pre = mm(dt_low, w_dt[...]) + dt_b[...]
    pre_out[...] = pre
    step = jnp.maximum(pre, 0.0) + jnp.log1p(jnp.exp(-jnp.abs(pre)))
    step_out[...] = step
    held = step + reset_of(meta, columns(0, meta))
    dec[...] = held
    sa[...] = step * act.astype(f32)
    xp[...] = jnp.zeros((T, 128), f32)
    xp[:, 0 : R + 2 * N] = proj
    turned = xp[...].T
    for i in range(T // STEPS):
        bc_out[i, :, 0:STEPS] = turned[R : R + 2 * N, i * STEPS : (i + 1) * STEPS]
    total = jnp.sum(held, axis=0, keepdims=True)
    high = total.astype(bf16)
    rest = (total - high.astype(f32)).astype(bf16)
    rates2[...] = -jnp.exp(a_log[...]) * LOG2E
    zero[...] = jnp.zeros((N, E), f32)
    states = scan_forward(dec, sa, bc_out, rates2, zero)
    sums = [high[:, tile].astype(f32) for tile in TILES] + [rest[:, tile].astype(f32) for tile in TILES]
    ended = jnp.concatenate(list(states) + sums, axis=0).astype(bf16)
    for j in range(BLOCKS):
        send[j] = ended


def joined(blocks, first, last, ends, rates2):
    def join(turn, states):
        sent = blocks[first(turn)].astype(f32)
        own = sent if ends is None else ends[first(turn)].astype(f32)
        total = sent[N * 8 : N * 8 + 8] + sent[N * 8 + 8 : N * 8 + 16]
        return tuple(
            jnp.exp2(rates2[:, tile] * total[q : q + 1]) * states[q] + own[q * N : (q + 1) * N]
            for q, tile in enumerate(TILES)
        )

    return lax.fori_loop(0, last, join, tuple(jnp.zeros((N, LANES), f32) for _ in TILES))


def roll_half(x):
    return pltpu.roll(x, HALF, axis=1)


def mamba_out(
    meta, got, tokens, step, act, bc, gate, a_log, d_skip, w_out, gain, w_q, w_k, w_v, grad_att,
    send, start_out, ssm_out, gated_out, middle_out, normed_out,
    dec, sa, ssm, rates2,
):
    place = meta[1]
    rates2[...] = -jnp.exp(a_log[...]) * LOG2E
    dec[...] = step[...] + reset_of(meta, columns(0, meta))
    act_f = act[...].astype(f32)
    sa[...] = step[...] * act_f
    for tile, state in zip(TILES, joined(got, lambda turn: turn, place, None, rates2)):
        start_out[:, tile] = state
    scan_forward(dec, sa, bc, rates2, start_out, ssm)
    result = ssm[...] + d_skip[...] * act_f
    ssm_out[...] = result
    gates = gate[...].astype(f32)
    gated = (result * (gates * sigmoid(gates))).astype(bf16)
    gated_out[...] = gated
    middle = tokens[...].astype(f32) + mm(gated, w_out[...])
    middle_out[...] = middle
    normed = (middle * inverse_rms(middle) * gain[...]).astype(bf16)
    normed_out[...] = normed
    queries = mm(normed, w_q[...]).astype(bf16).astype(f32) * (HD ** -0.5)
    keys = mm(normed, w_k[...])
    vals = mm(normed, w_v[...])
    grads = grad_att[...].astype(f32)
    low = lax.broadcasted_iota(i32, (T, 128), 1) < HALF
    for m in range(HEADS // 2):
        tile = slice(m * 128, (m + 1) * 128)
        for odd in range(2):
            for first, second, at, rows in ((keys, vals, 0, T), (queries, grads, T, HALF)):
                a, b = first[:, tile], second[:, tile]
                pair = jnp.where(low, a, roll_half(b)) if odd == 0 else jnp.where(low, roll_half(a), b)
                pair = pair.astype(bf16)
                dest = 2 * (2 * m + odd)
                if rows == T:
                    send[dest, 0:T] = pair
                    send[dest + 1, 0:T] = pair
                else:
                    send[dest, T:ROWS] = pair[0:HALF]
                    send[dest + 1, T:ROWS] = pair[HALF:T]


QCHUNK, QBLOCKS = 256, 4


def attention(meta, got, send, kv_t, scores, grads, kv_grad):
    parity = lax.rem(meta[1], 2)
    for i in range(BLOCKS):
        kv_t[:, i * T : (i + 1) * T] = got[i, 0:T].astype(f32).T.astype(bf16)
    lane = lax.broadcasted_iota(i32, (1, QCHUNK), 1)
    low_q = lax.broadcasted_iota(i32, (QCHUNK, 128), 1) < HD
    low_k = lax.broadcasted_iota(i32, (T, 128), 1) < HD
    key_row = lax.broadcasted_iota(i32, (T, QCHUNK), 0)
    for c in range(BLOCKS // QBLOCKS):
        qg = jnp.concatenate([got[c * QBLOCKS + b, T:ROWS] for b in range(QBLOCKS)], axis=0)
        q_only = jnp.where(low_q, qg.astype(f32), 0.0).astype(bf16)
        g_only = jnp.where(low_q, 0.0, qg.astype(f32)).astype(bf16)
        pos = (c * QBLOCKS + lane // HALF) * T + parity * HALF + lane % HALF
        begin = jnp.zeros((1, QCHUNK), i32)
        for k in range(DOCS):
            begin = jnp.maximum(begin, jnp.where(meta[2 + k] <= pos, meta[2 + k], 0))
        tiles = (c + 1) * QBLOCKS
        top = jnp.full((8, QCHUNK), MASKED, f32)
        for i in range(tiles):
            s = mm_nt(got[i, 0:T], q_only)
            allowed = key_row >= begin - i * T
            if i >= c * QBLOCKS:
                allowed = allowed & (key_row <= pos - i * T)
            s = jnp.where(allowed, s, MASKED)
            scores[i] = s
            top = jnp.maximum(top, jnp.max(s.reshape(T // 8, 8, QCHUNK), axis=0))
        top = jnp.max(top, axis=0, keepdims=True)
        total = jnp.zeros((8, QCHUNK), f32)
        cross = jnp.zeros((8, QCHUNK), f32)
        for i in range(tiles):
            p = jnp.exp2((scores[i] - top) * LOG2E)
            scores[i] = p
            g = mm_nt(got[i, 0:T], g_only)
            grads[i] = g
            total = total + jnp.sum(p.reshape(T // 8, 8, QCHUNK), axis=0)
            cross = cross + jnp.sum((p * g).reshape(T // 8, 8, QCHUNK), axis=0)
        inverse = 1.0 / jnp.sum(total, axis=0, keepdims=True)
        cross = jnp.sum(cross, axis=0, keepdims=True) * inverse
        out_t = jnp.zeros((128, QCHUNK), f32)
        dq_t = jnp.zeros((128, QCHUNK), f32)
        for i in range(tiles):
            prob = scores[i] * inverse
            low_p = prob.astype(bf16)
            low_s = (prob * (grads[i] - cross)).astype(bf16)
            turned = kv_t[:, i * T : (i + 1) * T]
            out_t = out_t + mm(turned, low_p)
            dq_t = dq_t + mm(turned, low_s)
            both = jnp.where(low_k, mm(low_s, qg), mm(low_p, qg))
            if i >= c * QBLOCKS:
                kv_grad[i] = both
            else:
                kv_grad[i] = kv_grad[i] + both
        pair = jnp.where(low_q, dq_t.T * (HD ** -0.5), out_t.T).astype(bf16)
        for b in range(QBLOCKS):
            send[c * QBLOCKS + b, T:ROWS] = pair[b * HALF : (b + 1) * HALF]
    for i in range(BLOCKS):
        send[i, 0:T] = kv_grad[i].astype(bf16)


def middle_back(
    meta, got, cot, middle, normed, low_ext, gated, gate, ssm, act, step, bc, a_log, d_skip,
    w_o, w_q, w_k, w_v, w_out, gain,
    send, mixed_far, grad_mid_far, g_far, grad_gate_far, keep_far, give, g_gain, g_skip,
    att, dq, dk, dv, dec, rates2, mixed, grad_mid_out, g_out, grad_gate_out, keep, sems,
):
    low = lax.broadcasted_iota(i32, (HALF, 128), 1) < HALF
    low_t = lax.broadcasted_iota(i32, (T, 128), 1) < HALF
    for m in range(HEADS // 2):
        tile = slice(m * 128, (m + 1) * 128)
        for p in range(2):
            a = got[4 * m + p, T:ROWS].astype(f32)
            b = got[4 * m + 2 + p, T:ROWS].astype(f32)
            rows = slice(p * HALF, (p + 1) * HALF)
            dq[rows, tile] = jnp.where(low, a, roll_half(b)).astype(bf16)
            att[rows, tile] = jnp.where(low, roll_half(a), b).astype(bf16)
        a = got[4 * m, 0:T].astype(f32) + got[4 * m + 1, 0:T].astype(f32)
        b = got[4 * m + 2, 0:T].astype(f32) + got[4 * m + 3, 0:T].astype(f32)
        dk[:, tile] = jnp.where(low_t, a, roll_half(b)).astype(bf16)
        dv[:, tile] = jnp.where(low_t, roll_half(a), b).astype(bf16)
    cot_low = cot[...]
    values = middle[...]
    mixed[...] = (values + mm(att[...], w_o[...])).astype(bf16)
    upstream = mm_nt(dq[...], w_q[...]) + mm_nt(dk[...], w_k[...]) + mm_nt(dv[...], w_v[...])
    back, gain_grad = norm_back(values, inverse_rms(values), gain[...], upstream)
    g_gain[...] = gain_grad
    grad_mid = cot_low.astype(f32) + back
    grad_mid_out[...] = grad_mid
    mid_low = grad_mid.astype(bf16)
    grad_gated = mm_nt(mid_low, w_out[...]).astype(bf16).astype(f32)
    gates = gate[...].astype(f32)
    sig = sigmoid(gates)
    g = grad_gated * (gates * sig)
    g_out[...] = g
    grad_gate = (grad_gated * ssm[...] * (sig * (1.0 + gates * (1.0 - sig)))).astype(bf16)
    grad_gate_out[...] = grad_gate
    for first, second, core in ((keep, give, 0), (give, keep, 1)):

        @pl.when(meta[2 + DOCS] == core)
        def _():
            first[:, 0:D] = att[...]
            first[:, D : 2 * D] = cot_low
            first[:, 2 * D : 3 * D] = normed[...]
            first[:, 3 * D : 4 * D] = dq[...]
            first[:, 4 * D : 5 * D] = dk[...]
            first[:, 5 * D : 6 * D] = dv[...]
            second[:, 0:E] = gated[...]
            second[:, E : E + D] = mid_low
            second[:, E + D : 2 * E] = low_ext[HALO : HALO + T]
            second[:, 2 * E : 3 * E] = grad_gate

    g_skip[...] = jnp.sum(g * act[...].astype(f32), axis=0, keepdims=True)
    saves = [
        pltpu.make_async_copy(held, place, sems.at[i])
        for i, (held, place) in enumerate(
            ((mixed, mixed_far), (grad_mid_out, grad_mid_far), (g_out, g_far), (grad_gate_out, grad_gate_far), (keep, keep_far))
        )
    ]
    for save in saves:
        save.start()
    dec[...] = step[...] + reset_of(meta, columns(0, meta))
    rates2[...] = -jnp.exp(a_log[...]) * LOG2E

    def block(turn, carry):
        carry = list(carry)
        i = T // STEPS - 1 - turn
        base = pl.multiple_of(i * STEPS, STEPS)
        cols = bc[i]
        for k in reversed(range(STEPS)):
            c_col = column(cols, N, k)
            for q, tile in enumerate(TILES):
                factor = jnp.exp2(dec[pl.ds(base, STEPS), tile][k : k + 1] * rates2[:, tile])
                carry[q] = factor * (carry[q] + c_col * g_out[pl.ds(base, STEPS), tile][k : k + 1])
        return tuple(carry)

    carry = lax.fori_loop(0, T // STEPS, block, tuple(jnp.zeros((N, LANES), f32) for _ in TILES))
    ended = jnp.concatenate(carry, axis=0).astype(bf16)
    for j in range(BLOCKS):
        send[j] = ended
    for save in saves:
        save.wait()


def mamba_back(
    meta, got, forward, start, g, act, step, pre_far, bc, dt_low_far, conv_far, ext_low_far, a_log, d_skip,
    conv_w, w_x_far, w_dt_far, tokens_far, halo, gain, w_in_far, grad_gate_far, grad_mid_far, g_gain_two, g_skip,
    grad_tokens, tail, keep, give, part_keep,
    dec, sa, decay, kept, gs, ab, ext, padded, grad_ext, vec, wide, rates, rates2, sum_b, sum_c,
    pre, dt_low, conv, ext_low, w_x, w_dt, tokens, w_in, grad_gate, grad_mid, sems,
):
    place = meta[1]
    loads = [
        pltpu.make_async_copy(source, held, sems.at[i])
        for i, (source, held) in enumerate(
            ((pre_far, pre), (dt_low_far, dt_low), (conv_far, conv), (ext_low_far, ext_low), (w_x_far, w_x), (w_dt_far, w_dt), (tokens_far, tokens), (w_in_far, w_in), (grad_gate_far, grad_gate), (grad_mid_far, grad_mid))
        )
    ]
    for load in loads:
        load.start()
    dec[...] = step[...] + reset_of(meta, columns(0, meta))
    act_f = act[...].astype(f32)
    sa[...] = step[...] * act_f
    rates[...] = -jnp.exp(a_log[...])
    rates2[...] = rates[...] * LOG2E

    ahead_carry = joined(forward, lambda turn: BLOCKS - 1 - turn, BLOCKS - 1 - place, got, rates2)
    for tile, state in zip(TILES, ahead_carry):
        wide[R : R + N, tile] = state

    def ahead(i, states):
        states = list(states)
        base = pl.multiple_of(i * STEPS, STEPS)
        cols = bc[i]
        for k in range(STEPS):
            b_col = column(cols, 0, k)
            total = jnp.zeros((N, LANES), f32)
            for q, tile in enumerate(TILES):
                rows = pl.ds(base, STEPS), tile
                factor = jnp.exp2(dec[rows][k : k + 1] * rates2[:, tile])
                moved = factor * states[q]
                decay[base + k, :, tile] = factor
                kept[base + k, :, tile] = moved
                states[q] = moved + b_col * sa[rows][k : k + 1]
                total = total + states[q] * g[rows][k : k + 1]
            sum_c[base + k] = total
        return tuple(states)

    lax.fori_loop(0, T // STEPS, ahead, tuple(start[:, tile] for tile in TILES))
    first_carry = tuple(wide[R : R + N, tile] for tile in TILES)
    wide[R + N : R + 2 * N] = jnp.zeros((N, E), f32)

    def behind(turn, carry):
        carry = list(carry)
        i = T // STEPS - 1 - turn
        base = pl.multiple_of(i * STEPS, STEPS)
        cols = bc[i]
        by_rate = [[None] * STEPS for _ in TILES]
        by_b = [[None] * STEPS for _ in TILES]
        along = [wide[R + N : R + 2 * N, tile] for tile in TILES]
        for k in reversed(range(STEPS)):
            b_col = column(cols, 0, k)
            c_col = column(cols, N, k)
            total = jnp.zeros((N, LANES), f32)
            for q, tile in enumerate(TILES):
                rows = pl.ds(base, STEPS), tile
                adjoint = g[rows][k : k + 1] * c_col + carry[q]
                carry[q] = decay[base + k, :, tile] * adjoint
                log_grad = adjoint * kept[base + k, :, tile]
                along[q] = along[q] + log_grad * step[rows][k : k + 1]
                by_rate[q][k] = halves(log_grad * rates[:, tile])
                by_b[q][k] = halves(adjoint * b_col)
                total = total + adjoint * sa[rows][k : k + 1]
            sum_b[base + k] = total
        for q, tile in enumerate(TILES):
            wide[R + N : R + 2 * N, tile] = along[q]
            gs[pl.ds(base, STEPS), tile] = stack_sums(by_rate[q])
            ab[pl.ds(base, STEPS), tile] = stack_sums(by_b[q])
        return tuple(carry)

    lax.fori_loop(0, T // STEPS, behind, first_carry)
    wide[R : R + N] = wide[R + N : R + 2 * N] * rates[...]
    lane = lax.broadcasted_iota(i32, (LANES, LANES), 1)
    turned = jnp.zeros((T, LANES), f32)
    for at, sums in ((0, sum_b), (N, sum_c)):
        for n in range(N):
            one = (lane == at + n).astype(f32).astype(bf16)
            values = sums[:, n, :]
            high = values.astype(bf16)
            turned = turned + mm(high, one) + mm((values - high.astype(f32)).astype(bf16), one)
    for load in loads:
        load.wait()
    adjoint_b = ab[...]
    grad_step = gs[...] + adjoint_b * act_f
    grad_act = g[...] * d_skip[...] + adjoint_b * step[...]
    grad_pre = (grad_step * sigmoid(pre[...])).astype(bf16)
    vec[...] = jnp.zeros((N, E), f32)
    vec[KERNEL + 1 : KERNEL + 2] = jnp.sum(grad_pre.astype(f32), axis=0, keepdims=True)
    vec[KERNEL + 2 : KERNEL + 3] = g_skip[...]
    wide[0:R] = mm_tn(dt_low[...], grad_pre)
    grad_proj = jnp.concatenate([mm_nt(grad_pre, w_dt[...]), turned[:, 0 : 2 * N]], axis=1).astype(bf16)
    gw_x = mm_tn(grad_proj, act[...])
    grad_act = grad_act + mm(grad_proj, w_x[...])
    grad_conv = grad_act * silu_slope(conv[...])
    vec[KERNEL : KERNEL + 1] = jnp.sum(grad_conv, axis=0, keepdims=True)
    padded[0:T] = grad_conv
    padded[T : T + 8] = jnp.zeros((8, E), f32)
    ext[...] = ext_low[...].astype(f32)
    own_doc = doc_of(meta, columns(0, meta))
    own = jnp.zeros((T, E), f32)
    lift = KERNEL - 1
    rows = lax.broadcasted_iota(i32, (T, 1), 0)
    for offset in range(KERNEL):
        same = (doc_of(meta, columns(offset - lift, meta)) == own_doc).astype(f32)
        low = HALO - lift + offset
        vec[offset : offset + 1] = jnp.sum(grad_conv * ext[low : low + T] * same, axis=0, keepdims=True)
        up = lift - offset
        ahead_same = (doc_of(meta, columns(0, meta)) == doc_of(meta, columns(up, meta))) & (rows < T - up)
        own = own + conv_w[offset : offset + 1] * padded[up : up + T] * ahead_same.astype(f32)
    grad_ext[HALO : HALO + T] = own
    first = meta[0]
    edges = [jnp.zeros((HALO - lift, E), f32)]
    for row in range(lift):
        edge = jnp.zeros((1, E), f32)
        here = doc_of(meta, first - lift + row + jnp.zeros((1, 1), i32))
        for offset in range(row + 1):
            at = row - offset
            same = (doc_of(meta, first + at + jnp.zeros((1, 1), i32)) == here).astype(f32)
            edge = edge + conv_w[offset : offset + 1] * padded[at : at + 1] * same
        edges.append(edge)
    grad_ext[0:HALO] = jnp.concatenate(edges, axis=0)
    low_edge = grad_ext[0:HALO].astype(bf16)
    low_own = grad_ext[HALO : HALO + T].astype(bf16)
    values = tokens[...].astype(f32)
    upstream = mm_nt(low_own, w_in[:, :E]) + mm_nt(grad_gate[...], w_in[:, E:])
    back, gain_own = norm_back(values, inverse_rms(values), gain[...], upstream)
    grad_tokens[...] = grad_mid[...] + back
    before = halo[...].astype(f32)
    back, gain_edge = norm_back(before, inverse_rms(before), gain[...], mm_nt(low_edge, w_in[:, :E]))
    tail[...] = back[HALO - 8 : HALO]
    vec[KERNEL + 3 : KERNEL + 4, 0:D] = gain_own + gain_edge
    vec[KERNEL + 3 : KERNEL + 4, D:E] = g_gain_two[...]
    wide[R + N : R + 2 * N] = vec[...]
    for core in range(2):

        @pl.when(meta[2 + DOCS] == core)
        def _():
            for j in range(D // 128):
                cols = slice(core * D + j * 128, core * D + (j + 1) * 128)
                keep[0:HALO, j * 128 : (j + 1) * 128] = low_edge[:, cols]
                keep[HALO : HALO + T, j * 128 : (j + 1) * 128] = low_own[:, cols]
                cols = slice((1 - core) * D + j * 128, (1 - core) * D + (j + 1) * 128)
                base = j * (HALO + T)
                give[base : base + HALO] = low_edge[:, cols]
                give[base + HALO : base + HALO + T] = low_own[:, cols]
            base = D // 128 * (HALO + T)
            for j in range(E // 128):
                cols = slice(j * 128, (j + 1) * 128)
                mine, other = (gw_x, wide) if core == 0 else (wide, gw_x)
                part_keep[j * 64 : (j + 1) * 64] = mine[:, cols]
                give[base + j * 64 : base + (j + 1) * 64] = other[:, cols].astype(bf16)


def early_weights(meta, keep, got, out, both):
    both[0:T] = keep[...]
    both[T : 2 * T] = got[...]
    left_right = (((0, 1), (2, 3), (2, 4), (2, 5)), ((0, 2), (1, 2), (3, 4), (3, 5)))
    for core in range(2):

        @pl.when(meta[2 + DOCS] == core)
        def _():
            for j, (a, b) in enumerate(left_right[core]):
                left, right = both[:, a * D : (a + 1) * D], both[:, b * D : (b + 1) * D]
                result = mm_tn(left, right).astype(bf16)
                for q in range(D // LANES):
                    out[(4 * j + q) * D : (4 * j + q + 1) * D] = result[:, q * LANES : (q + 1) * LANES]


def late_weights(keep, part_keep, low_own, low_other, got, out, whole):
    left = jnp.concatenate([low_own[...], low_other[...]], axis=0)
    rows = HALO + T
    for j in range(D // LANES):
        right = jnp.concatenate([keep[:, j * LANES : (j + 1) * LANES], got[j * rows : (j + 1) * rows]], axis=0)
        whole[j * D : (j + 1) * D] = mm_tn(left, right)
    base = D // LANES * rows
    whole[4 * D : 5 * D] = part_keep[...] + got[base : base + D].astype(f32)
    for d in range(SHARES):
        main = whole[d * MAIN : (d + 1) * MAIN]
        small = whole[4 * D + d * SMALL : 4 * D + (d + 1) * SMALL]
        out[d] = jnp.concatenate([main, small], axis=0).astype(bf16)


def add_early(early, late, out, held, sems):
    total = early[0].astype(f32)
    for j in range(1, SHARES):
        total = total + early[j].astype(f32)
    copies = []
    for j in range(SHARES):
        held[j] = jnp.concatenate([late[j].astype(f32), total], axis=0).astype(bf16)
        if j % BLOCKS == BLOCKS - 1:
            part = pl.ds(j + 1 - BLOCKS, BLOCKS)
            copies.append(pltpu.make_async_copy(held.at[part], out.at[part], sems.at[j // BLOCKS]))
            copies[-1].start()
    for copy in copies:
        copy.wait()


def add_late(got, out, held, sem):
    copy = pltpu.make_async_copy(got.at[:, pl.ds(0, 3 * N)], held, sem)
    copy.start()
    copy.wait()
    total = held[0].astype(f32)[0:LATE]
    for j in range(1, SHARES):
        total = total + held[j].astype(f32)[0:LATE]
    low = total.astype(bf16)
    for j in range(SHARES):
        out[j] = low


def finish_early(meta, mine, other, gw_o, gw_q, gw_k, gw_v, gw_out, gw_in, gate, sem):
    is_zero = meta[2 + DOCS] == 0
    for d in reversed(range(SHARES)):
        a, b = mine[d].astype(f32)[LATE:], other[d].astype(f32)[LATE:]
        j, q, r = d // 16, d // 4 % 4, d % 4 * T
        tile = TILES[q]
        (gw_o, gw_q, gw_k, gw_v)[j][r : r + T, tile] = jnp.where(is_zero, a, b)
        one = jnp.where(is_zero, b, a)
        if j < 2:
            gw_out[j * D + r : j * D + r + T, tile] = one
        else:
            low = (j - 2) * D + q * LANES
            gate[r : r + T, low : low + LANES] = one
        if d == SHARES // 2:
            copy = pltpu.make_async_copy(gate, gw_in.at[:, pl.ds(E, E)], sem)
            copy.start()
    copy.wait()


def finish_late(
    meta, mine, other, _, gw_in, gw_x_far, gw_dt_far, g_a_log_far, g_conv_w_far, g_conv_b_far,
    g_dt_b_far, g_skip_far, g_gain_one_far, g_gain_two_far,
    conv, gw_x, gw_dt, g_a_log, g_conv_w, g_conv_b, g_dt_b, g_skip, g_gain_one, g_gain_two, sems,
):
    is_zero = meta[2 + DOCS] == 0
    copies = []
    for d in range(SHARES):
        a, b = mine[d].astype(f32), other[d].astype(f32)
        zero = jnp.where(is_zero, a, b)
        one = jnp.where(is_zero, b, a)
        j, r = d // 16, d % 16 * MAIN
        conv[r : r + MAIN, j * LANES : (j + 1) * LANES] = zero[0:MAIN]
        conv[r : r + MAIN, D + j * LANES : D + (j + 1) * LANES] = one[0:MAIN]
        if d % 16 == 15:
            for side in range(2):
                cols = pl.ds(side * D + j * LANES, LANES)
                copies.append(pltpu.make_async_copy(conv.at[:, cols], gw_in.at[:, cols], sems.at[side, j]))
                copies[-1].start()
        q, r = d // 8, d % 8 * SMALL
        tile = TILES[q]
        gw_x[r : r + SMALL, tile] = zero[MAIN:]
        for out, low, high in ((gw_dt, 0, R), (g_a_log, R, R + N)):
            if low <= r < high:
                out[r - low : r - low + SMALL, tile] = one[MAIN:]
        if r == R + N:
            g_conv_w[:, tile] = one[MAIN : MAIN + KERNEL]
            at = MAIN + KERNEL
            for i, out in enumerate((g_conv_b, g_dt_b, g_skip)):
                out[:, tile] = one[at + i : at + i + 1]
            out = g_gain_one if q < 4 else g_gain_two
            out[:, TILES[q % 4]] = one[at + 3 : at + 4]
    smalls = (
        (gw_x, gw_x_far),
        (gw_dt, gw_dt_far),
        (g_a_log, g_a_log_far),
        (g_conv_w, g_conv_w_far),
        (g_conv_b, g_conv_b_far),
        (g_dt_b, g_dt_b_far),
        (g_skip, g_skip_far),
        (g_gain_one, g_gain_one_far),
        (g_gain_two, g_gain_two_far),
    )
    for i, (held, place) in enumerate(smalls):
        copies.append(pltpu.make_async_copy(held, place, sems.at[2 + i // 4, i % 4]))
        copies[-1].start()
    for copy in copies:
        copy.wait()


MEGABYTES = dict(
    mamba_in=16, mamba_out=16, attention=16, middle_back=20, early_weights=12, mamba_back=38, late_weights=12,
    add_late=8, add_early=14, finish_early=24, finish_late=12,
)


def call(body, name, outs, scratch, *args, smem=True, outside=(), aliases=None, far=(), far_out=(), there=(), sems=()):
    aliases = aliases or {}
    args = [pltpu.with_memory_space_constraint(x, pltpu.HBM) if i in far else x for i, x in enumerate(args)]
    specs = [pl.BlockSpec(memory_space=pl.ANY if i in aliases or i in there else pltpu.VMEM) for i in range(len(args))]
    if smem:
        specs[0] = pl.BlockSpec(memory_space=pltpu.SMEM)
    return pl.pallas_call(
        body,
        name=name,
        out_shape=[pltpu.HBM(s, t) if i in far_out else jax.ShapeDtypeStruct(s, t) for i, (s, t) in enumerate(outs)],
        in_specs=specs,
        out_specs=[pl.BlockSpec(memory_space=pl.ANY if i in outside else pltpu.VMEM) for i in range(len(outs))],
        scratch_shapes=[pltpu.VMEM(s, t) for s, t in scratch]
        + [pltpu.SemaphoreType.DMA(n) for n in sems],
        input_output_aliases=aliases,
        compiler_params=pltpu.CompilerParams(vmem_limit_bytes=MEGABYTES[name] << 20),
    )(*args)


def shift(x, by):
    pairs = [(i, i + by) for i in range(BLOCKS) if 0 <= i + by < BLOCKS]
    return lax.ppermute(x, PLACE, pairs)


def swap(x):
    return lax.all_to_all(x, PLACE, 0, 0, tiled=True)


def partner(x):
    return lax.ppermute(x, "core", [(0, 1), (1, 0)])


def trade(x):
    return lax.all_to_all(x, SAME, 0, 0, tiled=True)


def layer(
    tokens, starts, gain_one, w_in, conv_w, conv_b, w_x, w_dt, dt_bias, a_log, d_skip, w_out,
    gain_two, w_q, w_k, w_v, w_o, cotangent,
):
    tokens, cot = tokens[0], cotangent[0]
    place = lax.axis_index(PLACE)
    core = lax.axis_index("core").astype(i32)
    meta = jnp.concatenate([jnp.stack([place * T, place]).astype(i32), starts[0], core[None]])
    row = lambda v: v.reshape(1, -1)
    halo = shift(tokens[T - HALO :], 1)
    tn = ((N, E), f32)
    te, tel, td, tdl = ((T, E), f32), ((T, E), bf16), ((T, D), f32), ((T, D), bf16)
    w_x = w_x.T
    send, grad_att, low_ext, ext, gate, conv, act, step, pre, bc, dt_low = call(
        mamba_in, "mamba_in",
        [((BLOCKS, SENT, LANES), bf16), tdl, ((HALO + T, D), bf16), ((HALO + T, E), bf16), tel, te, tel, te, te,
         ((T // STEPS, 2 * N, 128), f32), ((T, R), bf16)],
        [((HALO + T, E), f32), te, te, ((T, 128), f32), tn, tn],
        meta, tokens, halo, row(gain_one), w_in, conv_w, row(conv_b), w_x, w_dt, row(dt_bias), a_log, cot, w_o,
        far=(1, 3, 4, 5, 6, 7, 8, 9, 10, 11, 12), far_out=(2, 3, 5, 8, 10),
    )
    low_other = partner(low_ext)
    forward = swap(send)
    packed, start, ssm, gated, middle, normed = call(
        mamba_out, "mamba_out",
        [((BLOCKS, ROWS, 128), bf16), ((N, E), f32), te, tel, td, tdl],
        [te, te, te, tn],
        meta, forward, tokens, step, act, bc, gate, a_log, row(d_skip), w_out, row(gain_two),
        w_q, w_k, w_v, grad_att, far_out=(1,),
    )
    (back,) = call(
        attention, "attention",
        [((BLOCKS, ROWS, 128), bf16)],
        [((128, BLOCKS * T), bf16), ((BLOCKS, T, QCHUNK), f32), ((BLOCKS, T, QCHUNK), f32),
         ((BLOCKS, T, 128), f32)],
        meta, swap(packed),
    )
    wide = ((T, 6 * D), bf16)
    send, mixed, grad_mid, g, grad_gate, keep, give, g_gain_two, g_skip = call(
        middle_back, "middle_back",
        [((BLOCKS, N * 8, LANES), bf16), tdl, td, te, tel, wide, wide, ((1, D), f32), ((1, E), f32)],
        [tdl] * 4 + [te, tn, tdl, td, te, tel, wide],
        meta, swap(back), cot, middle, normed, low_ext, gated, gate, ssm, act, step, bc, a_log,
        row(d_skip), w_o, w_q, w_k, w_v, w_out, row(gain_two), far_out=(1, 2, 3, 4, 5, 7, 8),
        outside=(1, 2, 3, 4, 5), sems=((5,),),
    )
    (early,) = call(
        early_weights, "early_weights", [((16 * D, LANES), bf16)], [((2 * T, 6 * D), bf16)],
        meta, keep, partner(give), far=(1,),
    )
    early, behind, low_other = lax.optimization_barrier((early, swap(send), low_other))
    early = trade(early.reshape(SHARES, T, LANES))
    grad_tokens, tail, keep, give, part_keep = call(
        mamba_back, "mamba_back",
        [td, ((8, D), f32), ((HALO + T, D), bf16), ((4 * (HALO + T) + D, 128), bf16), ((D, 128), f32)],
        [te, te, ((T, N, E), f32), ((T, N, E), f32), te, te, ((HALO + T, E), f32),
         ((T + 8, E), f32), ((HALO + T, E), f32), ((N, E), f32), ((64, E), f32), tn, tn,
         ((T, N, LANES), f32), ((T, N, LANES), f32),
         te, ((T, R), bf16), te, ((HALO + T, E), bf16), ((64, E), bf16), ((R, E), bf16), tdl, ((D, 2 * E), bf16), tel, td],
        meta, behind, forward, start, g, act, step, pre, bc, dt_low, conv, ext, a_log,
        row(d_skip), conv_w, w_x, w_dt, tokens, halo, row(gain_one), w_in, grad_gate, grad_mid,
        g_gain_two, g_skip, far=tuple(range(1, 25)), far_out=(0, 1, 2, 4),
        there=(7, 9, 10, 11, 15, 16, 17, 20, 21, 22), sems=((10,),),
    )
    (late,) = call(
        late_weights, "late_weights", [((SHARES, LATE, LANES), bf16)], [((5 * D, LANES), f32)],
        keep, part_keep, low_ext, low_other, partner(give), smem=False, far=(0, 1, 2, 3), far_out=(0,),
    )
    (both,) = call(
        add_early, "add_early", [((SHARES, LATE + T, LANES), bf16)], [((SHARES, LATE + T, LANES), bf16)],
        early, late, smem=False, far=(1,), far_out=(0,), outside=(0,), sems=((4,),),
    )
    shares = trade(both)
    (late,) = call(
        add_late, "add_late", [((SHARES, LATE, LANES), bf16)], [((SHARES, 3 * N, LANES), bf16)],
        shares, smem=False, far=(0,), there=(0,), sems=((),),
    )
    late = trade(late)
    gw_o, gw_q, gw_k, gw_v, gw_out, gw_in = call(
        finish_early, "finish_early",
        [((D, D), f32)] * 4 + [((E, D), f32), ((D, 2 * E), f32)], [((D, E), f32)],
        meta, shares, partner(shares), outside=(5,), far=(1, 2), sems=((),),
    )
    grad_tokens, gw_in = lax.optimization_barrier((grad_tokens, gw_in))
    grad_tokens = grad_tokens.at[T - 8 :].add(shift(tail, -1))
    late, gw_in, grad_tokens = lax.optimization_barrier((late, gw_in, grad_tokens))
    gw_in, gw_x, gw_dt, g_a_log, g_conv_w, g_conv_b, g_dt_b, g_skip, g_gain_one, g_gain_two = call(
        finish_late, "finish_late",
        [((D, 2 * E), f32), ((64, E), f32), ((R, E), f32), tn, ((KERNEL, E), f32), ((1, E), f32),
         ((1, E), f32), ((1, E), f32), ((1, D), f32), ((1, D), f32)],
        [((D, E), f32), ((64, E), f32), ((R, E), f32), tn, ((KERNEL, E), f32), ((1, E), f32),
         ((1, E), f32), ((1, E), f32), ((1, D), f32), ((1, D), f32)],
        meta, late, partner(late), gw_in, outside=tuple(range(10)), aliases={3: 0}, sems=((5, 4),),
    )
    return (
        mixed[None], grad_tokens[None], g_gain_one[0], gw_in, g_conv_w, g_conv_b[0], gw_x.T, gw_dt,
        g_dt_b[0], g_a_log, g_skip[0], gw_out, g_gain_two[0], gw_q, gw_k, gw_v, gw_o,
    )


def solution(mesh):
    rows, seq, head = mesh.devices.shape
    fine = Mesh(mesh.devices.reshape(rows // 2, 2, seq, head), ALL)
    split = P(("y", "core"), PLACE, None)
    return jax.shard_map(
        layer,
        mesh=fine,
        in_specs=(split, P(("y", "core"), None)) + (P(),) * 15 + (split,),
        out_specs=(split, split) + (P(),) * 15,
        check_vma=False,
    )
```

```python
import functools

import jax
import jax.numpy as jnp
from jax import lax
from jax.experimental import pallas as pl
from jax.experimental.pallas import tpu as pltpu
from jax.sharding import Mesh, PartitionSpec as P

T, D, E, N, R, HD = 128, 512, 1024, 16, 32, 64
HEADS, BLOCKS, HALF, DOCS, KERNEL, HALO = 8, 16, 64, 6, 4, 16
LANES, STEPS = 128, 8
TILES = [slice(q * LANES, (q + 1) * LANES) for q in range(E // LANES)]
ROWS = T + HALF
SENT = N * 8 + 16
RESET = 1e4
LOG2E = 1.4426950408889634
EPS = 1e-05
MASKED = -1e30
PLACE = ("seq", "head")
ALL = ("y", "core", "seq", "head")
SAME, SHARES, MAIN, SMALL, LATE = ("y", "seq", "head"), 64, 32, 8, 40
bf16, f32, i32 = jnp.bfloat16, jnp.float32, jnp.int32


def mm(a, b):
    return jnp.dot(a, b, preferred_element_type=f32)


def mm_nt(a, b):
    return lax.dot_general(a, b, (((1,), (1,)), ((), ())), preferred_element_type=f32)


def mm_tn(a, b):
    return lax.dot_general(a, b, (((0,), (0,)), ((), ())), preferred_element_type=f32)


def doc_of(meta, pos):
    count = jnp.zeros(pos.shape, i32)
    for k in range(DOCS):
        count = count + (meta[2 + k] <= pos).astype(i32)
    return count


def reset_of(meta, pos):
    hit = meta[2] == pos
    for k in range(1, DOCS):
        hit = hit | (meta[2 + k] == pos)
    return jnp.where(hit, RESET, 0.0)


def inverse_rms(x):
    return lax.rsqrt(jnp.mean(x * x, axis=-1, keepdims=True) + EPS)


def sigmoid(x):
    return 1.0 / (1.0 + jnp.exp(-x))


def silu_slope(x):
    s = sigmoid(x)
    return s * (1.0 + x * (1.0 - s))


def norm_back(values, inverse, gain, upstream):
    scaled = upstream * gain
    inner = jnp.mean(values * scaled, axis=-1, keepdims=True)
    back = inverse * scaled - values * (inverse * inverse * inverse) * inner
    return back, jnp.sum(upstream * values * inverse, axis=0, keepdims=True)


def columns(offset, meta):
    first = meta[0]
    return first + offset + lax.broadcasted_iota(i32, (T, 1), 0)


def stack_sums(parts):
    row = lax.broadcasted_iota(i32, parts[0].shape, 0)
    for by in (1, 2, 4):
        first = (row & by) == 0
        parts = [
            jnp.where(first, a, b) + pltpu.roll(jnp.where(first, b, a), by, axis=0)
            for a, b in zip(parts[0::2], parts[1::2])
        ]
    return parts[0]


def column(block, low, k):
    return jnp.broadcast_to(block[low : low + N, k : k + 1], (N, LANES))


def halves(x):
    return x[0:8] + x[8:16]


def scan_forward(dec, sa, bc, rates2, start, result=None):
    def block(i, states):
        states = list(states)
        base = pl.multiple_of(i * STEPS, STEPS)
        cols = bc[i]
        sums = [[None] * STEPS for _ in TILES]
        for k in range(STEPS):
            b_col = column(cols, 0, k)
            c_col = column(cols, N, k)
            for q, tile in enumerate(TILES):
                factor = jnp.exp2(dec[pl.ds(base, STEPS), tile][k : k + 1] * rates2[:, tile])
                states[q] = factor * states[q] + b_col * sa[pl.ds(base, STEPS), tile][k : k + 1]
                if result is not None:
                    sums[q][k] = halves(states[q] * c_col)
        if result is not None:
            for q, tile in enumerate(TILES):
                result[pl.ds(base, STEPS), tile] = stack_sums(sums[q])
        return tuple(states)

    return lax.fori_loop(0, T // STEPS, block, tuple(start[:, tile] for tile in TILES))


def mamba_in(
    meta, tokens, halo, gain, w_in, conv_w, conv_b, w_x, w_dt, dt_b, a_log, cot, w_o,
    send, grad_att, low_out, ext_out, gate_out, conv_out, act_out, step_out, pre_out, bc_out, dt_out,
    ext, dec, sa, xp, rates2, zero,
):
    grad_att[...] = mm_nt(cot[...], w_o[...]).astype(bf16)
    own = tokens[...].astype(f32)
    before = halo[...].astype(f32)
    low_own = (own * inverse_rms(own) * gain[...]).astype(bf16)
    low_before = (before * inverse_rms(before) * gain[...]).astype(bf16)
    conv_own = mm(low_own, w_in[:, :E]).astype(bf16)
    conv_before = mm(low_before, w_in[:, :E]).astype(bf16)
    low_out[0:HALO] = low_before
    low_out[HALO : HALO + T] = low_own
    ext_out[0:HALO] = conv_before
    ext_out[HALO : HALO + T] = conv_own
    ext[0:HALO] = conv_before.astype(f32)
    ext[HALO : HALO + T] = conv_own.astype(f32)
    gate_out[...] = mm(low_own, w_in[:, E:]).astype(bf16)
    own_doc = doc_of(meta, columns(0, meta))
    conv = jnp.broadcast_to(conv_b[...], (T, E))
    for offset in range(KERNEL):
        same = (doc_of(meta, columns(offset - KERNEL + 1, meta)) == own_doc).astype(f32)
        low = HALO - KERNEL + 1 + offset
        conv = conv + conv_w[offset : offset + 1] * ext[low : low + T] * same
    conv_out[...] = conv
    act = (conv * sigmoid(conv)).astype(bf16)
    act_out[...] = act
    proj = mm_nt(act, w_x[...])
    dt_low = proj[:, :R].astype(bf16)
    dt_out[...] = dt_low
    pre = mm(dt_low, w_dt[...]) + dt_b[...]
    pre_out[...] = pre
    step = jnp.maximum(pre, 0.0) + jnp.log1p(jnp.exp(-jnp.abs(pre)))
    step_out[...] = step
    held = step + reset_of(meta, columns(0, meta))
    dec[...] = held
    sa[...] = step * act.astype(f32)
    xp[...] = jnp.zeros((T, 128), f32)
    xp[:, 0 : R + 2 * N] = proj
    turned = xp[...].T
    for i in range(T // STEPS):
        bc_out[i, :, 0:STEPS] = turned[R : R + 2 * N, i * STEPS : (i + 1) * STEPS]
    total = jnp.sum(held, axis=0, keepdims=True)
    high = total.astype(bf16)
    rest = (total - high.astype(f32)).astype(bf16)
    rates2[...] = -jnp.exp(a_log[...]) * LOG2E
    zero[...] = jnp.zeros((N, E), f32)
    states = scan_forward(dec, sa, bc_out, rates2, zero)
    sums = [high[:, tile].astype(f32) for tile in TILES] + [rest[:, tile].astype(f32) for tile in TILES]
    ended = jnp.concatenate(list(states) + sums, axis=0).astype(bf16)
    for j in range(BLOCKS):
        send[j] = ended


def joined(blocks, first, last, ends, rates2):
    def join(turn, states):
        sent = blocks[first(turn)].astype(f32)
        own = sent if ends is None else ends[first(turn)].astype(f32)
        total = sent[N * 8 : N * 8 + 8] + sent[N * 8 + 8 : N * 8 + 16]
        return tuple(
            jnp.exp2(rates2[:, tile] * total[q : q + 1]) * states[q] + own[q * N : (q + 1) * N]
            for q, tile in enumerate(TILES)
        )

    return lax.fori_loop(0, last, join, tuple(jnp.zeros((N, LANES), f32) for _ in TILES))


def roll_half(x):
    return pltpu.roll(x, HALF, axis=1)


def mamba_out(
    meta, got, tokens, step, act, bc, gate, a_log, d_skip, w_out, gain, w_q, w_k, w_v, grad_att,
    send, start_out, ssm_out, gated_out, middle_out, normed_out,
    dec, sa, ssm, rates2,
):
    place = meta[1]
    rates2[...] = -jnp.exp(a_log[...]) * LOG2E
    dec[...] = step[...] + reset_of(meta, columns(0, meta))
    act_f = act[...].astype(f32)
    sa[...] = step[...] * act_f
    for tile, state in zip(TILES, joined(got, lambda turn: turn, place, None, rates2)):
        start_out[:, tile] = state
    scan_forward(dec, sa, bc, rates2, start_out, ssm)
    result = ssm[...] + d_skip[...] * act_f
    ssm_out[...] = result
    gates = gate[...].astype(f32)
    gated = (result * (gates * sigmoid(gates))).astype(bf16)
    gated_out[...] = gated
    middle = tokens[...].astype(f32) + mm(gated, w_out[...])
    middle_out[...] = middle
    normed = (middle * inverse_rms(middle) * gain[...]).astype(bf16)
    normed_out[...] = normed
    queries = mm(normed, w_q[...]).astype(bf16).astype(f32) * (HD ** -0.5)
    keys = mm(normed, w_k[...])
    vals = mm(normed, w_v[...])
    grads = grad_att[...].astype(f32)
    low = lax.broadcasted_iota(i32, (T, 128), 1) < HALF
    for m in range(HEADS // 2):
        tile = slice(m * 128, (m + 1) * 128)
        for odd in range(2):
            for first, second, at, rows in ((keys, vals, 0, T), (queries, grads, T, HALF)):
                a, b = first[:, tile], second[:, tile]
                pair = jnp.where(low, a, roll_half(b)) if odd == 0 else jnp.where(low, roll_half(a), b)
                pair = pair.astype(bf16)
                dest = 2 * (2 * m + odd)
                if rows == T:
                    send[dest, 0:T] = pair
                    send[dest + 1, 0:T] = pair
                else:
                    send[dest, T:ROWS] = pair[0:HALF]
                    send[dest + 1, T:ROWS] = pair[HALF:T]


QCHUNK, QBLOCKS = 256, 4


def attention(meta, got, send, kv_t, scores, grads, kv_grad):
    parity = lax.rem(meta[1], 2)
    for i in range(BLOCKS):
        kv_t[:, i * T : (i + 1) * T] = got[i, 0:T].astype(f32).T.astype(bf16)
    lane = lax.broadcasted_iota(i32, (1, QCHUNK), 1)
    low_q = lax.broadcasted_iota(i32, (QCHUNK, 128), 1) < HD
    low_k = lax.broadcasted_iota(i32, (T, 128), 1) < HD
    key_row = lax.broadcasted_iota(i32, (T, QCHUNK), 0)
    for c in range(BLOCKS // QBLOCKS):
        qg = jnp.concatenate([got[c * QBLOCKS + b, T:ROWS] for b in range(QBLOCKS)], axis=0)
        q_only = jnp.where(low_q, qg.astype(f32), 0.0).astype(bf16)
        g_only = jnp.where(low_q, 0.0, qg.astype(f32)).astype(bf16)
        pos = (c * QBLOCKS + lane // HALF) * T + parity * HALF + lane % HALF
        begin = jnp.zeros((1, QCHUNK), i32)
        for k in range(DOCS):
            begin = jnp.maximum(begin, jnp.where(meta[2 + k] <= pos, meta[2 + k], 0))
        tiles = (c + 1) * QBLOCKS
        top = jnp.full((8, QCHUNK), MASKED, f32)
        for i in range(tiles):
            s = mm_nt(got[i, 0:T], q_only)
            allowed = key_row >= begin - i * T
            if i >= c * QBLOCKS:
                allowed = allowed & (key_row <= pos - i * T)
            s = jnp.where(allowed, s, MASKED)
            scores[i] = s
            top = jnp.maximum(top, jnp.max(s.reshape(T // 8, 8, QCHUNK), axis=0))
        top = jnp.max(top, axis=0, keepdims=True)
        total = jnp.zeros((8, QCHUNK), f32)
        cross = jnp.zeros((8, QCHUNK), f32)
        for i in range(tiles):
            p = jnp.exp2((scores[i] - top) * LOG2E)
            scores[i] = p
            g = mm_nt(got[i, 0:T], g_only)
            grads[i] = g
            total = total + jnp.sum(p.reshape(T // 8, 8, QCHUNK), axis=0)
            cross = cross + jnp.sum((p * g).reshape(T // 8, 8, QCHUNK), axis=0)
        inverse = 1.0 / jnp.sum(total, axis=0, keepdims=True)
        cross = jnp.sum(cross, axis=0, keepdims=True) * inverse
        out_t = jnp.zeros((128, QCHUNK), f32)
        dq_t = jnp.zeros((128, QCHUNK), f32)
        for i in range(tiles):
            prob = scores[i] * inverse
            low_p = prob.astype(bf16)
            low_s = (prob * (grads[i] - cross)).astype(bf16)
            turned = kv_t[:, i * T : (i + 1) * T]
            out_t = out_t + mm(turned, low_p)
            dq_t = dq_t + mm(turned, low_s)
            both = jnp.where(low_k, mm(low_s, qg), mm(low_p, qg))
            if i >= c * QBLOCKS:
                kv_grad[i] = both
            else:
                kv_grad[i] = kv_grad[i] + both
        pair = jnp.where(low_q, dq_t.T * (HD ** -0.5), out_t.T).astype(bf16)
        for b in range(QBLOCKS):
            send[c * QBLOCKS + b, T:ROWS] = pair[b * HALF : (b + 1) * HALF]
    for i in range(BLOCKS):
        send[i, 0:T] = kv_grad[i].astype(bf16)


def middle_back(
    meta, got, cot, middle, normed, low_ext, gated, gate, ssm, act, step, bc, a_log, d_skip,
    w_o, w_q, w_k, w_v, w_out, gain,
    send, mixed_far, grad_mid_far, g_far, grad_gate_far, keep_far, give, g_gain, g_skip,
    att, dq, dk, dv, dec, rates2, mixed, grad_mid_out, g_out, grad_gate_out, keep, sems,
):
    low = lax.broadcasted_iota(i32, (HALF, 128), 1) < HALF
    low_t = lax.broadcasted_iota(i32, (T, 128), 1) < HALF
    for m in range(HEADS // 2):
        tile = slice(m * 128, (m + 1) * 128)
        for p in range(2):
            a = got[4 * m + p, T:ROWS].astype(f32)
            b = got[4 * m + 2 + p, T:ROWS].astype(f32)
            rows = slice(p * HALF, (p + 1) * HALF)
            dq[rows, tile] = jnp.where(low, a, roll_half(b)).astype(bf16)
            att[rows, tile] = jnp.where(low, roll_half(a), b).astype(bf16)
        a = got[4 * m, 0:T].astype(f32) + got[4 * m + 1, 0:T].astype(f32)
        b = got[4 * m + 2, 0:T].astype(f32) + got[4 * m + 3, 0:T].astype(f32)
        dk[:, tile] = jnp.where(low_t, a, roll_half(b)).astype(bf16)
        dv[:, tile] = jnp.where(low_t, roll_half(a), b).astype(bf16)
    cot_low = cot[...]
    values = middle[...]
    mixed[...] = (values + mm(att[...], w_o[...])).astype(bf16)
    upstream = mm_nt(dq[...], w_q[...]) + mm_nt(dk[...], w_k[...]) + mm_nt(dv[...], w_v[...])
    back, gain_grad = norm_back(values, inverse_rms(values), gain[...], upstream)
    g_gain[...] = gain_grad
    grad_mid = cot_low.astype(f32) + back
    grad_mid_out[...] = grad_mid
    mid_low = grad_mid.astype(bf16)
    grad_gated = mm_nt(mid_low, w_out[...]).astype(bf16).astype(f32)
    gates = gate[...].astype(f32)
    sig = sigmoid(gates)
    g = grad_gated * (gates * sig)
    g_out[...] = g
    grad_gate = (grad_gated * ssm[...] * (sig * (1.0 + gates * (1.0 - sig)))).astype(bf16)
    grad_gate_out[...] = grad_gate
    for first, second, core in ((keep, give, 0), (give, keep, 1)):

        @pl.when(meta[2 + DOCS] == core)
        def _():
            first[:, 0:D] = att[...]
            first[:, D : 2 * D] = cot_low
            first[:, 2 * D : 3 * D] = normed[...]
            first[:, 3 * D : 4 * D] = dq[...]
            first[:, 4 * D : 5 * D] = dk[...]
            first[:, 5 * D : 6 * D] = dv[...]
            second[:, 0:E] = gated[...]
            second[:, E : E + D] = mid_low
            second[:, E + D : 2 * E] = low_ext[HALO : HALO + T]
            second[:, 2 * E : 3 * E] = grad_gate

    g_skip[...] = jnp.sum(g * act[...].astype(f32), axis=0, keepdims=True)
    saves = [
        pltpu.make_async_copy(held, place, sems.at[i])
        for i, (held, place) in enumerate(
            ((mixed, mixed_far), (grad_mid_out, grad_mid_far), (g_out, g_far), (grad_gate_out, grad_gate_far), (keep, keep_far))
        )
    ]
    for save in saves:
        save.start()
    dec[...] = step[...] + reset_of(meta, columns(0, meta))
    rates2[...] = -jnp.exp(a_log[...]) * LOG2E

    def block(turn, carry):
        carry = list(carry)
        i = T // STEPS - 1 - turn
        base = pl.multiple_of(i * STEPS, STEPS)
        cols = bc[i]
        for k in reversed(range(STEPS)):
            c_col = column(cols, N, k)
            for q, tile in enumerate(TILES):
                factor = jnp.exp2(dec[pl.ds(base, STEPS), tile][k : k + 1] * rates2[:, tile])
                carry[q] = factor * (carry[q] + c_col * g_out[pl.ds(base, STEPS), tile][k : k + 1])
        return tuple(carry)

    carry = lax.fori_loop(0, T // STEPS, block, tuple(jnp.zeros((N, LANES), f32) for _ in TILES))
    ended = jnp.concatenate(carry, axis=0).astype(bf16)
    for j in range(BLOCKS):
        send[j] = ended
    for save in saves:
        save.wait()


def mamba_back(
    meta, got, forward, start, g, act, step, pre_far, bc, dt_low_far, conv_far, ext_low_far, a_log, d_skip,
    conv_w, w_x_far, w_dt_far, tokens_far, halo, gain, w_in_far, grad_gate_far, grad_mid_far, g_gain_two, g_skip,
    grad_tokens, tail, keep, give, part_keep,
    dec, sa, decay, kept, gs, ab, ext, padded, grad_ext, vec, wide, rates, rates2, sum_b, sum_c,
    pre, dt_low, conv, ext_low, w_x, w_dt, tokens, w_in, grad_gate, grad_mid, sems,
):
    place = meta[1]
    loads = [
        pltpu.make_async_copy(source, held, sems.at[i])
        for i, (source, held) in enumerate(
            ((pre_far, pre), (dt_low_far, dt_low), (conv_far, conv), (ext_low_far, ext_low), (w_x_far, w_x), (w_dt_far, w_dt), (tokens_far, tokens), (w_in_far, w_in), (grad_gate_far, grad_gate), (grad_mid_far, grad_mid))
        )
    ]
    for load in loads:
        load.start()
    dec[...] = step[...] + reset_of(meta, columns(0, meta))
    act_f = act[...].astype(f32)
    sa[...] = step[...] * act_f
    rates[...] = -jnp.exp(a_log[...])
    rates2[...] = rates[...] * LOG2E

    ahead_carry = joined(forward, lambda turn: BLOCKS - 1 - turn, BLOCKS - 1 - place, got, rates2)
    for tile, state in zip(TILES, ahead_carry):
        wide[R : R + N, tile] = state

    def ahead(i, states):
        states = list(states)
        base = pl.multiple_of(i * STEPS, STEPS)
        cols = bc[i]
        for k in range(STEPS):
            b_col = column(cols, 0, k)
            total = jnp.zeros((N, LANES), f32)
            for q, tile in enumerate(TILES):
                rows = pl.ds(base, STEPS), tile
                factor = jnp.exp2(dec[rows][k : k + 1] * rates2[:, tile])
                moved = factor * states[q]
                decay[base + k, :, tile] = factor
                kept[base + k, :, tile] = moved
                states[q] = moved + b_col * sa[rows][k : k + 1]
                total = total + states[q] * g[rows][k : k + 1]
            sum_c[base + k] = total
        return tuple(states)

    lax.fori_loop(0, T // STEPS, ahead, tuple(start[:, tile] for tile in TILES))
    first_carry = tuple(wide[R : R + N, tile] for tile in TILES)
    wide[R + N : R + 2 * N] = jnp.zeros((N, E), f32)

    def behind(turn, carry):
        carry = list(carry)
        i = T // STEPS - 1 - turn
        base = pl.multiple_of(i * STEPS, STEPS)
        cols = bc[i]
        by_rate = [[None] * STEPS for _ in TILES]
        by_b = [[None] * STEPS for _ in TILES]
        along = [wide[R + N : R + 2 * N, tile] for tile in TILES]
        for k in reversed(range(STEPS)):
            b_col = column(cols, 0, k)
            c_col = column(cols, N, k)
            total = jnp.zeros((N, LANES), f32)
            for q, tile in enumerate(TILES):
                rows = pl.ds(base, STEPS), tile
                adjoint = g[rows][k : k + 1] * c_col + carry[q]
                carry[q] = decay[base + k, :, tile] * adjoint
                log_grad = adjoint * kept[base + k, :, tile]
                along[q] = along[q] + log_grad * step[rows][k : k + 1]
                by_rate[q][k] = halves(log_grad * rates[:, tile])
                by_b[q][k] = halves(adjoint * b_col)
                total = total + adjoint * sa[rows][k : k + 1]
            sum_b[base + k] = total
        for q, tile in enumerate(TILES):
            wide[R + N : R + 2 * N, tile] = along[q]
            gs[pl.ds(base, STEPS), tile] = stack_sums(by_rate[q])
            ab[pl.ds(base, STEPS), tile] = stack_sums(by_b[q])
        return tuple(carry)

    lax.fori_loop(0, T // STEPS, behind, first_carry)
    wide[R : R + N] = wide[R + N : R + 2 * N] * rates[...]
    lane = lax.broadcasted_iota(i32, (LANES, LANES), 1)
    turned = jnp.zeros((T, LANES), f32)
    for at, sums in ((0, sum_b), (N, sum_c)):
        for n in range(N):
            one = (lane == at + n).astype(f32).astype(bf16)
            values = sums[:, n, :]
            high = values.astype(bf16)
            turned = turned + mm(high, one) + mm((values - high.astype(f32)).astype(bf16), one)
    for load in loads:
        load.wait()
    adjoint_b = ab[...]
    grad_step = gs[...] + adjoint_b * act_f
    grad_act = g[...] * d_skip[...] + adjoint_b * step[...]
    grad_pre = (grad_step * sigmoid(pre[...])).astype(bf16)
    vec[...] = jnp.zeros((N, E), f32)
    vec[KERNEL + 1 : KERNEL + 2] = jnp.sum(grad_pre.astype(f32), axis=0, keepdims=True)
    vec[KERNEL + 2 : KERNEL + 3] = g_skip[...]
    wide[0:R] = mm_tn(dt_low[...], grad_pre)
    grad_proj = jnp.concatenate([mm_nt(grad_pre, w_dt[...]), turned[:, 0 : 2 * N]], axis=1).astype(bf16)
    gw_x = mm_tn(grad_proj, act[...])
    grad_act = grad_act + mm(grad_proj, w_x[...])
    grad_conv = grad_act * silu_slope(conv[...])
    vec[KERNEL : KERNEL + 1] = jnp.sum(grad_conv, axis=0, keepdims=True)
    padded[0:T] = grad_conv
    padded[T : T + 8] = jnp.zeros((8, E), f32)
    ext[...] = ext_low[...].astype(f32)
    own_doc = doc_of(meta, columns(0, meta))
    own = jnp.zeros((T, E), f32)
    lift = KERNEL - 1
    rows = lax.broadcasted_iota(i32, (T, 1), 0)
    for offset in range(KERNEL):
        same = (doc_of(meta, columns(offset - lift, meta)) == own_doc).astype(f32)
        low = HALO - lift + offset
        vec[offset : offset + 1] = jnp.sum(grad_conv * ext[low : low + T] * same, axis=0, keepdims=True)
        up = lift - offset
        ahead_same = (doc_of(meta, columns(0, meta)) == doc_of(meta, columns(up, meta))) & (rows < T - up)
        own = own + conv_w[offset : offset + 1] * padded[up : up + T] * ahead_same.astype(f32)
    grad_ext[HALO : HALO + T] = own
    first = meta[0]
    edges = [jnp.zeros((HALO - lift, E), f32)]
    for row in range(lift):
        edge = jnp.zeros((1, E), f32)
        here = doc_of(meta, first - lift + row + jnp.zeros((1, 1), i32))
        for offset in range(row + 1):
            at = row - offset
            same = (doc_of(meta, first + at + jnp.zeros((1, 1), i32)) == here).astype(f32)
            edge = edge + conv_w[offset : offset + 1] * padded[at : at + 1] * same
        edges.append(edge)
    grad_ext[0:HALO] = jnp.concatenate(edges, axis=0)
    low_edge = grad_ext[0:HALO].astype(bf16)
    low_own = grad_ext[HALO : HALO + T].astype(bf16)
    values = tokens[...].astype(f32)
    upstream = mm_nt(low_own, w_in[:, :E]) + mm_nt(grad_gate[...], w_in[:, E:])
    back, gain_own = norm_back(values, inverse_rms(values), gain[...], upstream)
    grad_tokens[...] = grad_mid[...] + back
    before = halo[...].astype(f32)
    back, gain_edge = norm_back(before, inverse_rms(before), gain[...], mm_nt(low_edge, w_in[:, :E]))
    tail[...] = back[HALO - 8 : HALO]
    vec[KERNEL + 3 : KERNEL + 4, 0:D] = gain_own + gain_edge
    vec[KERNEL + 3 : KERNEL + 4, D:E] = g_gain_two[...]
    wide[R + N : R + 2 * N] = vec[...]
    for core in range(2):

        @pl.when(meta[2 + DOCS] == core)
        def _():
            for j in range(D // 128):
                cols = slice(core * D + j * 128, core * D + (j + 1) * 128)
                keep[0:HALO, j * 128 : (j + 1) * 128] = low_edge[:, cols]
                keep[HALO : HALO + T, j * 128 : (j + 1) * 128] = low_own[:, cols]
                cols = slice((1 - core) * D + j * 128, (1 - core) * D + (j + 1) * 128)
                base = j * (HALO + T)
                give[base : base + HALO] = low_edge[:, cols]
                give[base + HALO : base + HALO + T] = low_own[:, cols]
            base = D // 128 * (HALO + T)
            for j in range(E // 128):
                cols = slice(j * 128, (j + 1) * 128)
                mine, other = (gw_x, wide) if core == 0 else (wide, gw_x)
                part_keep[j * 64 : (j + 1) * 64] = mine[:, cols]
                give[base + j * 64 : base + (j + 1) * 64] = other[:, cols].astype(bf16)


def early_weights(meta, keep, got, out, both):
    both[0:T] = keep[...]
    both[T : 2 * T] = got[...]
    left_right = (((0, 1), (2, 3), (2, 4), (2, 5)), ((0, 2), (1, 2), (3, 4), (3, 5)))
    for core in range(2):

        @pl.when(meta[2 + DOCS] == core)
        def _():
            for j, (a, b) in enumerate(left_right[core]):
                left, right = both[:, a * D : (a + 1) * D], both[:, b * D : (b + 1) * D]
                result = mm_tn(left, right).astype(bf16)
                for q in range(D // LANES):
                    out[(4 * j + q) * D : (4 * j + q + 1) * D] = result[:, q * LANES : (q + 1) * LANES]


def late_weights(keep, part_keep, low_own, low_other, got, out, whole):
    left = jnp.concatenate([low_own[...], low_other[...]], axis=0)
    rows = HALO + T
    for j in range(D // LANES):
        right = jnp.concatenate([keep[:, j * LANES : (j + 1) * LANES], got[j * rows : (j + 1) * rows]], axis=0)
        whole[j * D : (j + 1) * D] = mm_tn(left, right)
    base = D // LANES * rows
    whole[4 * D : 5 * D] = part_keep[...] + got[base : base + D].astype(f32)
    for d in range(SHARES):
        main = whole[d * MAIN : (d + 1) * MAIN]
        small = whole[4 * D + d * SMALL : 4 * D + (d + 1) * SMALL]
        out[d] = jnp.concatenate([main, small], axis=0).astype(bf16)


def add_early(early, late, out, held, sems):
    total = early[0].astype(f32)
    for j in range(1, SHARES):
        total = total + early[j].astype(f32)
    copies = []
    for j in range(SHARES):
        held[j] = jnp.concatenate([late[j].astype(f32), total], axis=0).astype(bf16)
        if j % BLOCKS == BLOCKS - 1:
            part = pl.ds(j + 1 - BLOCKS, BLOCKS)
            copies.append(pltpu.make_async_copy(held.at[part], out.at[part], sems.at[j // BLOCKS]))
            copies[-1].start()
    for copy in copies:
        copy.wait()


def add_late(got, out, held, sems):
    parts = [pl.ds(i * BLOCKS, BLOCKS) for i in range(SHARES // BLOCKS)]
    loads = [
        pltpu.make_async_copy(got.at[part, pl.ds(0, 3 * N)], held.at[part], sems.at[i])
        for i, part in enumerate(parts)
    ]
    for load in loads:
        load.start()
    total = jnp.zeros((LATE, LANES), f32)
    for j in range(SHARES):
        if j % BLOCKS == 0:
            loads[j // BLOCKS].wait()
        total = total + held[j].astype(f32)[0:LATE]
    low = total.astype(bf16)
    for j in range(SHARES):
        out[j] = low


def finish_early(meta, mine, other, gw_o, gw_q, gw_k, gw_v, gw_out, gw_in, gate, sem):
    is_zero = meta[2 + DOCS] == 0
    for d in reversed(range(SHARES)):
        a, b = mine[d].astype(f32)[LATE:], other[d].astype(f32)[LATE:]
        j, q, r = d // 16, d // 4 % 4, d % 4 * T
        tile = TILES[q]
        (gw_o, gw_q, gw_k, gw_v)[j][r : r + T, tile] = jnp.where(is_zero, a, b)
        one = jnp.where(is_zero, b, a)
        if j < 2:
            gw_out[j * D + r : j * D + r + T, tile] = one
        else:
            low = (j - 2) * D + q * LANES
            gate[r : r + T, low : low + LANES] = one
        if d == SHARES // 2:
            copy = pltpu.make_async_copy(gate, gw_in.at[:, pl.ds(E, E)], sem)
            copy.start()
    copy.wait()


def finish_late(
    meta, mine, other, _, gw_in, gw_x_far, gw_dt_far, g_a_log_far, g_conv_w_far, g_conv_b_far,
    g_dt_b_far, g_skip_far, g_gain_one_far, g_gain_two_far,
    conv, gw_x, gw_dt, g_a_log, g_conv_w, g_conv_b, g_dt_b, g_skip, g_gain_one, g_gain_two, sems,
):
    is_zero = meta[2 + DOCS] == 0
    copies = []
    for d in range(SHARES):
        a, b = mine[d].astype(f32), other[d].astype(f32)
        zero = jnp.where(is_zero, a, b)
        one = jnp.where(is_zero, b, a)
        j, r = d // 16, d % 16 * MAIN
        conv[r : r + MAIN, j * LANES : (j + 1) * LANES] = zero[0:MAIN]
        conv[r : r + MAIN, D + j * LANES : D + (j + 1) * LANES] = one[0:MAIN]
        if d % 16 == 15:
            for side in range(2):
                cols = pl.ds(side * D + j * LANES, LANES)
                copies.append(pltpu.make_async_copy(conv.at[:, cols], gw_in.at[:, cols], sems.at[side, j]))
                copies[-1].start()
        q, r = d // 8, d % 8 * SMALL
        tile = TILES[q]
        gw_x[r : r + SMALL, tile] = zero[MAIN:]
        for out, low, high in ((gw_dt, 0, R), (g_a_log, R, R + N)):
            if low <= r < high:
                out[r - low : r - low + SMALL, tile] = one[MAIN:]
        if r == R + N:
            g_conv_w[:, tile] = one[MAIN : MAIN + KERNEL]
            at = MAIN + KERNEL
            for i, out in enumerate((g_conv_b, g_dt_b, g_skip)):
                out[:, tile] = one[at + i : at + i + 1]
            out = g_gain_one if q < 4 else g_gain_two
            out[:, TILES[q % 4]] = one[at + 3 : at + 4]
    smalls = (
        (gw_x, gw_x_far),
        (gw_dt, gw_dt_far),
        (g_a_log, g_a_log_far),
        (g_conv_w, g_conv_w_far),
        (g_conv_b, g_conv_b_far),
        (g_dt_b, g_dt_b_far),
        (g_skip, g_skip_far),
        (g_gain_one, g_gain_one_far),
        (g_gain_two, g_gain_two_far),
    )
    for i, (held, place) in enumerate(smalls):
        copies.append(pltpu.make_async_copy(held, place, sems.at[2 + i // 4, i % 4]))
        copies[-1].start()
    for copy in copies:
        copy.wait()


MEGABYTES = dict(
    mamba_in=16, mamba_out=16, attention=16, middle_back=20, early_weights=12, mamba_back=38, late_weights=12,
    add_late=8, add_early=14, finish_early=24, finish_late=12,
)


def call(body, name, outs, scratch, *args, smem=True, outside=(), aliases=None, far=(), far_out=(), there=(), sems=()):
    aliases = aliases or {}
    args = [pltpu.with_memory_space_constraint(x, pltpu.HBM) if i in far else x for i, x in enumerate(args)]
    specs = [pl.BlockSpec(memory_space=pl.ANY if i in aliases or i in there else pltpu.VMEM) for i in range(len(args))]
    if smem:
        specs[0] = pl.BlockSpec(memory_space=pltpu.SMEM)
    return pl.pallas_call(
        body,
        name=name,
        out_shape=[pltpu.HBM(s, t) if i in far_out else jax.ShapeDtypeStruct(s, t) for i, (s, t) in enumerate(outs)],
        in_specs=specs,
        out_specs=[pl.BlockSpec(memory_space=pl.ANY if i in outside else pltpu.VMEM) for i in range(len(outs))],
        scratch_shapes=[pltpu.VMEM(s, t) for s, t in scratch]
        + [pltpu.SemaphoreType.DMA(n) for n in sems],
        input_output_aliases=aliases,
        compiler_params=pltpu.CompilerParams(vmem_limit_bytes=MEGABYTES[name] << 20),
    )(*args)


def shift(x, by):
    pairs = [(i, i + by) for i in range(BLOCKS) if 0 <= i + by < BLOCKS]
    return lax.ppermute(x, PLACE, pairs)


def swap(x):
    return lax.all_to_all(x, PLACE, 0, 0, tiled=True)


def partner(x):
    return lax.ppermute(x, "core", [(0, 1), (1, 0)])


def trade(x):
    return lax.all_to_all(x, SAME, 0, 0, tiled=True)


def layer(
    tokens, starts, gain_one, w_in, conv_w, conv_b, w_x, w_dt, dt_bias, a_log, d_skip, w_out,
    gain_two, w_q, w_k, w_v, w_o, cotangent,
):
    tokens, cot = tokens[0], cotangent[0]
    place = lax.axis_index(PLACE)
    core = lax.axis_index("core").astype(i32)
    meta = jnp.concatenate([jnp.stack([place * T, place]).astype(i32), starts[0], core[None]])
    row = lambda v: v.reshape(1, -1)
    halo = shift(tokens[T - HALO :], 1)
    tn = ((N, E), f32)
    te, tel, td, tdl = ((T, E), f32), ((T, E), bf16), ((T, D), f32), ((T, D), bf16)
    w_x = w_x.T
    send, grad_att, low_ext, ext, gate, conv, act, step, pre, bc, dt_low = call(
        mamba_in, "mamba_in",
        [((BLOCKS, SENT, LANES), bf16), tdl, ((HALO + T, D), bf16), ((HALO + T, E), bf16), tel, te, tel, te, te,
         ((T // STEPS, 2 * N, 128), f32), ((T, R), bf16)],
        [((HALO + T, E), f32), te, te, ((T, 128), f32), tn, tn],
        meta, tokens, halo, row(gain_one), w_in, conv_w, row(conv_b), w_x, w_dt, row(dt_bias), a_log, cot, w_o,
        far=(1, 3, 4, 5, 6, 7, 8, 9, 10, 11, 12), far_out=(2, 3, 5, 8, 10),
    )
    low_other = partner(low_ext)
    forward = swap(send)
    packed, start, ssm, gated, middle, normed = call(
        mamba_out, "mamba_out",
        [((BLOCKS, ROWS, 128), bf16), ((N, E), f32), te, tel, td, tdl],
        [te, te, te, tn],
        meta, forward, tokens, step, act, bc, gate, a_log, row(d_skip), w_out, row(gain_two),
        w_q, w_k, w_v, grad_att, far_out=(1,),
    )
    (back,) = call(
        attention, "attention",
        [((BLOCKS, ROWS, 128), bf16)],
        [((128, BLOCKS * T), bf16), ((BLOCKS, T, QCHUNK), f32), ((BLOCKS, T, QCHUNK), f32),
         ((BLOCKS, T, 128), f32)],
        meta, swap(packed),
    )
    wide = ((T, 6 * D), bf16)
    send, mixed, grad_mid, g, grad_gate, keep, give, g_gain_two, g_skip = call(
        middle_back, "middle_back",
        [((BLOCKS, N * 8, LANES), bf16), tdl, td, te, tel, wide, wide, ((1, D), f32), ((1, E), f32)],
        [tdl] * 4 + [te, tn, tdl, td, te, tel, wide],
        meta, swap(back), cot, middle, normed, low_ext, gated, gate, ssm, act, step, bc, a_log,
        row(d_skip), w_o, w_q, w_k, w_v, w_out, row(gain_two), far_out=(1, 2, 3, 4, 5, 7, 8),
        outside=(1, 2, 3, 4, 5), sems=((5,),),
    )
    (early,) = call(
        early_weights, "early_weights", [((16 * D, LANES), bf16)], [((2 * T, 6 * D), bf16)],
        meta, keep, partner(give), far=(1,),
    )
    early, behind, low_other = lax.optimization_barrier((early, swap(send), low_other))
    early = trade(early.reshape(SHARES, T, LANES))
    grad_tokens, tail, keep, give, part_keep = call(
        mamba_back, "mamba_back",
        [td, ((8, D), f32), ((HALO + T, D), bf16), ((4 * (HALO + T) + D, 128), bf16), ((D, 128), f32)],
        [te, te, ((T, N, E), f32), ((T, N, E), f32), te, te, ((HALO + T, E), f32),
         ((T + 8, E), f32), ((HALO + T, E), f32), ((N, E), f32), ((64, E), f32), tn, tn,
         ((T, N, LANES), f32), ((T, N, LANES), f32),
         te, ((T, R), bf16), te, ((HALO + T, E), bf16), ((64, E), bf16), ((R, E), bf16), tdl, ((D, 2 * E), bf16), tel, td],
        meta, behind, forward, start, g, act, step, pre, bc, dt_low, conv, ext, a_log,
        row(d_skip), conv_w, w_x, w_dt, tokens, halo, row(gain_one), w_in, grad_gate, grad_mid,
        g_gain_two, g_skip, far=tuple(range(1, 25)), far_out=(0, 1, 2, 4),
        there=(7, 9, 10, 11, 15, 16, 17, 20, 21, 22), sems=((10,),),
    )
    (late,) = call(
        late_weights, "late_weights", [((SHARES, LATE, LANES), bf16)], [((5 * D, LANES), f32)],
        keep, part_keep, low_ext, low_other, partner(give), smem=False, far=(0, 1, 2, 3), far_out=(0,),
    )
    (both,) = call(
        add_early, "add_early", [((SHARES, LATE + T, LANES), bf16)], [((SHARES, LATE + T, LANES), bf16)],
        early, late, smem=False, far=(1,), far_out=(0,), outside=(0,), sems=((4,),),
    )
    shares = trade(both)
    (late,) = call(
        add_late, "add_late", [((SHARES, LATE, LANES), bf16)], [((SHARES, 3 * N, LANES), bf16)],
        shares, smem=False, far=(0,), there=(0,), sems=((4,),),
    )
    late = trade(late)
    gw_o, gw_q, gw_k, gw_v, gw_out, gw_in = call(
        finish_early, "finish_early",
        [((D, D), f32)] * 4 + [((E, D), f32), ((D, 2 * E), f32)], [((D, E), f32)],
        meta, shares, partner(shares), outside=(5,), far=(1, 2), sems=((),),
    )
    grad_tokens, gw_in = lax.optimization_barrier((grad_tokens, gw_in))
    grad_tokens = grad_tokens.at[T - 8 :].add(shift(tail, -1))
    late, gw_in, grad_tokens = lax.optimization_barrier((late, gw_in, grad_tokens))
    gw_in, gw_x, gw_dt, g_a_log, g_conv_w, g_conv_b, g_dt_b, g_skip, g_gain_one, g_gain_two = call(
        finish_late, "finish_late",
        [((D, 2 * E), f32), ((64, E), f32), ((R, E), f32), tn, ((KERNEL, E), f32), ((1, E), f32),
         ((1, E), f32), ((1, E), f32), ((1, D), f32), ((1, D), f32)],
        [((D, E), f32), ((64, E), f32), ((R, E), f32), tn, ((KERNEL, E), f32), ((1, E), f32),
         ((1, E), f32), ((1, E), f32), ((1, D), f32), ((1, D), f32)],
        meta, late, partner(late), gw_in, outside=tuple(range(10)), aliases={3: 0}, sems=((5, 4),),
    )
    return (
        mixed[None], grad_tokens[None], g_gain_one[0], gw_in, g_conv_w, g_conv_b[0], gw_x.T, gw_dt,
        g_dt_b[0], g_a_log, g_skip[0], gw_out, g_gain_two[0], gw_q, gw_k, gw_v, gw_o,
    )


def solution(mesh):
    rows, seq, head = mesh.devices.shape
    fine = Mesh(mesh.devices.reshape(rows // 2, 2, seq, head), ALL)
    split = P(("y", "core"), PLACE, None)
    return jax.shard_map(
        layer,
        mesh=fine,
        in_specs=(split, P(("y", "core"), None)) + (P(),) * 15 + (split,),
        out_specs=(split, split) + (P(),) * 15,
        check_vma=False,
    )
```
